32 devices in a mesh: gx: 8 (over y, x, core), gy: 4 (over z).
Axes of the slice: x: 2, y: 2, z: 4, core: 2. Of those that a mesh axis runs over, the one named last changes fastest.
Arguments:
- tokens: bfloat16 [16384, 1536], P(('gx', 'gy')), may hold values from -6 to 6
- attn_gain: float32 [1536], replicated, may hold values from 0.25 to 1.75
- query_key_value_weight: bfloat16 [1536, 2560], P('gx', 'gy'), may hold values from -0.15625 to 0.15625
- out_weight: bfloat16 [1536, 1536], P('gy', 'gx'), may hold values from -0.875 to 0.875
- moe_gain: float32 [1536], replicated, may hold values from 0.25 to 1.75
- router_weight: bfloat16 [40, 1536], P('gy', 'gx'), may hold values from -0.078125 to 0.078125
- expert_in: bfloat16 [40, 1536, 1024], P('gy', 'gx'), may hold values from -0.15625 to 0.15625
- expert_out: bfloat16 [40, 1536, 512], P('gy', 'gx'), may hold values from -0.75 to 0.75
- expert_ids: int32 [16384, 8], P('gx'), may hold values from 0 to 39, all different within a row
- route_order: int32 [8, 16384], P('gx'), may hold values from 0 to 16383, each once within a row
- segment_ids: int32 [8, 2048], P('gx'), may hold values from 0 to 15, never falling along the last dimension, each value on 1 to 256 neighbouring positions
- out_grad: bfloat16 [16384, 1536], P(('gx', 'gy')), may hold values from -6 to 6
Outputs:
- layer_out: bfloat16 [16384, 1536], P(('gx', 'gy'))
- input_grad: float32 [16384, 1536], P(('gx', 'gy'))
- attn_gain_grad: float32 [1536], replicated
- qkv_grad: float32 [1536, 2560], P('gx', 'gy')
- out_weight_grad: float32 [1536, 1536], P('gy', 'gx')
- moe_gain_grad: float32 [1536], replicated
- router_grad: float32 [40, 1536], P('gy', 'gx')
- expert_in_grad: float32 [40, 1536, 1024], P('gy', 'gx')
- expert_out_grad: float32 [40, 1536, 512], P('gy', 'gx')
The draws below stay inside these ranges and needn't reach their ends.
Inputs may be any that keep to these rules, and one draw needn't show every extreme that they name: `expert_ids`: the 8 experts of a token differ from one another. `route_order`: each row holds every number of 0 to 16383 once; entry t * 8 + k is the rank of the k-th choice of the sequence's token t. `segment_ids`: document numbers never fall along a row; a document holds at most 256 positions.
All inputs are finite; a program needn't handle non-finite values.
Results may differ from the reference program's by a relative error of at most 0.02.
Values may be sent and summed in bfloat16 or wider, within the bound.
No kernel may reach another device: no remote copies, remote signals or barrier semaphores. Data moves between devices by JAX's collectives and lax.ppermute only.
A program may use at most 320 MiB of HBM per device.

```python
import math
import jax
import jax.numpy as jnp
import numpy as np
from jax import lax

D = 1536
HQ = 24
KEY_VALUE_HEADS = 8
HEAD_WIDTH = 64
E = 40
FF = 512
TOPK = 8
TOK_DEV = 2048
SEGMAX = 256
QUERIES_PER_GROUP = 3
QKV = 2560
CAP = 460
PAIRS = 16384
SEQS = 8
TOKENS = 16384
SEGS = 16


def block_levels(rng, extent, split, low, largest):
    loudness, own = 1.0, jax.random.fold_in(rng, 6)
    for position, shards_of in split:
        heights = jnp.exp(jax.random.uniform(jax.random.fold_in(own, position), (shards_of,), jnp.float32, low / len(split), largest / len(split)))
        loudness = loudness * jnp.repeat(heights, extent[position] // shards_of).reshape([-1 if axis == position else 1 for axis in range(len(extent))])
    return loudness


def picks_of(rng, rows, amount, top, lift):
    order = jax.random.permutation(jax.random.fold_in(rng, 1), amount)
    boost = order
    for power in range(3):
        boost = boost * boost // amount
    boost = boost * lift // amount
    lots = jax.random.randint(jax.random.fold_in(rng, 2), (rows, amount), 0, 4096) + boost
    sure = jax.random.permutation(jax.random.fold_in(rng, 3), rows)[jnp.arange(amount) % rows]
    lots = jnp.where(jnp.arange(rows)[:, None] == sure[None, :], 1 << 14, lots)
    score = lots * amount + jnp.arange(amount)
    return lax.top_k(score.astype(jnp.int32), top)[1].astype(jnp.int32)


def profile(amount, total, most, slope):
    weights = [(1 << 20) // math.isqrt(grade ** slope) + 1 for grade in range(2, amount + 1)]
    spare, counts = total - most - (amount - 1), [1] * (amount - 1)
    while spare > 0:
        free = [i for i in range(amount - 1) if counts[i] < most]
        pool, left = sum([weights[i] for i in free]), spare
        for i in free:
            more = min(most - counts[i], max(1, left * weights[i] // pool), spare)
            counts[i] = counts[i] + more
            spare = spare - more
    return np.array([most] + counts)


def uneven_parts(rng, amount, total, bound, skew):
    if amount == 2:
        one = jax.random.randint(rng, (), max(1, total - bound), min(bound, total - 1) + 1)
        return jnp.stack([one, total - one])
    sizes = jnp.asarray(profile(amount, total, bound, skew), jnp.int32)
    couples = (amount - 1) // 2
    source_of, sink = sizes[1:1 + 2 * couples:2], sizes[2:2 + 2 * couples:2]
    margin = jnp.minimum(source_of - 1, bound - sink)
    moved = jax.random.randint(jax.random.fold_in(rng, 1), (couples,), 0, 1 << 20) % (margin + 1)
    sizes = sizes.at[1:1 + 2 * couples:2].set(source_of - moved).at[2:2 + 2 * couples:2].set(sink + moved)
    return sizes[jax.random.permutation(jax.random.fold_in(rng, 2), amount)]


def gaussian(rng, shape, deviation, bound, cuts=(), kind=jnp.bfloat16):
    gain = block_levels(rng, shape, cuts, -0.22, 0.18) if cuts else 1.0
    entries = jax.random.normal(rng, shape, jnp.float32) * deviation * gain
    return jnp.minimum(jnp.maximum(entries, -bound), bound).astype(kind)


def setup_inputs(seed: int = 0) -> dict:
    seeds = jax.random.split(jax.random.key(seed), 13)
    return {
        "tokens": gaussian(seeds[0], (TOKENS, D), 1.0, 6.0, ((0, 32),)),
        "attn_gain": jnp.clip(1.0 + 0.15 * jax.random.normal(seeds[1], (D,), jnp.float32), 0.25, 1.75),
        "query_key_value_weight": gaussian(seeds[2], (D, QKV), D ** -0.5, 0.15625, ((0, 8), (1, 4))),
        "out_weight": gaussian(seeds[3], (HQ * HEAD_WIDTH, D), (HQ * HEAD_WIDTH // 32) ** -0.5, 0.875, ((0, 4), (1, 8))),
        "moe_gain": jnp.clip(1.0 + 0.15 * jax.random.normal(seeds[4], (D,), jnp.float32), 0.25, 1.75),
        "router_weight": gaussian(seeds[5], (E, D), (4 * D) ** -0.5, 0.078125, ((0, 4), (1, 8))),
        "expert_in": gaussian(seeds[6], (E, D, 2 * FF), D ** -0.5, 0.15625, ((0, 4), (1, 8))),
        "expert_out": gaussian(seeds[7], (E, D, FF), (FF // 8) ** -0.5, 0.75, ((0, 4), (1, 8))),
        "expert_ids": picks_of(seeds[8], TOKENS, E, TOPK, 1638),
        "route_order": jax.vmap(lambda own: jax.random.permutation(own, PAIRS))(jax.random.split(seeds[9], SEQS)).reshape((SEQS, PAIRS)).astype(jnp.int32),
        "segment_ids": jax.vmap(lambda own: jnp.searchsorted(jnp.cumsum(uneven_parts(own, SEGS, TOK_DEV, SEGMAX, 1)), jnp.arange(TOK_DEV), side="right"))(jax.random.split(seeds[10], SEQS)).reshape((SEQS, TOK_DEV)).astype(jnp.int32),
        "out_grad": gaussian(seeds[11], (TOKENS, D), 1.0, 6.0, ((0, 32),)),
    }


EPS = 1e-05
HIGHER_PRECISION = lax.Precision.HIGHEST
MASKED = -1e+30

@jax.custom_vjp
def low(v):
    return lax.optimization_barrier(v.astype(jnp.bfloat16)).astype(jnp.float32)

@jax.custom_vjp
def lowered_backward(v):
    return v

def low_keep(v):
    return (low(v), None)

def low_pass(kept, grad):
    return (grad,)

def back_keep(v):
    return (v, None)

def back_low(kept, grad):
    return (low(grad),)
low.defvjp(low_keep, low_pass)
lowered_backward.defvjp(back_keep, back_low)

def rope_tables(count_total, width):
    half_width = width // 2
    freq = jnp.exp(jnp.arange(half_width, dtype=jnp.float32) * (-2.0 * jnp.log(10000.0) / width))
    angle = jnp.arange(count_total, dtype=jnp.float32)[:, None] * freq[None, :]
    return (jnp.cos(angle), jnp.sin(angle))

def rotate(value_rows, cosine, sine):
    half_width = value_rows.shape[-1] // 2
    target_shape = (value_rows.shape[0],) + (1,) * (value_rows.ndim - 2) + (half_width,)
    cosine = cosine.reshape(target_shape)
    sine = sine.reshape(target_shape)
    first_half = value_rows[..., :half_width]
    second_half = value_rows[..., half_width:]
    return jnp.concatenate([first_half * cosine - second_half * sine, second_half * cosine + first_half * sine], axis=-1)

def slot_tables(expert_list, order, experts, first_expert):
    pairs = expert_list.shape[0] * expert_list.shape[1]
    flat_ids = expert_list.reshape(-1)
    numbers = jnp.arange(pairs, dtype=jnp.int32)
    at_rank = jnp.zeros((pairs,), jnp.int32).at[order].set(numbers)
    rank_expert = flat_ids[at_rank] - first_expert
    match_table = (rank_expert[:, None] == jnp.arange(experts, dtype=jnp.int32)[None, :]).astype(jnp.int32)
    earlier = jnp.cumsum(match_table, axis=0, dtype=jnp.int32) - match_table
    slot_rank = lax.optimization_barrier(jnp.sum(earlier * match_table, axis=1, dtype=jnp.int32))
    slot_index = slot_rank[order]
    local_id = flat_ids - first_expert
    kept_pair = (local_id >= 0) & (local_id < experts) & (slot_index < CAP)
    target = jnp.where(kept_pair, local_id * CAP + slot_index, experts * CAP)
    owner = jnp.full((experts * CAP,), pairs, jnp.int32).at[target].set(numbers, mode='drop')
    filled = owner < pairs
    owner = jnp.where(filled, owner, 0)
    return (owner, owner // TOPK, filled)

def attend_rows(query_block, seg_block, start, key_rows, value_rows, segment_labels):
    raw_scores = jnp.einsum('qgih,kgh->giqk', query_block, key_rows, precision=HIGHER_PRECISION)
    scores = HEAD_WIDTH ** (-0.5) * lowered_backward(raw_scores)
    query_pos = start + jnp.arange(query_block.shape[0], dtype=jnp.int32)
    key_pos = jnp.arange(key_rows.shape[0], dtype=jnp.int32)
    allowed = (seg_block[:, None] == segment_labels[None, :]) & (key_pos[None, :] <= query_pos[:, None])
    scores = jnp.where(allowed[None, None], scores, MASKED)
    row_top = lax.optimization_barrier(jnp.max(scores, axis=-1, keepdims=True))
    weights = jnp.exp(scores - row_top)
    probs = weights / lax.optimization_barrier(jnp.sum(weights, axis=-1, keepdims=True))
    return jnp.einsum('giqk,kgh->qgih', low(probs), value_rows, precision=HIGHER_PRECISION)

def sequence_layer(params, inputs, expert_list, order, segment_labels):
    attn_gain, query_key_value_weight, out_weight, moe_gain, router_weight, expert_in, expert_out = params
    length_total = inputs.shape[0]
    scale_one = lax.rsqrt(lax.optimization_barrier(jnp.mean(inputs * inputs, axis=1, keepdims=True)) + EPS)
    first_normed = low(inputs * scale_one * attn_gain)
    project_rows = lowered_backward(jnp.dot(first_normed, query_key_value_weight, precision=HIGHER_PRECISION)).reshape(length_total, KEY_VALUE_HEADS, QUERIES_PER_GROUP + 2, HEAD_WIDTH)
    cosine, sine = rope_tables(length_total, HEAD_WIDTH)
    query_rows = low(rotate(project_rows[:, :, :QUERIES_PER_GROUP], cosine, sine))
    key_rows = low(rotate(project_rows[:, :, QUERIES_PER_GROUP], cosine, sine))
    value_rows = low(project_rows[:, :, QUERIES_PER_GROUP + 1])
    block_step = min(512, length_total)
    count_total = length_total // block_step
    attend_window = jax.checkpoint(attend_rows)
    attended_rows = lax.map(lambda element_entry: attend_window(element_entry[0], element_entry[1], element_entry[2], key_rows, value_rows, segment_labels), (query_rows.reshape(count_total, block_step, KEY_VALUE_HEADS, QUERIES_PER_GROUP, HEAD_WIDTH), segment_labels.reshape(count_total, block_step), jnp.arange(count_total, dtype=jnp.int32) * block_step))
    mixed = low(lowered_backward(attended_rows.reshape(length_total, HQ * HEAD_WIDTH)))
    branch = lowered_backward(jnp.dot(mixed, out_weight, precision=HIGHER_PRECISION))
    middle = inputs + branch
    scale_two = lax.rsqrt(lax.optimization_barrier(jnp.mean(middle * middle, axis=1, keepdims=True)) + EPS)
    normed_two = low(middle * scale_two * moe_gain)
    logits = jnp.dot(normed_two, router_weight.T, precision=HIGHER_PRECISION)
    chosen = jnp.take_along_axis(logits, expert_list, axis=1)
    raised = jnp.exp(chosen)
    gates = raised / lax.optimization_barrier(jnp.sum(raised, axis=1, keepdims=True))
    owner, token_of, filled = slot_tables(expert_list, order, E, 0)
    dispatched = jnp.where(filled[:, None], normed_two[token_of], 0.0).reshape(E, CAP, D)
    gate_up = lowered_backward(jnp.einsum('ecd,edf->ecf', dispatched, expert_in, precision=HIGHER_PRECISION))
    hidden = low(jax.nn.silu(gate_up[..., :FF]) * gate_up[..., FF:])
    rows_out = lowered_backward(jnp.einsum('ecf,edf->ecd', hidden, expert_out, precision=HIGHER_PRECISION)).reshape(E * CAP, D)
    slot_gate = jnp.where(filled, gates.reshape(-1)[owner], 0.0)
    combined = jnp.zeros((length_total, D), jnp.float32).at[token_of].add(rows_out * slot_gate[:, None])
    return middle + lowered_backward(combined)

def reference(tokens, attn_gain, query_key_value_weight, out_weight, moe_gain, router_weight, expert_in, expert_out, expert_ids, route_order, segment_ids, out_grad):
    count_total = segment_ids.shape[0]
    length_total = segment_ids.shape[1]
    params = (attn_gain.astype(jnp.float32), query_key_value_weight.astype(jnp.float32), out_weight.astype(jnp.float32), moe_gain.astype(jnp.float32), router_weight.astype(jnp.float32), expert_in.astype(jnp.float32), expert_out.astype(jnp.float32))
    inputs = tokens.astype(jnp.float32).reshape(count_total, length_total, D)
    expert_list = expert_ids.reshape(count_total, length_total, TOPK)
    layer = jax.checkpoint(sequence_layer)

    def forward(inputs, params):
        return lax.map(lambda element_entry: layer(params, element_entry[0], element_entry[1], element_entry[2], element_entry[3]), (inputs, expert_list, route_order, segment_ids))
    outputs, pullback = jax.vjp(forward, inputs, params)
    input_grad, grads = pullback(out_grad.astype(jnp.float32).reshape(count_total, length_total, D))
    return (outputs.reshape(count_total * length_total, D).astype(jnp.bfloat16), input_grad.reshape(count_total * length_total, D), grads[0], grads[1], grads[2], grads[3], grads[4], grads[5], grads[6])
```

```python
import functools

import jax
import jax.numpy as jnp
from jax import lax
from jax.experimental import pallas as pl
from jax.experimental.pallas import tpu as pltpu
from jax.sharding import PartitionSpec as P

D = 1536
HEAD_WIDTH = 64
FF = 512
TOPK = 8
SEGMAX = 256
QUERIES_PER_GROUP = 3
CAP = 460
SLOTS = 464
WINDOW = 128
CHUNK = 256
LANES = 128
SUBLANES = 16

EPS = 1e-05
MASKED = -1e30
SCORE_SCALE = HEAD_WIDTH ** (-0.5)
VMEM_BYTES = 60 * 1024 * 1024
F32 = jnp.float32
BF16 = jnp.bfloat16


def dot_nn(a, b):
    return lax.dot_general(a, b, (((1,), (0,)), ((), ())), preferred_element_type=F32)


def dot_nt(a, b):
    return lax.dot_general(a, b, (((1,), (1,)), ((), ())), preferred_element_type=F32)


def dot_tn(a, b):
    return lax.dot_general(a, b, (((0,), (0,)), ((), ())), preferred_element_type=F32)


def params(**more):
    return pltpu.CompilerParams(vmem_limit_bytes=VMEM_BYTES, **more)


def cost(micros):
    return pl.CostEstimate(
        flops=int(micros * 1.1e9), bytes_accessed=int(micros * 3.6e6), transcendentals=0
    )


def store_halves(half_ref, mine_ref, other_ref, columns, value):
    slices, depth, _ = mine_ref.shape
    for parity in range(2):
        own = half_ref[0] == parity
        for ref, taken in ((mine_ref, own), (other_ref, jnp.logical_not(own))):

            @pl.when(taken)
            def _(ref=ref, parity=parity):
                for n in range(slices):
                    at = (2 * n + parity) * depth
                    ref[n, :, columns] = value[at : at + depth]


def whole(shape):
    return pl.BlockSpec(shape, lambda *_: (0,) * len(shape))


def once(shape):
    return pl.BlockSpec(shape, lambda *_: (0,) * len(shape), pipeline_mode=pl.Buffered(1))


def rope_tiles(first_row, rows):
    half = HEAD_WIDTH // 2
    freq = jnp.exp(jnp.arange(half, dtype=F32) * (-2.0 * jnp.log(10000.0) / HEAD_WIDTH))
    position = (first_row + jnp.arange(rows, dtype=jnp.int32)).astype(F32)
    angle = position[:, None] * freq[None, :]
    cosine, sine = jnp.cos(angle), jnp.sin(angle)
    return (
        jnp.concatenate([cosine] * 4, axis=1),
        jnp.concatenate([-sine, sine, -sine, sine], axis=1),
    )


def swap_halves(tile):
    lane = lax.broadcasted_iota(jnp.int32, tile.shape, 1)
    half = HEAD_WIDTH // 2
    return jnp.where(
        lane % HEAD_WIDTH < half,
        pltpu.roll(tile, LANES - half, axis=1),
        pltpu.roll(tile, half, axis=1),
    )


def rotate_tile(tile, cosine, sine, sign):
    return tile * cosine + sign * swap_halves(tile) * sine


def key_tables(cosine, sine):
    lane = lax.broadcasted_iota(jnp.int32, cosine.shape, 1)
    is_key = lane < HEAD_WIDTH
    return jnp.where(is_key, cosine, 1.0), jnp.where(is_key, sine, 0.0)


def project_kernel(normed_ref, weight_ref, cos_ref, sin_ref, query_ref, kv_ref):
    width = query_ref.shape[1] + kv_ref.shape[1]
    weight = weight_ref[...].reshape(D, weight_ref.shape[-1])[:, :width]
    project = dot_nn(normed_ref[...], weight)
    cosine, sine = cos_ref[...], sin_ref[...]
    key_cos, key_sin = key_tables(cosine, sine)
    for col in range(0, query_ref.shape[1], LANES):
        tile = rotate_tile(project[:, col : col + LANES], cosine, sine, 1.0)
        query_ref[:, col : col + LANES] = tile.astype(BF16)
    for col in range(0, kv_ref.shape[1], LANES):
        at = query_ref.shape[1] + col
        tile = rotate_tile(project[:, at : at + LANES], key_cos, key_sin, 1.0)
        kv_ref[:, col : col + LANES] = tile.astype(BF16)


def group_windows(kv, halo, group):
    col = group * 2 * HEAD_WIDTH
    keys = jnp.concatenate(
        [halo[:, col : col + HEAD_WIDTH], kv[:, col : col + HEAD_WIDTH]], axis=0
    )
    col = col + HEAD_WIDTH
    values = jnp.concatenate(
        [halo[:, col : col + HEAD_WIDTH], kv[:, col : col + HEAD_WIDTH]], axis=0
    )
    return keys, values


def stack_heads(block, group, start):
    at = group * QUERIES_PER_GROUP * HEAD_WIDTH
    return jnp.concatenate(
        [
            block[start : start + SEGMAX, at + i * HEAD_WIDTH : at + (i + 1) * HEAD_WIDTH]
            for i in range(QUERIES_PER_GROUP)
        ],
        axis=0,
    )


def probs_of(keys, queries, bias):
    scores = dot_nt(keys, queries) * SCORE_SCALE
    scores = scores + jnp.concatenate([bias] * QUERIES_PER_GROUP, axis=1)
    top = jnp.max(scores, axis=0, keepdims=True)
    weights = jnp.exp(scores - top)
    total = jnp.sum(weights, axis=0, keepdims=True)
    return weights * (1.0 / total)


def attend_kernel(query_ref, kv_ref, halo_ref, bias_ref, mixed_ref):
    rows = query_ref.shape[0]
    span = 2 * SEGMAX
    groups = kv_ref.shape[1] // (2 * HEAD_WIDTH)
    query, kv, halo = query_ref[...], kv_ref[...], halo_ref[...]
    used = groups * QUERIES_PER_GROUP * HEAD_WIDTH
    if used < mixed_ref.shape[1]:
        mixed_ref[:, used:] = jnp.zeros((rows, mixed_ref.shape[1] - used), BF16)
    for group in range(groups):
        keys, values = group_windows(kv, halo, group)
        values_t = values.T
        at = group * QUERIES_PER_GROUP * HEAD_WIDTH
        for start in range(0, rows, SEGMAX):
            queries = stack_heads(query, group, start)
            probs = probs_of(
                keys[start : start + span], queries, bias_ref[start // SEGMAX]
            ).astype(BF16)
            out_t = dot_nn(values_t[:, start : start + span], probs)
            for i in range(QUERIES_PER_GROUP):
                mixed_ref[
                    start : start + SEGMAX, at + i * HEAD_WIDTH : at + (i + 1) * HEAD_WIDTH
                ] = out_t[:, i * SEGMAX : (i + 1) * SEGMAX].T.astype(BF16)


def branch_kernel(mixed_ref, weight_ref, inputs_ref, gain_ref, middle_ref, normed_ref, total_ref):
    block = pl.program_id(0)
    weight = weight_ref[...].reshape(D, weight_ref.shape[-1])
    part = dot_nt(mixed_ref[...], weight)

    @pl.when(block == 0)
    def _():
        total_ref[...] = inputs_ref[...].astype(F32) + part

    @pl.when(block > 0)
    def _():
        total_ref[...] += part

    @pl.when(block == pl.num_programs(0) - 1)
    def _():
        middle = total_ref[...]
        scale = lax.rsqrt(jnp.mean(middle * middle, axis=1, keepdims=True) + EPS)
        middle_ref[...] = middle
        normed_ref[...] = (middle * scale * gain_ref[...]).astype(BF16)


def middle_back_kernel(
    own_ref, up_ref, down_ref, high_ref, low_ref, router_ref, middle_ref, gain_ref, grad_ref,
    middle_grad_ref, branch_ref, gain_grad_ref,
):
    grad = own_ref[...].astype(F32) + up_ref[...].astype(F32) + down_ref[...].astype(F32)
    router = router_ref[...]
    grad = grad + dot_nt(high_ref[...], router) + dot_nt(low_ref[...], router)
    back, gain_grad = norm_back(middle_ref[...], gain_ref[...], grad)
    middle_grad = grad_ref[...].astype(F32) + back
    middle_grad_ref[...] = middle_grad
    branch_ref[...] = middle_grad.astype(BF16)

    @pl.when(pl.program_id(0) == 0)
    def _():
        gain_grad_ref[...] = gain_grad

    @pl.when(pl.program_id(0) > 0)
    def _():
        gain_grad_ref[...] += gain_grad


def attend_back_kernel(
    half_ref, query_ref, kv_ref, halo_ref, bias_ref, weight_ref, mixed_ref, branch_ref,
    router_ref, cos_ref, sin_ref, dquery_ref, dkv_ref, dhalo_ref, mine_ref, other_ref,
    turned_ref, raw_ref,
):
    block = pl.program_id(0)
    rows = query_ref.shape[0]
    span = 2 * SEGMAX
    width = query_ref.shape[1]
    groups = kv_ref.shape[1] // (2 * HEAD_WIDTH)

    @pl.when(block == 0)
    def _():
        turned_ref[...] = branch_ref[...].T

    weight = weight_ref[...].reshape(D, weight_ref.shape[-1])
    mixed_grad = dot_nn(branch_ref[...], weight).astype(BF16)
    out_grad = dot_nn(turned_ref[...], mixed_ref[...]).astype(BF16)
    store_halves(half_ref, mine_ref, other_ref, slice(0, width), out_grad)
    store_halves(half_ref, mine_ref, other_ref, slice(width, width + LANES), router_ref[...])
    query, kv, halo = query_ref[...], kv_ref[...], halo_ref[...]
    used = groups * QUERIES_PER_GROUP * HEAD_WIDTH
    if used < width:
        raw_ref[:, used:] = jnp.zeros((rows, width - used), F32)
    for group in range(groups):
        keys, values = group_windows(kv, halo, group)
        keys_t = keys.T
        at = group * QUERIES_PER_GROUP * HEAD_WIDTH
        key_parts, value_parts = [], []
        for start in range(0, rows, SEGMAX):
            queries = stack_heads(query, group, start)
            grads = stack_heads(mixed_grad, group, start)
            window = keys[start : start + span]
            probs = probs_of(window, queries, bias_ref[start // SEGMAX])
            prob_grad = dot_nt(values[start : start + span], grads)
            inner = jnp.sum(probs * prob_grad, axis=0, keepdims=True)
            score_grad = (SCORE_SCALE * probs * (prob_grad - inner)).astype(BF16)
            key_parts.append(dot_nn(score_grad, queries))
            value_parts.append(dot_nn(probs.astype(BF16), grads))
            query_t = dot_nn(keys_t[:, start : start + span], score_grad)
            for i in range(QUERIES_PER_GROUP):
                raw_ref[
                    start : start + SEGMAX, at + i * HEAD_WIDTH : at + (i + 1) * HEAD_WIDTH
                ] = query_t[:, i * SEGMAX : (i + 1) * SEGMAX].T
        col = group * 2 * HEAD_WIDTH
        for parts, lane in ((key_parts, col), (value_parts, col + HEAD_WIDTH)):
            dhalo_ref[:, lane : lane + HEAD_WIDTH] = parts[0][:SEGMAX].astype(dhalo_ref.dtype)
            for n in range(len(parts)):
                own = parts[n][SEGMAX:]
                if n + 1 < len(parts):
                    own = own + parts[n + 1][:SEGMAX]
                dkv_ref[n * SEGMAX : (n + 1) * SEGMAX, lane : lane + HEAD_WIDTH] = own
    cosine, sine = cos_ref[...], sin_ref[...]
    for col in range(0, width, LANES):
        tile = rotate_tile(raw_ref[:, col : col + LANES], cosine, sine, -1.0)
        dquery_ref[:, col : col + LANES] = tile.astype(BF16)


def project_back_kernel(
    half_ref, dquery_ref, dkv_ref, halo_ref, normed_t_ref, weight_ref, cos_ref, sin_ref,
    inputs_ref, gain_ref, middle_grad_ref, mine_ref, other_ref, input_grad_ref, gain_grad_ref,
    total_ref,
):
    block = pl.program_id(0)
    rows, width = dquery_ref.shape
    key_cos, key_sin = key_tables(cos_ref[...], sin_ref[...])
    tiles = [dquery_ref[...]]
    for col in range(0, dkv_ref.shape[1], LANES):
        extra = halo_ref[:, col : col + LANES].astype(F32)
        if rows > SEGMAX:
            extra = jnp.concatenate([jnp.zeros((rows - SEGMAX, LANES), F32), extra], axis=0)
        tile = dkv_ref[:, col : col + LANES] + extra
        tiles.append(rotate_tile(tile, key_cos, key_sin, -1.0).astype(BF16))
    grads = jnp.concatenate(tiles, axis=1)
    weight = weight_ref[...].reshape(D, weight_ref.shape[-1])[:, : grads.shape[1]]
    dweight = dot_nn(normed_t_ref[...], grads).astype(BF16)
    store_halves(half_ref, mine_ref, other_ref, slice(0, grads.shape[1]), dweight)
    part = dot_nt(grads, weight)

    @pl.when(block == 0)
    def _():
        total_ref[...] = part

    @pl.when(block > 0)
    def _():
        total_ref[...] += part

    @pl.when(block == pl.num_programs(0) - 1)
    def _():
        inputs = inputs_ref[...].astype(F32)
        back, gain_grad = norm_back(inputs, gain_ref[...], total_ref[...])
        input_grad_ref[...] = middle_grad_ref[...] + back
        gain_grad_ref[...] = gain_grad


def norm_back(resid, gain, grad):
    scale = lax.rsqrt(jnp.mean(resid * resid, axis=1, keepdims=True) + EPS)
    gain_grad = jnp.sum(grad * resid * scale, axis=0, keepdims=True)
    scaled = grad * gain
    inner = jnp.sum(scaled * resid, axis=1, keepdims=True)
    return scale * scaled - resid * (scale * scale * scale * inner / D), gain_grad


def slots_kernel(experts, first_ref, ids_ref, rank_ref, pos_ref, ends_ref):
    length = ids_ref.shape[1]
    row = lax.broadcasted_iota(jnp.int32, (SUBLANES, length), 0)
    wanted = jnp.where(row < experts, row + first_ref[0], -1)
    rank = jnp.full((SUBLANES, length), 1 << 30, jnp.int32)
    for k in range(TOPK):
        rank = jnp.where(ids_ref[k : k + 1, :] == wanted, rank_ref[k : k + 1, :], rank)
    limit = jnp.zeros((SUBLANES, 1), jnp.int32)
    for bit in reversed(range((length * TOPK).bit_length())):
        higher = limit + (1 << bit)
        count = jnp.sum(jnp.where(rank < higher, 1.0, 0.0), axis=1, keepdims=True)
        limit = jnp.where(count <= CAP, higher, limit)
    kept = jnp.where(rank < limit, 1.0, 0.0)
    before = jnp.where(
        lax.broadcasted_iota(jnp.int32, (CHUNK, CHUNK), 0)
        < lax.broadcasted_iota(jnp.int32, (CHUNK, CHUNK), 1),
        1.0,
        0.0,
    ).astype(BF16)
    lane = lax.broadcasted_iota(jnp.int32, ends_ref.shape, 1)
    so_far = jnp.zeros((SUBLANES, 1), F32)
    ends = jnp.zeros(ends_ref.shape, F32)
    for n in range(length // CHUNK):
        part = kept[:, n * CHUNK : (n + 1) * CHUNK]
        place = dot_nn(part.astype(BF16), before) + so_far
        pos_ref[n] = jnp.where(part > 0.5, place, -1.0).astype(jnp.int32)
        so_far = so_far + jnp.sum(part, axis=1, keepdims=True)
        ends = jnp.where(lane == n + 1, so_far, ends)
    ends_ref[...] = ends.astype(jnp.int32)


def slot_windows(ends_ref, experts, chunk):
    firsts = [ends_ref[e, chunk] // SUBLANES * SUBLANES for e in range(experts)]
    ends = [ends_ref[e, chunk + 1] for e in range(experts)]
    count = jnp.int32(0)
    for first, end in zip(firsts, ends):
        count = jnp.maximum(count, (end - first + WINDOW - 1) // WINDOW)
    return firsts, ends, count


def dispatch_kernel(with_gates, experts, *refs):
    if with_gates:
        shard_ref, ends_ref, *x_refs, pos_ref, router_ref, member_ref, out_ref, gate_ref, hot_ref = refs
        gate_ref[...] = jnp.zeros(gate_ref.shape, F32)
    else:
        shard_ref, ends_ref, *x_refs, pos_ref, out_ref, hot_ref = refs
    out_ref[...] = jnp.zeros(out_ref.shape, BF16)
    row = lax.broadcasted_iota(jnp.int32, (WINDOW, CHUNK), 0)
    for n, x_ref in enumerate(x_refs):
        halves = x_ref.shape[0] // CHUNK
        for half in range(halves):
            chunk = shard_ref[n] * halves + half
            x = x_ref[half * CHUNK : (half + 1) * CHUNK, :]
            pos = pos_ref[chunk]
            firsts, ends, count = slot_windows(ends_ref, experts, chunk)
            if with_gates:
                logits = jnp.where(member_ref[chunk] > 0.5, dot_nn(x, router_ref[...]), MASKED)
                raised = jnp.exp(logits)
                gates = raised / jnp.sum(raised, axis=1, keepdims=True)
                lane = lax.broadcasted_iota(jnp.int32, gates.shape, 1)
                gates = jnp.where(lane < SUBLANES, gates, 0.0)
                high = gates.astype(BF16).astype(F32)
                gates = (high + pltpu.roll(gates - high, SUBLANES, axis=1)).astype(BF16)

            def body(n_window, _):
                for e in range(experts):
                    start = firsts[e] + n_window * WINDOW
                    at = jnp.minimum(start, SLOTS - WINDOW)
                    place = pos[e : e + 1, :]
                    place = jnp.where(place >= start, place - at, -1)
                    hot_ref[e * WINDOW : (e + 1) * WINDOW, :] = jnp.where(
                        row == place, 1.0, 0.0
                    ).astype(BF16)
                hot = hot_ref[...]
                rows = dot_nn(hot, x)
                if with_gates:
                    gate_rows = dot_nn(hot, gates)
                for e in range(experts):
                    start = firsts[e] + n_window * WINDOW
                    at = pl.multiple_of(jnp.minimum(start, SLOTS - WINDOW), SUBLANES)

                    @pl.when(start < ends[e])
                    def _():
                        out_ref[e, pl.ds(at, WINDOW), :] += rows[
                            e * WINDOW : (e + 1) * WINDOW
                        ].astype(BF16)
                        if with_gates:
                            gate_ref[e, pl.ds(at, WINDOW), :] += gate_rows[
                                e * WINDOW : (e + 1) * WINDOW
                            ]

                return 0

            lax.fori_loop(0, count, body, 0)


def combine_kernel(with_pairs, sizes, *refs):
    piece_ref, ends_ref, place_ref = refs[:3]
    rows_refs = refs[3 : 3 + len(sizes)]
    refs = refs[3 + len(sizes) :]
    if with_pairs:
        pair_refs = refs[: len(sizes)]
        *out_refs, pair_out_ref, held_ref, held_pair_ref, hot_ref, total_ref = refs[len(sizes) :]
    else:
        *out_refs, held_ref, hot_ref, total_ref = refs
    experts = sum(sizes)
    home = [(n, e) for n, size in enumerate(sizes) for e in range(size)]
    halves = pl.num_programs(0) // len(out_refs)
    piece = pl.program_id(0) // halves
    chunk = piece_ref[piece] * halves + pl.program_id(0) % halves
    firsts, ends, count = slot_windows(ends_ref, experts, chunk)
    lane = lax.broadcasted_iota(jnp.int32, (CHUNK, WINDOW), 1)
    places = place_ref[...]
    total_ref[...] = jnp.zeros(total_ref.shape, F32)
    if with_pairs:
        pair_out_ref[...] = jnp.zeros(pair_out_ref.shape, F32)

    def body(n_window, _):
        for e in range(experts):
            start = firsts[e] + n_window * WINDOW
            at = pl.multiple_of(jnp.minimum(start, SLOTS - WINDOW), SUBLANES)
            place = places[:, e : e + 1]
            place = jnp.where(place >= start, place - at, -1)
            cols = slice(e * WINDOW, (e + 1) * WINDOW)
            hot_ref[:, cols] = jnp.where(lane == place, 1.0, 0.0).astype(BF16)
            n, own = home[e]
            held_ref[cols, :] = rows_refs[n][own, pl.ds(at, WINDOW), :]
            if with_pairs:
                held_pair_ref[cols, :] = pair_refs[n][own, pl.ds(at, WINDOW), :]
        hot = hot_ref[...]
        total_ref[...] += dot_nn(hot, held_ref[...])
        if with_pairs:
            pair_out_ref[...] += dot_nn(hot, held_pair_ref[...])
        return 0

    lax.fori_loop(0, count, body, 0)
    for n, out_ref in enumerate(out_refs):

        @pl.when(piece == n)
        def _():
            out_ref[...] = total_ref[...].astype(BF16)


def expert_kernel(
    first, half_ref, x_ref, grad_ref, gate_ref, weight_ref,
    y_ref, z_ref, pair_ref, mine_ref, other_ref,
):
    e = first + pl.program_id(0)
    x, slot_grad = x_ref[0], grad_ref[0]
    w_in, w_out = weight_ref[0, :, : 2 * FF], weight_ref[0, :, 2 * FF :]
    lane = lax.broadcasted_iota(jnp.int32, gate_ref.shape[1:], 1)
    gate = jnp.sum(
        jnp.where((lane == e) | (lane == e + SUBLANES), gate_ref[0], 0.0), axis=1, keepdims=True
    )
    gate_up = dot_nn(x, w_in)
    gate_part, up_part = gate_up[:, :FF], gate_up[:, FF:]
    sigmoid = jax.nn.sigmoid(gate_part)
    silu = gate_part * sigmoid
    hidden = (silu * up_part).astype(BF16)
    raw = dot_nn(slot_grad, w_out)
    pair = jnp.sum(hidden.astype(F32) * raw, axis=1, keepdims=True)
    high = pair.astype(BF16).astype(F32)
    pair_ref[0] = jnp.where(
        lane == e, high, jnp.where(lane == e + SUBLANES, pair - high, 0.0)
    ).astype(BF16)
    hidden_grad = gate * raw
    gate_up_grad = jnp.concatenate(
        [
            (hidden_grad * up_part * sigmoid * (1.0 + gate_part * (1.0 - sigmoid))).astype(BF16),
            (hidden_grad * silu).astype(BF16),
        ],
        axis=1,
    )
    z_ref[0] = dot_nt(gate_up_grad, w_in).astype(BF16)
    y_ref[0] = (gate * dot_nt(hidden, w_out)).astype(BF16)
    rows_grad = (gate * slot_grad.astype(F32)).astype(BF16)
    in_term = dot_tn(x, gate_up_grad).astype(BF16)
    out_term = dot_tn(rows_grad, hidden).astype(BF16)
    store_halves(half_ref, mine_ref, other_ref, slice(0, 2 * FF), in_term)
    store_halves(half_ref, mine_ref, other_ref, slice(2 * FF, 3 * FF), out_term)


def after(value, *others):
    return lax.optimization_barrier((value,) + others)[0]


def pair_scatter(mine, other, size, *gates):
    taken = after(lax.ppermute(other, "gx", [(s, s ^ 1) for s in range(size)]), *gates)
    mine = (mine.astype(F32) + taken.astype(F32)).astype(mine.dtype)
    groups = [list(range(0, size, 2)), list(range(1, size, 2))]
    total = lax.psum_scatter(mine, "gx", scatter_dimension=0, tiled=True, axis_index_groups=groups)
    return lax.optimization_barrier(total)[0]


def direct_gather(part, size):
    return jnp.stack(
        [part]
        + [
            lax.ppermute(part, "gy", [(s, (s + k) % size) for s in range(size)])
            for k in range(1, size)
        ]
    )


def chain_gather(part, size):
    me = lax.axis_index("gy")
    rising, falling, up, down = [], [], part, part
    for step in range(size - 1):
        up = lax.ppermute(up, "gy", [(s, s + 1) for s in range(step, size - 1)])
        down = lax.ppermute(down, "gy", [(s + 1, s) for s in range(0, size - 1 - step)])
        rising.append(up)
        falling.append(down)
    pieces = [part] + [
        jnp.where(me >= k, rising[k - 1], falling[size - 1 - k]) for k in range(1, size)
    ]
    return pieces, list(zip(rising, falling))


def chain_sum(parts, size):
    def added(a, b):
        return (a.astype(F32) + b.astype(F32)).astype(a.dtype)

    steps, up, down = [], None, None
    for step in range(1, size):
        above, below = parts[step], parts[size - step]
        above = above if up is None else added(above, up)
        below = below if down is None else added(below, down)
        up = lax.ppermute(above, "gy", [(s, s + 1) for s in range(step)])
        down = lax.ppermute(below, "gy", [(size - 1 - s, size - 2 - s) for s in range(step)])
        steps.append((up, down))
    return parts[0].astype(F32) + up.astype(F32) + down.astype(F32), steps


def shards(
    nx,
    ny,
    tokens,
    attn_gain,
    query_key_value_weight,
    out_weight,
    moe_gain,
    router_weight,
    expert_in,
    expert_out,
    expert_ids,
    route_order,
    segment_ids,
    out_grad,
):
    rows = tokens.shape[0]
    length = segment_ids.shape[1]
    depth = out_weight.shape[1]
    heads_width = out_weight.shape[0]
    groups = heads_width // (HEAD_WIDTH * QUERIES_PER_GROUP)
    spare = -heads_width % LANES
    width = heads_width + spare
    kv_width = groups * 2 * HEAD_WIDTH
    joined = width + kv_width
    experts = router_weight.shape[0]
    all_experts = experts * ny
    chunks = length // CHUNK
    me = lax.axis_index("gy")
    first_expert = me * experts
    first_row = me * rows
    both = ("gx", "gy")

    pos, ends = pl.pallas_call(
        functools.partial(slots_kernel, experts),
        in_specs=[
            pl.BlockSpec(memory_space=pltpu.SMEM),
            pl.BlockSpec(memory_space=pltpu.VMEM),
            pl.BlockSpec(memory_space=pltpu.VMEM),
        ],
        out_shape=[
            jax.ShapeDtypeStruct((chunks, SUBLANES, CHUNK), jnp.int32),
            jax.ShapeDtypeStruct((SUBLANES, LANES), jnp.int32),
        ],
        compiler_params=params(),
        cost_estimate=cost(3),
        name="slots",
    )(
        first_expert.reshape(1),
        expert_ids.T,
        route_order[0].reshape(length, TOPK).T,
    )
    places = jnp.pad(
        pos.transpose(0, 2, 1).reshape(length, SUBLANES), ((0, 0), (0, LANES - SUBLANES))
    )
    ends = ends[:, : chunks + 1]
    pieces = (me - jnp.arange(ny, dtype=jnp.int32)) % ny
    lane_expert = jnp.arange(LANES, dtype=jnp.int32)
    turned_expert = (me - lane_expert // experts) % ny * experts + lane_expert % experts
    turned_expert = jnp.where(lane_expert < all_experts, turned_expert, -1)
    members = jnp.any(expert_ids[:, :, None] == turned_expert[None, None, :], axis=1)
    members = members.astype(F32).reshape(chunks, CHUNK, LANES)
    own_ids = lax.dynamic_slice_in_dim(expert_ids, first_row, rows, 0)
    own_members = jnp.any(own_ids[:, :, None] == turned_expert[None, None, :], axis=1).astype(F32)

    grouped = query_key_value_weight.reshape(depth, groups, QUERIES_PER_GROUP + 2, HEAD_WIDTH)
    own_joined = jnp.concatenate(
        [
            jnp.pad(
                grouped[:, :, :QUERIES_PER_GROUP].reshape(depth, heads_width), ((0, 0), (0, spare))
            ),
            grouped[:, :, QUERIES_PER_GROUP:].reshape(depth, kv_width),
        ],
        axis=1,
    )
    own_second = jnp.concatenate(
        [
            jnp.pad(out_weight.T, ((0, 0), (0, spare))),
            jnp.pad(router_weight.T, ((0, 0), (0, LANES - experts))),
        ],
        axis=1,
    )
    line_joined = direct_gather(own_joined, ny)
    line_second = direct_gather(after(own_second, line_joined, pos, ends, places, members), ny)
    joined_weights = lax.all_gather(line_joined, "gx", axis=0)
    second_weights = lax.all_gather(line_second, "gx", axis=0)
    cut = experts // 2
    bounds = ((0, cut), (cut, experts))
    own_experts = [
        jnp.concatenate([expert_in[lo:hi], expert_out[lo:hi]], axis=2) for lo, hi in bounds
    ]
    wide = []
    for own in own_experts:
        wide.append(lax.all_gather(own, "gx", axis=1, tiled=True))

    grad_pieces, grad_steps = chain_gather(after(out_grad, line_joined), ny)

    inputs = tokens.astype(F32)
    scale_one = lax.rsqrt(jnp.mean(inputs * inputs, axis=1, keepdims=True) + EPS)
    normed_one = (inputs * scale_one * attn_gain[None, :]).astype(BF16)
    normed_one_t = normed_one.T
    cosine, sine = rope_tiles(first_row, rows)
    labels = jnp.concatenate([jnp.full((SEGMAX,), -1, jnp.int32), segment_ids[0]])
    labels = lax.dynamic_slice_in_dim(labels, first_row, rows + SEGMAX, 0)
    position = jnp.arange(rows + SEGMAX, dtype=jnp.int32)
    bias = jnp.stack(
        [
            jnp.where(
                (labels[s : s + 2 * SEGMAX, None] == labels[None, s + SEGMAX : s + 2 * SEGMAX])
                & (
                    position[s : s + 2 * SEGMAX, None]
                    <= position[None, s + SEGMAX : s + 2 * SEGMAX]
                ),
                0.0,
                MASKED,
            ).astype(F32)
            for s in range(0, rows, SEGMAX)
        ]
    )
    weight_spec = pl.BlockSpec((nx, pl.Squeezed(), depth, joined), lambda b: (0, b, 0, 0))
    out_spec = pl.BlockSpec((nx, pl.Squeezed(), depth, width), lambda b: (0, b, 0, 0))
    query, kv = pl.pallas_call(
        project_kernel,
        grid=(ny,),
        in_specs=[
            whole((rows, D)),
            weight_spec,
            whole((rows, LANES)),
            whole((rows, LANES)),
        ],
        out_specs=[
            pl.BlockSpec((rows, width), lambda b: (0, b)),
            pl.BlockSpec((rows, kv_width), lambda b: (0, b)),
        ],
        out_shape=[
            jax.ShapeDtypeStruct((rows, ny * width), BF16),
            jax.ShapeDtypeStruct((rows, ny * kv_width), BF16),
        ],
        compiler_params=params(),
        cost_estimate=cost(10),
        name="project",
    )(after(normed_one, bias, grad_steps[0]), joined_weights, cosine, sine)
    halo = lax.ppermute(kv[rows - SEGMAX :], "gy", [(s, s + 1) for s in range(ny - 1)])
    block_rows = lambda n, w: pl.BlockSpec((n, w), lambda b: (0, b))
    below_rows = lambda n, w: pl.BlockSpec((n, w), lambda b: (0, (b + ny - 1) % ny))
    above_rows = lambda n, w: pl.BlockSpec((n, w), lambda b: (0, (b + 1) % ny))
    mixed = pl.pallas_call(
        attend_kernel,
        grid=(ny,),
        in_specs=[
            block_rows(rows, width),
            block_rows(rows, kv_width),
            below_rows(SEGMAX, kv_width),
            whole(bias.shape),
        ],
        out_specs=block_rows(rows, width),
        out_shape=jax.ShapeDtypeStruct((rows, ny * width), BF16),
        compiler_params=params(),
        cost_estimate=cost(20),
        name="attend",
    )(query, kv, halo, bias)
    middle, normed_two = pl.pallas_call(
        branch_kernel,
        grid=(ny,),
        in_specs=[block_rows(rows, width), out_spec, whole((rows, D)), whole((1, D))],
        out_specs=[whole((rows, D)), whole((rows, D))],
        out_shape=[
            jax.ShapeDtypeStruct((rows, D), F32),
            jax.ShapeDtypeStruct((rows, D), BF16),
        ],
        scratch_shapes=[pltpu.VMEM((rows, D), F32)],
        compiler_params=params(),
        cost_estimate=cost(7),
        name="branch",
    )(mixed, second_weights, after(tokens, grad_steps[1]), moe_gain[None, :])

    router = second_weights[:, :, :, width : width + experts].transpose(0, 2, 1, 3)
    router = router.reshape(D, all_experts)
    router = jnp.pad(router, ((0, 0), (0, LANES - all_experts)))
    normed_pieces = chain_gather(normed_two, ny)[0]
    smem = pl.BlockSpec(memory_space=pltpu.SMEM)
    vmem = pl.BlockSpec(memory_space=pltpu.VMEM)
    slot_rows = jax.ShapeDtypeStruct((experts, SLOTS, D), BF16)
    slot_lanes = lambda kind: jax.ShapeDtypeStruct((experts, SLOTS, LANES), kind)
    hot = pltpu.VMEM((experts * WINDOW, CHUNK), BF16)
    slot_grads = pl.pallas_call(
        functools.partial(dispatch_kernel, False, experts),
        in_specs=[smem, smem] + [vmem] * (ny + 1),
        out_specs=vmem,
        out_shape=slot_rows,
        scratch_shapes=[hot],
        compiler_params=params(),
        cost_estimate=cost(26),
        name="dispatch_grads",
    )(pieces, ends, *grad_pieces, pos)
    dispatched, slot_gates = pl.pallas_call(
        functools.partial(dispatch_kernel, True, experts),
        in_specs=[smem, smem] + [vmem] * (ny + 3),
        out_specs=[vmem, vmem],
        out_shape=[slot_rows, slot_lanes(F32)],
        scratch_shapes=[hot],
        compiler_params=params(),
        cost_estimate=cost(31),
        name="dispatch_rows",
    )(pieces, ends, *normed_pieces, pos, router, members)

    half = (lax.axis_index("gx") % 2).reshape(1)
    y_rows, z_rows, slot_pairs, weight_terms = [], [], [], []
    for n, (lo, hi) in enumerate(bounds):
        outer = lambda *shape: pl.BlockSpec((1,) + shape, lambda e, lo=lo: (lo + e, 0, 0))
        inner = lambda *shape: pl.BlockSpec((1,) + shape, lambda e: (e, 0, 0))
        slices = pl.BlockSpec((nx // 2, pl.Squeezed(), depth, 3 * FF), lambda e: (0, e, 0, 0))
        y, z, pair, mine, other = pl.pallas_call(
            functools.partial(expert_kernel, lo),
            grid=(hi - lo,),
            in_specs=[
                smem,
                outer(SLOTS, D),
                outer(SLOTS, D),
                outer(SLOTS, LANES),
                inner(D, 3 * FF),
            ],
            out_specs=[inner(SLOTS, D), inner(SLOTS, D), inner(SLOTS, LANES), slices, slices],
            out_shape=[
                jax.ShapeDtypeStruct((hi - lo, SLOTS, D), BF16),
                jax.ShapeDtypeStruct((hi - lo, SLOTS, D), BF16),
                jax.ShapeDtypeStruct((hi - lo, SLOTS, LANES), BF16),
                jax.ShapeDtypeStruct((nx // 2, hi - lo, depth, 3 * FF), BF16),
                jax.ShapeDtypeStruct((nx // 2, hi - lo, depth, 3 * FF), BF16),
            ],
            compiler_params=params(),
            cost_estimate=cost(43),
            name="experts",
        )(half, dispatched, slot_grads, slot_gates, wide[n])
        y_rows.append(y)
        z_rows.append(z)
        slot_pairs.append(pair)
        weight_terms.append((mine, other))
    def combine(rows_in, which, pairs=None):
        held = pltpu.VMEM((experts * WINDOW, D), BF16)
        hot_t = pltpu.VMEM((CHUNK, experts * WINDOW), BF16)
        total = pltpu.VMEM((CHUNK, D), F32)
        more = pairs is not None
        halves = chunks // ny
        here = pieces[jnp.array(which)]

        def place_map(c, piece_ref):
            return (piece_ref[c // halves] * halves + c % halves, 0)

        def out_map(n):
            return lambda c, piece_ref: (jnp.clip(c - n * halves, 0, halves - 1), 0)

        return pl.pallas_call(
            functools.partial(combine_kernel, more, tuple(hi - lo for lo, hi in bounds)),
            grid_spec=pltpu.PrefetchScalarGridSpec(
                num_scalar_prefetch=1,
                grid=(halves * len(which),),
                in_specs=[smem, pl.BlockSpec((CHUNK, LANES), place_map)]
                + [once((hi - lo, SLOTS, D)) for lo, hi in bounds]
                + [once((hi - lo, SLOTS, LANES)) for lo, hi in bounds] * more,
                out_specs=[pl.BlockSpec((CHUNK, D), out_map(n)) for n in range(len(which))]
                + [pl.BlockSpec((CHUNK, LANES), lambda c, _: (c, 0))] * more,
                scratch_shapes=[held]
                + [pltpu.VMEM((experts * WINDOW, LANES), BF16)] * more
                + [hot_t, total],
            ),
            out_shape=[jax.ShapeDtypeStruct((rows, D), BF16)] * len(which)
            + [jax.ShapeDtypeStruct((len(which) * rows, LANES), F32)] * more,
            compiler_params=params(),
            cost_estimate=cost(5 * len(which)),
            name="combine_grads" if more else "combine_rows",
        )(here, ends, places, *rows_in, *(pairs if more else []))

    outer_pieces = sorted({1, ny - 1})
    inner_pieces = [k for k in range(ny) if k not in outer_pieces]
    token_sum, pair_lanes = [None] * ny, [None] * ny
    for which in (outer_pieces, inner_pieces):
        *sums, lanes = combine(z_rows, which, slot_pairs)
        for n, k in enumerate(which):
            token_sum[k] = sums[n]
            pair_lanes[k] = lanes[n * rows : (n + 1) * rows]
    weight_sums = [
        pair_scatter(*weight_terms[0], nx),
        pair_scatter(*weight_terms[1], nx, token_sum[outer_pieces[0]]),
    ]
    gathered = []
    for k in range(ny):
        lanes = pair_lanes[-k % ny]
        mine = (lanes[:, :experts] + lanes[:, SUBLANES : SUBLANES + experts]).T
        gathered.append(
            mine if k == 0 else lax.ppermute(mine, "gy", [(s, (s + k) % ny) for s in range(ny)])
        )
    own_pairs = jnp.concatenate(gathered, axis=0).T
    own_pairs = jnp.pad(own_pairs, ((0, 0), (0, LANES - all_experts)))
    own_logits = jnp.where(own_members > 0.5, dot_nn(normed_two, router), MASKED)
    own_raised = jnp.exp(own_logits)
    own_gates = own_raised / jnp.sum(own_raised, axis=1, keepdims=True)
    logit_grad = own_gates * (own_pairs - jnp.sum(own_gates * own_pairs, axis=1, keepdims=True))
    high = logit_grad.astype(BF16)
    low = (logit_grad - high.astype(F32)).astype(BF16)
    router_term = dot_tn(normed_two, high) + dot_tn(normed_two, low)
    router_term = router_term[:, :all_experts].reshape(D, ny, experts).transpose(1, 0, 2)
    router_term = jnp.pad(router_term.astype(BF16), ((0, 0), (0, 0), (0, LANES - experts)))

    _, token_steps = chain_sum(token_sum, ny)
    row_block = lambda w: pl.BlockSpec((LANES, w), lambda r: (r, 0))
    middle_grad, branch_grad, moe_gain_grad = pl.pallas_call(
        middle_back_kernel,
        grid=(rows // LANES,),
        in_specs=[row_block(D)] * 3
        + [row_block(LANES)] * 2
        + [whole((D, LANES)), row_block(D), whole((1, D)), row_block(D)],
        out_specs=[row_block(D), row_block(D), whole((1, D))],
        out_shape=[
            jax.ShapeDtypeStruct((rows, D), F32),
            jax.ShapeDtypeStruct((rows, D), BF16),
            jax.ShapeDtypeStruct((1, D), F32),
        ],
        compiler_params=params(),
        cost_estimate=cost(6),
        name="middle_back",
    )(token_sum[0], *token_steps[-1], high, low, router, middle, moe_gain[None, :], out_grad)

    combined = combine(y_rows, outer_pieces + inner_pieces)
    combined = [combined[(outer_pieces + inner_pieces).index(k)] for k in range(ny)]
    combined_sum, sum_steps = chain_sum([after(part, branch_grad) for part in combined], ny)
    layer_out = (middle + combined_sum).astype(BF16)

    slices = lambda w: pl.BlockSpec(
        (nx // 2, pl.Squeezed(), depth, w), lambda b: (0, b, 0, 0)
    )
    sliced = lambda w: jax.ShapeDtypeStruct((nx // 2, ny, depth, w), BF16)
    dquery, dkv, dhalo, *second_terms = pl.pallas_call(
        attend_back_kernel,
        grid=(ny,),
        in_specs=[
            smem,
            block_rows(rows, width),
            block_rows(rows, kv_width),
            below_rows(SEGMAX, kv_width),
            whole(bias.shape),
            out_spec,
            block_rows(rows, width),
            whole((rows, D)),
            pl.BlockSpec((pl.Squeezed(), D, LANES), lambda b: (b, 0, 0)),
            whole((rows, LANES)),
            whole((rows, LANES)),
        ],
        out_specs=[
            block_rows(rows, width),
            block_rows(rows, kv_width),
            block_rows(SEGMAX, kv_width),
            slices(width + LANES),
            slices(width + LANES),
        ],
        out_shape=[
            jax.ShapeDtypeStruct((rows, ny * width), BF16),
            jax.ShapeDtypeStruct((rows, ny * kv_width), F32),
            jax.ShapeDtypeStruct((SEGMAX, ny * kv_width), BF16),
            sliced(width + LANES),
            sliced(width + LANES),
        ],
        scratch_shapes=[pltpu.VMEM((D, rows), BF16), pltpu.VMEM((rows, width), F32)],
        compiler_params=params(),
        cost_estimate=cost(37),
        name="attend_back",
    )(half, query, kv, halo, bias, second_weights, mixed, after(branch_grad, weight_sums[0], combined), router_term,
      cosine, sine)
    halo_grad = lax.ppermute(dhalo, "gy", [(s + 1, s) for s in range(ny - 1)])
    *joined_terms, input_grad, attn_gain_grad = pl.pallas_call(
        project_back_kernel,
        grid=(ny,),
        in_specs=[
            smem,
            block_rows(rows, width),
            block_rows(rows, kv_width),
            above_rows(SEGMAX, kv_width),
            whole((D, rows)),
            weight_spec,
            whole((rows, LANES)),
            whole((rows, LANES)),
            whole((rows, D)),
            whole((1, D)),
            whole((rows, D)),
        ],
        out_specs=[
            slices(joined),
            slices(joined),
            whole((rows, D)),
            whole((1, D)),
        ],
        out_shape=[
            sliced(joined),
            sliced(joined),
            jax.ShapeDtypeStruct((rows, D), F32),
            jax.ShapeDtypeStruct((1, D), F32),
        ],
        scratch_shapes=[pltpu.VMEM((rows, D), F32)],
        compiler_params=params(),
        cost_estimate=cost(21),
        name="project_back",
    )(half, dquery, dkv, halo_grad, normed_one_t, joined_weights, cosine, sine, tokens, attn_gain[None, :],
      after(middle_grad, sum_steps[0]))

    second_sum = pair_scatter(*second_terms, nx, dkv)
    joined_sum = pair_scatter(*joined_terms, nx, weight_sums[-1], second_sum, sum_steps[1])
    gain_sums = jnp.concatenate([attn_gain_grad, moe_gain_grad])
    for axis, size in (("gx", nx), ("gy", ny)):
        bit = 1
        while bit < size:
            pairs = [(s, s ^ bit) for s in range(size)]
            gain_sums = gain_sums + lax.ppermute(gain_sums, axis, pairs)
            bit = 2 * bit
    second_sum = chain_sum([second_sum[k] for k in range(ny)], ny)[0]
    joined_sum = chain_sum([joined_sum[k] for k in range(ny)], ny)[0]
    weight_sum = jnp.concatenate(weight_sums, axis=0).astype(F32)
    in_grad, down_grad = weight_sum[..., : 2 * FF], weight_sum[..., 2 * FF :]
    qkv_grad = jnp.concatenate(
        [
            joined_sum[:, :heads_width].reshape(depth, groups, QUERIES_PER_GROUP, HEAD_WIDTH),
            joined_sum[:, width:].reshape(depth, groups, 2, HEAD_WIDTH),
        ],
        axis=2,
    ).reshape(query_key_value_weight.shape)
    out_weight_grad = second_sum[:, :heads_width].T
    router_grad = second_sum[:, width : width + experts].T
    return (
        layer_out,
        input_grad,
        gain_sums[0],
        qkv_grad,
        out_weight_grad,
        gain_sums[1],
        router_grad,
        in_grad,
        down_grad,
    )


def solution(mesh):
    in_specs = (
        P(("gx", "gy"), None),
        P(),
        P("gx", "gy"),
        P("gy", "gx"),
        P(),
        P("gy", "gx"),
        P("gy", "gx", None),
        P("gy", "gx", None),
        P("gx", None),
        P("gx", None),
        P("gx", None),
        P(("gx", "gy"), None),
    )
    out_specs = (
        P(("gx", "gy"), None),
        P(("gx", "gy"), None),
        P(),
        P("gx", "gy"),
        P("gy", "gx"),
        P(),
        P("gy", "gx"),
        P("gy", "gx", None),
        P("gy", "gx", None),
    )
    body = functools.partial(shards, mesh.shape["gx"], mesh.shape["gy"])
    return jax.shard_map(body, mesh=mesh, in_specs=in_specs, out_specs=out_specs, check_vma=False)
```

```python
import functools

import jax
import jax.numpy as jnp
from jax import lax
from jax.experimental import pallas as pl
from jax.experimental.pallas import tpu as pltpu
from jax.sharding import PartitionSpec as P

D = 1536
HEAD_WIDTH = 64
FF = 512
TOPK = 8
SEGMAX = 256
QUERIES_PER_GROUP = 3
CAP = 460
SLOTS = 464
WINDOW = 128
SHORT_WINDOW = 96
CHUNK = 256
LANES = 128
SUBLANES = 16

EPS = 1e-05
MASKED = -1e30
SCORE_SCALE = HEAD_WIDTH ** (-0.5)
VMEM_BYTES = 60 * 1024 * 1024
F32 = jnp.float32
BF16 = jnp.bfloat16


def dot_nn(a, b):
    return lax.dot_general(a, b, (((1,), (0,)), ((), ())), preferred_element_type=F32)


def dot_nt(a, b):
    return lax.dot_general(a, b, (((1,), (1,)), ((), ())), preferred_element_type=F32)


def dot_tn(a, b):
    return lax.dot_general(a, b, (((0,), (0,)), ((), ())), preferred_element_type=F32)


def params(**more):
    return pltpu.CompilerParams(vmem_limit_bytes=VMEM_BYTES, **more)


def cost(micros):
    return pl.CostEstimate(
        flops=int(micros * 1.1e9), bytes_accessed=int(micros * 3.6e6), transcendentals=0
    )


def store_halves(half_ref, mine_ref, other_ref, columns, value):
    slices, depth, _ = mine_ref.shape
    for parity in range(2):
        own = half_ref[0] == parity
        for ref, taken in ((mine_ref, own), (other_ref, jnp.logical_not(own))):

            @pl.when(taken)
            def _(ref=ref, parity=parity):
                for n in range(slices):
                    at = (2 * n + parity) * depth
                    ref[n, :, columns] = value[at : at + depth]


def whole(shape):
    return pl.BlockSpec(shape, lambda *_: (0,) * len(shape))


def once(shape):
    return pl.BlockSpec(shape, lambda *_: (0,) * len(shape), pipeline_mode=pl.Buffered(1))


def rope_tiles(first_row, rows):
    half = HEAD_WIDTH // 2
    freq = jnp.exp(jnp.arange(half, dtype=F32) * (-2.0 * jnp.log(10000.0) / HEAD_WIDTH))
    position = (first_row + jnp.arange(rows, dtype=jnp.int32)).astype(F32)
    angle = position[:, None] * freq[None, :]
    cosine, sine = jnp.cos(angle), jnp.sin(angle)
    return (
        jnp.concatenate([cosine] * 4, axis=1),
        jnp.concatenate([-sine, sine, -sine, sine], axis=1),
    )


def swap_halves(tile):
    lane = lax.broadcasted_iota(jnp.int32, tile.shape, 1)
    half = HEAD_WIDTH // 2
    return jnp.where(
        lane % HEAD_WIDTH < half,
        pltpu.roll(tile, LANES - half, axis=1),
        pltpu.roll(tile, half, axis=1),
    )


def rotate_tile(tile, cosine, sine, sign):
    return tile * cosine + sign * swap_halves(tile) * sine


def key_tables(cosine, sine):
    lane = lax.broadcasted_iota(jnp.int32, cosine.shape, 1)
    is_key = lane < HEAD_WIDTH
    return jnp.where(is_key, cosine, 1.0), jnp.where(is_key, sine, 0.0)


def hold_weight(first_ref, rest_ref, held_ref):
    @pl.when(pl.program_id(0) == 0)
    def _():
        held_ref[...] = first_ref[...].reshape(held_ref.shape)

    @pl.when(pl.program_id(0) > 0)
    def _():
        held_ref[...] = rest_ref[...].reshape(held_ref.shape)


def project_kernel(
    normed_ref, first_ref, rest_ref, cos_ref, sin_ref, query_ref, kv_ref, held_ref
):
    hold_weight(first_ref, rest_ref, held_ref)
    project = dot_nn(normed_ref[...], held_ref[...])
    cosine, sine = cos_ref[...], sin_ref[...]
    key_cos, key_sin = key_tables(cosine, sine)
    for col in range(0, query_ref.shape[1], LANES):
        tile = rotate_tile(project[:, col : col + LANES], cosine, sine, 1.0)
        query_ref[:, col : col + LANES] = tile.astype(BF16)
    for col in range(0, kv_ref.shape[1], LANES):
        at = query_ref.shape[1] + col
        tile = rotate_tile(project[:, at : at + LANES], key_cos, key_sin, 1.0)
        kv_ref[:, col : col + LANES] = tile.astype(BF16)


def group_windows(before, own, group):
    col = group * 2 * HEAD_WIDTH
    return [
        jnp.concatenate([before[:, at : at + HEAD_WIDTH], own[:, at : at + HEAD_WIDTH]], axis=0)
        for at in (col, col + HEAD_WIDTH)
    ]


def stack_heads(block, group):
    at = group * QUERIES_PER_GROUP * HEAD_WIDTH
    return jnp.concatenate(
        [
            block[:, at + i * HEAD_WIDTH : at + (i + 1) * HEAD_WIDTH]
            for i in range(QUERIES_PER_GROUP)
        ],
        axis=0,
    )


def store_heads(ref, group, value_t):
    at = group * QUERIES_PER_GROUP * HEAD_WIDTH
    for i in range(QUERIES_PER_GROUP):
        part = value_t[:, i * SEGMAX : (i + 1) * SEGMAX].T
        ref[:, at + i * HEAD_WIDTH : at + (i + 1) * HEAD_WIDTH] = part.astype(ref.dtype)


def clear_spare(ref, groups):
    used = groups * QUERIES_PER_GROUP * HEAD_WIDTH
    if used < ref.shape[1]:
        ref[:, used:] = jnp.zeros((ref.shape[0], ref.shape[1] - used), ref.dtype)


def probs_of(keys, queries, bias):
    scores = dot_nt(keys, queries) * SCORE_SCALE
    scores = scores + jnp.concatenate([bias] * QUERIES_PER_GROUP, axis=1)
    top = jnp.max(scores, axis=0, keepdims=True)
    weights = jnp.exp(scores - top)
    total = jnp.sum(weights, axis=0, keepdims=True)
    return weights * (1.0 / total)


def attend_kernel(query_ref, own_ref, before_ref, bias_ref, mixed_ref):
    groups = own_ref.shape[1] // (2 * HEAD_WIDTH)
    query, own, before, bias = query_ref[...], own_ref[...], before_ref[...], bias_ref[...]
    clear_spare(mixed_ref, groups)
    for group in range(groups):
        keys, values = group_windows(before, own, group)
        probs = probs_of(keys, stack_heads(query, group), bias).astype(BF16)
        store_heads(mixed_ref, group, dot_nn(values.T, probs))


def attend_back_kernel(
    query_ref, own_ref, before_ref, bias_ref, first_ref, rest_ref, branch_ref, cos_ref, sin_ref,
    dquery_ref, down_ref, dbefore_ref, raw_ref, held_ref,
):
    groups = own_ref.shape[1] // (2 * HEAD_WIDTH)
    hold_weight(first_ref, rest_ref, held_ref)
    mixed_grad = dot_nn(branch_ref[...], held_ref[...]).astype(BF16)
    query, own, before, bias = query_ref[...], own_ref[...], before_ref[...], bias_ref[...]
    clear_spare(raw_ref, groups)
    for group in range(groups):
        keys, values = group_windows(before, own, group)
        queries, grads = stack_heads(query, group), stack_heads(mixed_grad, group)
        probs = probs_of(keys, queries, bias)
        prob_grad = dot_nt(values, grads)
        inner = jnp.sum(probs * prob_grad, axis=0, keepdims=True)
        score_grad = (SCORE_SCALE * probs * (prob_grad - inner)).astype(BF16)
        store_heads(raw_ref, group, dot_nn(keys.T, score_grad))
        col = group * 2 * HEAD_WIDTH
        for at, part in (
            (col, dot_nn(score_grad, queries)),
            (col + HEAD_WIDTH, dot_nn(probs.astype(BF16), grads)),
        ):
            dbefore_ref[:, at : at + HEAD_WIDTH] = part[:SEGMAX].astype(dbefore_ref.dtype)
            down_ref[:, at : at + HEAD_WIDTH] = part[SEGMAX:]
    cosine, sine = cos_ref[...], sin_ref[...]
    for col in range(0, query_ref.shape[1], LANES):
        tile = rotate_tile(raw_ref[:, col : col + LANES], cosine, sine, -1.0)
        dquery_ref[:, col : col + LANES] = tile.astype(BF16)


def branch_weights_kernel(experts, halves, normed_t_ref, *refs):
    branch_refs, refs = refs[:halves], refs[halves:]
    high_refs, low_refs, refs = refs[:halves], refs[halves : 2 * halves], refs[2 * halves :]
    *mixed_refs, term_ref, turned_ref, router_ref = refs
    block = pl.program_id(0)
    width = mixed_refs[0].shape[1]

    @pl.when(block == 0)
    def _():
        turned_ref[...] = jnp.concatenate([ref[...].T for ref in branch_refs], axis=1)
        high, low = (
            jnp.concatenate([ref[...] for ref in part], axis=0) for part in (high_refs, low_refs)
        )
        normed_t = normed_t_ref[...]
        router_ref[...] = dot_nn(normed_t, high) + dot_nn(normed_t, low)

    mixed = jnp.concatenate([ref[...] for ref in mixed_refs], axis=0)
    out_grad = dot_nn(turned_ref[...], mixed).astype(BF16)
    slices, depth, _ = term_ref.shape
    term_ref[:, :, :width] = out_grad.reshape(slices, depth, width)
    router = pltpu.roll(router_ref[...], (LANES - block * experts) % LANES, axis=1)
    term_ref[:, :, width:] = router.astype(BF16).reshape(slices, depth, LANES)


def branch_kernel(halves, *refs):
    mixed_refs = refs[:halves]
    first_ref, rest_ref, inputs_ref, gain_ref, middle_ref, *normed_refs = refs[halves:]
    width = first_ref.shape[-1]
    blocks = [first_ref[...].reshape(D, width)]
    blocks += [rest_ref[:, n].reshape(D, width) for n in range(rest_ref.shape[1])]
    weight = jnp.concatenate(blocks, axis=1)
    mixed = jnp.concatenate([ref[...] for ref in mixed_refs], axis=0)
    middle = inputs_ref[...].astype(F32) + dot_nt(mixed, weight)
    scale = lax.rsqrt(jnp.mean(middle * middle, axis=1, keepdims=True) + EPS)
    middle_ref[...] = middle
    normed = (middle * scale * gain_ref[...]).astype(BF16)
    for n, ref in enumerate(normed_refs):
        ref[...] = normed[n * CHUNK : (n + 1) * CHUNK]


def middle_back_kernel(
    own_ref, up_ref, down_ref, gates_ref, select_ref, router_ref, middle_ref, gain_ref, grad_ref,
    middle_grad_ref, branch_ref, high_ref, low_ref, gain_grad_ref,
):
    grad = own_ref[...].astype(F32) + up_ref[...].astype(F32) + down_ref[...].astype(F32)
    pairs = dot_nn(grad[:, D:].astype(BF16), select_ref[...])
    gates, router = gates_ref[...], router_ref[...]
    logit_grad = gates * (pairs - jnp.sum(gates * pairs, axis=1, keepdims=True))
    high = logit_grad.astype(BF16)
    low = (logit_grad - high.astype(F32)).astype(BF16)
    high_ref[...] = high
    low_ref[...] = low
    grad = grad[:, :D] + dot_nt(high, router) + dot_nt(low, router)
    back, gain_grad = norm_back(middle_ref[...], gain_ref[...], grad)
    middle_grad = grad_ref[...].astype(F32) + back
    middle_grad_ref[...] = middle_grad
    branch_ref[...] = middle_grad.astype(BF16)

    @pl.when(pl.program_id(0) == 0)
    def _():
        gain_grad_ref[...] = gain_grad

    @pl.when(pl.program_id(0) > 0)
    def _():
        gain_grad_ref[...] += gain_grad


def project_back_kernel(halves, *refs):
    dquery_refs, refs = refs[:halves], refs[halves:]
    own_refs, refs = refs[:halves], refs[halves:]
    next_refs, refs = refs[:halves], refs[halves:]
    normed_t_ref, first_ref, rest_ref, cos_ref, sin_ref, term_ref, total_ref, held_ref = refs
    block = pl.program_id(0)
    key_cos, key_sin = key_tables(cos_ref[...], sin_ref[...])
    tiles = [jnp.concatenate([ref[...] for ref in dquery_refs], axis=0)]
    for col in range(0, own_refs[0].shape[1], LANES):
        cols = slice(col, col + LANES)
        tile = jnp.concatenate(
            [own[:, cols] + after_[:, cols].astype(F32) for own, after_ in zip(own_refs, next_refs)],
            axis=0,
        )
        tiles.append(rotate_tile(tile, key_cos, key_sin, -1.0).astype(BF16))
    grads = jnp.concatenate(tiles, axis=1)
    hold_weight(first_ref, rest_ref, held_ref)
    dweight = dot_nn(normed_t_ref[...], grads).astype(BF16)
    term_ref[...] = dweight.reshape(term_ref.shape)
    part = dot_nt(grads, held_ref[...])

    @pl.when(block == 0)
    def _():
        total_ref[...] = part

    @pl.when(block > 0)
    def _():
        total_ref[...] += part


def input_back_kernel(
    inputs_ref, total_ref, gain_ref, middle_grad_ref, input_grad_ref, gain_grad_ref
):
    back, gain_grad = norm_back(inputs_ref[...].astype(F32), gain_ref[...], total_ref[...])
    input_grad_ref[...] = middle_grad_ref[...] + back

    @pl.when(pl.program_id(0) == 0)
    def _():
        gain_grad_ref[...] = gain_grad

    @pl.when(pl.program_id(0) > 0)
    def _():
        gain_grad_ref[...] += gain_grad


def joined_sum_kernel(groups, *refs):
    *part_refs, out_ref = refs
    rows = out_ref.shape[0]
    total = part_refs[0][...].astype(F32)
    for ref in part_refs[1:]:
        total = total + ref[:rows, :].astype(F32)
    queries = QUERIES_PER_GROUP * HEAD_WIDTH
    span = queries + 2 * HEAD_WIDTH
    width = total.shape[1] - groups * 2 * HEAD_WIDTH
    for group in range(groups):
        at = group * span
        out_ref[:, at : at + queries] = total[:, group * queries : (group + 1) * queries]
        col = width + group * 2 * HEAD_WIDTH
        out_ref[:, at + queries : at + span] = total[:, col : col + 2 * HEAD_WIDTH]


def norm_back(resid, gain, grad):
    scale = lax.rsqrt(jnp.mean(resid * resid, axis=1, keepdims=True) + EPS)
    gain_grad = jnp.sum(grad * resid * scale, axis=0, keepdims=True)
    scaled = grad * gain
    inner = jnp.sum(scaled * resid, axis=1, keepdims=True)
    return scale * scaled - resid * (scale * scale * scale * inner / D), gain_grad


def slots_kernel(experts, first_ref, ids_ref, rank_ref, pos_ref, ends_ref):
    length = ids_ref.shape[1]
    row = lax.broadcasted_iota(jnp.int32, (SUBLANES, length), 0)
    wanted = jnp.where(row < experts, row + first_ref[0], -1)
    rank = jnp.full((SUBLANES, length), 1 << 30, jnp.int32)
    for k in range(TOPK):
        rank = jnp.where(ids_ref[k : k + 1, :] == wanted, rank_ref[k : k + 1, :], rank)
    limit = jnp.zeros((SUBLANES, 1), jnp.int32)
    for bit in reversed(range((length * TOPK).bit_length())):
        higher = limit + (1 << bit)
        count = jnp.sum(jnp.where(rank < higher, 1.0, 0.0), axis=1, keepdims=True)
        limit = jnp.where(count <= CAP, higher, limit)
    kept = jnp.where(rank < limit, 1.0, 0.0)
    before = jnp.where(
        lax.broadcasted_iota(jnp.int32, (CHUNK, CHUNK), 0)
        < lax.broadcasted_iota(jnp.int32, (CHUNK, CHUNK), 1),
        1.0,
        0.0,
    ).astype(BF16)
    lane = lax.broadcasted_iota(jnp.int32, ends_ref.shape, 1)
    so_far = jnp.zeros((SUBLANES, 1), F32)
    ends = jnp.zeros(ends_ref.shape, F32)
    for n in range(length // CHUNK):
        part = kept[:, n * CHUNK : (n + 1) * CHUNK]
        place = dot_nn(part.astype(BF16), before) + so_far
        pos_ref[n] = jnp.where(part > 0.5, place, -1.0).astype(jnp.int32)
        so_far = so_far + jnp.sum(part, axis=1, keepdims=True)
        ends = jnp.where(lane == n + 1, so_far, ends)
    ends_ref[...] = ends.astype(jnp.int32)


def slot_windows(ends_ref, experts, chunk, window):
    firsts = [ends_ref[e, chunk] // SUBLANES * SUBLANES for e in range(experts)]
    ends = [ends_ref[e, chunk + 1] for e in range(experts)]
    count = jnp.int32(0)
    for first, end in zip(firsts, ends):
        count = jnp.maximum(count, (end - first + window - 1) // window)
    return firsts, ends, count


def window_start(first, n_window, window):
    return pl.multiple_of(jnp.minimum(first + n_window * window, SLOTS - window), SUBLANES)


def dispatch_kernel(with_gates, experts, size, *refs):
    shard_ref, ends_ref, *refs = refs
    if with_gates:
        *x_refs, pos_ref, router_ref, member_ref, out_ref, gate_ref, hot_ref, held_ref, sems = refs
    else:
        *x_refs, pos_ref, out_ref, hot_ref, held_ref, sems = refs
    window = hot_ref.shape[0] // experts
    span = 2 * size - 1
    parts = len(x_refs) // span
    part_rows = held_ref.shape[1] // parts

    def fetch(n, part, source):
        rows = pl.ds(part * part_rows, part_rows)
        return pltpu.make_async_copy(
            x_refs[part * span + source], held_ref.at[n, rows, :], sems.at[n, part]
        )

    for n in range(size):
        for part in range(parts):
            if n == 0:
                fetch(n, part, 0).start()
            else:
                below = shard_ref[0] >= n

                @pl.when(below)
                def _(n=n, part=part):
                    fetch(n, part, n).start()

                @pl.when(jnp.logical_not(below))
                def _(n=n, part=part):
                    fetch(n, part, span - n).start()

    out_ref[...] = jnp.zeros(out_ref.shape, BF16)
    if with_gates:
        gate_ref[...] = jnp.zeros(gate_ref.shape, F32)
    row = lax.broadcasted_iota(jnp.int32, (window, CHUNK), 0)
    halves = held_ref.shape[1] // CHUNK
    for n in range(size):
        for part in range(parts):
            fetch(n, part, 0).wait()
        for half in range(halves):
            chunk = shard_ref[n] * halves + half
            x = held_ref[n, half * CHUNK : (half + 1) * CHUNK, :]
            pos = pos_ref[chunk]
            firsts, ends, count = slot_windows(ends_ref, experts, chunk, window)
            if with_gates:
                logits = jnp.where(member_ref[chunk] > 0.5, dot_nn(x, router_ref[...]), MASKED)
                raised = jnp.exp(logits)
                gates = raised / jnp.sum(raised, axis=1, keepdims=True)
                lane = lax.broadcasted_iota(jnp.int32, gates.shape, 1)
                gates = jnp.where(lane < SUBLANES, gates, 0.0)
                high = gates.astype(BF16).astype(F32)
                gates = (high + pltpu.roll(gates - high, SUBLANES, axis=1)).astype(BF16)

            def body(n_window, _):
                for e in range(experts):
                    start = firsts[e] + n_window * window
                    at = window_start(firsts[e], n_window, window)
                    place = pos[e : e + 1, :]
                    place = jnp.where(place >= start, place - at, -1)
                    hot_ref[e * window : (e + 1) * window, :] = jnp.where(
                        row == place, 1.0, 0.0
                    ).astype(BF16)
                hot = hot_ref[...]
                rows = dot_nn(hot, x)
                if with_gates:
                    gate_rows = dot_nn(hot, gates)
                for e in range(experts):
                    start = firsts[e] + n_window * window
                    at = window_start(firsts[e], n_window, window)
                    part = slice(e * window, (e + 1) * window)

                    @pl.when(start < ends[e])
                    def _():
                        out_ref[e, pl.ds(at, window), :] += rows[part].astype(BF16)
                        if with_gates:
                            gate_ref[e, pl.ds(at, window), :] += gate_rows[part]

                return 0

            lax.fori_loop(0, count, body, 0)


def combine_kernel(with_pairs, sizes, order, *refs):
    piece_ref, ends_ref, place_ref, *refs = refs
    rows_refs, refs = refs[: len(sizes)], refs[len(sizes) :]
    if with_pairs:
        pair_refs, refs = refs[: len(sizes)], refs[len(sizes) :]
        *out_refs, held_ref, sems, hot_ref, total_ref, held_pair_ref, pair_total_ref = refs
    else:
        *out_refs, held_ref, sems, hot_ref, total_ref = refs
    experts = sum(sizes)
    count_out = len(out_refs)
    home = [(n, e) for n, size in enumerate(sizes) for e in range(size)]
    step, steps = pl.program_id(0), pl.num_programs(0)
    halves = steps // len(order)
    visits = steps // count_out

    def chunk_of(at_step):
        return piece_ref[at_step // halves] * halves + at_step % halves

    def copies(chunk, n_window, slot):
        firsts = slot_windows(ends_ref, experts, chunk, WINDOW)[0]
        return [
            pltpu.make_async_copy(
                rows_refs[n].at[own, pl.ds(window_start(firsts[e], n_window, WINDOW), WINDOW), :],
                held_ref.at[slot, pl.ds(e * WINDOW, WINDOW), :],
                sems.at[slot, e],
            )
            for e, (n, own) in enumerate(home)
        ]

    @pl.when(step == 0)
    def _():
        for copy in copies(chunk_of(step), 0, 0):
            copy.start()

    @pl.when(step + 1 < steps)
    def _():
        for copy in copies(chunk_of(step + 1), 0, (step + 1) % 2):
            copy.start()

    chunk = chunk_of(step)
    firsts, ends, count = slot_windows(ends_ref, experts, chunk, WINDOW)
    lane = lax.broadcasted_iota(jnp.int32, (CHUNK, WINDOW), 1)
    places = place_ref[...]

    def mark(n_window):
        for e, (n, own) in enumerate(home):
            start = firsts[e] + n_window * WINDOW
            at = window_start(firsts[e], n_window, WINDOW)
            place = places[:, e : e + 1]
            place = jnp.where(place >= start, place - at, -1)
            cols = slice(e * WINDOW, (e + 1) * WINDOW)
            hot_ref[:, cols] = jnp.where(lane == place, 1.0, 0.0).astype(BF16)
            if with_pairs:
                held_pair_ref[cols, :] = pair_refs[n][own, pl.ds(at, WINDOW), :]

    mark(0)
    for copy in copies(chunk, 0, step % 2):
        copy.wait()
    total_ref[...] = dot_nn(hot_ref[...], held_ref[step % 2])
    if with_pairs:
        pair_total_ref[...] = dot_nn(hot_ref[...], held_pair_ref[...])

    def body(n_window, _):
        more = copies(chunk, n_window, 2)
        for copy in more:
            copy.start()
        mark(n_window)
        for copy in more:
            copy.wait()
        total_ref[...] += dot_nn(hot_ref[...], held_ref[2])
        if with_pairs:
            pair_total_ref[...] += dot_nn(hot_ref[...], held_pair_ref[...])
        return 0

    lax.fori_loop(1, count, body, 0)
    for n, out_ref in enumerate(out_refs):

        @pl.when(step // visits == n)
        def _(n=n * visits // halves, out_ref=out_ref):
            out_ref[:, :D] = total_ref[...].astype(BF16)
            if with_pairs:
                place = -order[n] % len(order) * 2 * experts
                out_ref[:, D:] = pltpu.roll(pair_total_ref[...], place, axis=1).astype(BF16)


def expert_kernel(
    first, experts, half_ref, x_ref, grad_ref, gate_ref, weight_ref, y_ref, z_ref, pair_ref, *term_refs,
):
    e = first + pl.program_id(0)
    x, slot_grad = x_ref[0], grad_ref[0]
    w_in, w_out = weight_ref[0, :, : 2 * FF], weight_ref[0, :, 2 * FF :]
    lane = lax.broadcasted_iota(jnp.int32, gate_ref.shape[1:], 1)
    gate = jnp.sum(
        jnp.where((lane == e) | (lane == e + SUBLANES), gate_ref[0], 0.0), axis=1, keepdims=True
    )
    gate_up = dot_nn(x, w_in)
    gate_part, up_part = gate_up[:, :FF], gate_up[:, FF:]
    sigmoid = jax.nn.sigmoid(gate_part)
    silu = gate_part * sigmoid
    hidden = (silu * up_part).astype(BF16)
    raw = dot_nn(slot_grad, w_out)
    pair = jnp.sum(hidden.astype(F32) * raw, axis=1, keepdims=True)
    high = pair.astype(BF16).astype(F32)
    pair_ref[0] = jnp.where(
        lane == e, high, jnp.where(lane == e + experts, pair - high, 0.0)
    ).astype(BF16)
    hidden_grad = gate * raw
    gate_up_grad = jnp.concatenate(
        [
            (hidden_grad * up_part * sigmoid * (1.0 + gate_part * (1.0 - sigmoid))).astype(BF16),
            (hidden_grad * silu).astype(BF16),
        ],
        axis=1,
    )
    z_ref[0] = dot_nt(gate_up_grad, w_in).astype(BF16)
    y_ref[0] = (gate * dot_nt(hidden, w_out)).astype(BF16)
    rows_grad = (gate * slot_grad.astype(F32)).astype(BF16)
    in_term = dot_tn(x, gate_up_grad).astype(BF16)
    out_term = dot_tn(rows_grad, hidden).astype(BF16)
    if len(term_refs) == 2:
        store_halves(half_ref, *term_refs, slice(0, 2 * FF), in_term)
        store_halves(half_ref, *term_refs, slice(2 * FF, 3 * FF), out_term)
    else:
        term_ref = term_refs[0]
        slices, depth, _ = term_ref.shape
        term_ref[:, :, : 2 * FF] = in_term.reshape(slices, depth, 2 * FF)
        term_ref[:, :, 2 * FF :] = out_term.reshape(slices, depth, FF)


def after(value, *others):
    return lax.optimization_barrier((value,) + others)[0]


def pair_scatter(mine, other, size, *gates):
    taken = after(lax.ppermute(other, "gx", [(s, s ^ 1) for s in range(size)]), *gates)
    mine = (mine.astype(F32) + taken.astype(F32)).astype(mine.dtype)
    groups = [list(range(0, size, 2)), list(range(1, size, 2))]
    total = lax.psum_scatter(mine, "gx", scatter_dimension=0, tiled=True, axis_index_groups=groups)
    return lax.optimization_barrier(total)[0]


def direct_gather(part, size):
    return jnp.stack(
        [
            lax.ppermute(part, "gy", [(s, (s + k) % size) for s in range(size)])
            for k in range(1, size)
        ]
    )


def gather_step(pair, step, size, *gates):
    up, down = (after(part, *gates) if gates else part for part in pair)
    return (
        lax.ppermute(up, "gy", [(s, s + 1) for s in range(step, size - 1)]),
        lax.ppermute(down, "gy", [(s + 1, s) for s in range(0, size - 1 - step)]),
    )


def sum_step(parts, pair, step, size, *gates):
    above, below = parts[step], parts[size - step]
    if gates:
        pair = tuple(after(part, *gates) for part in pair)
    if pair is not None:
        above, below = (
            (a.astype(F32) + b.astype(F32)).astype(a.dtype)
            for a, b in zip((above, below), pair)
        )
    return (
        lax.ppermute(above, "gy", [(s, s + 1) for s in range(step)]),
        lax.ppermute(below, "gy", [(size - 1 - s, size - 2 - s) for s in range(step)]),
    )


def sum_steps_of(parts, size, gates):
    steps, pair = [], None
    for step in range(1, size):
        pair = sum_step(parts, pair, step, size, *gates.get(step, ()))
        steps.append(pair)
    return steps


def direct_sum(parts, size):
    total = parts[0].astype(F32)
    for k in range(1, size):
        total = total + lax.ppermute(
            parts[k], "gy", [(s, (s - k) % size) for s in range(size)]
        ).astype(F32)
    return total


def summed(parts, steps):
    return parts[0].astype(F32) + steps[-1][0].astype(F32) + steps[-1][1].astype(F32)


def shards(
    nx,
    ny,
    tokens,
    attn_gain,
    query_key_value_weight,
    out_weight,
    moe_gain,
    router_weight,
    expert_in,
    expert_out,
    expert_ids,
    route_order,
    segment_ids,
    out_grad,
):
    rows = tokens.shape[0]
    length = segment_ids.shape[1]
    depth = out_weight.shape[1]
    heads_width = out_weight.shape[0]
    groups = heads_width // (HEAD_WIDTH * QUERIES_PER_GROUP)
    spare = -heads_width % LANES
    width = heads_width + spare
    kv_width = groups * 2 * HEAD_WIDTH
    joined = width + kv_width
    experts = router_weight.shape[0]
    all_experts = experts * ny
    chunks = length // CHUNK
    own_chunks = rows // CHUNK
    me = lax.axis_index("gy")
    first_expert = me * experts
    first_row = me * rows
    both = ("gx", "gy")

    pos, ends = pl.pallas_call(
        functools.partial(slots_kernel, experts),
        in_specs=[
            pl.BlockSpec(memory_space=pltpu.SMEM),
            pl.BlockSpec(memory_space=pltpu.VMEM),
            pl.BlockSpec(memory_space=pltpu.VMEM),
        ],
        out_shape=[
            jax.ShapeDtypeStruct((chunks, SUBLANES, CHUNK), jnp.int32),
            jax.ShapeDtypeStruct((SUBLANES, LANES), jnp.int32),
        ],
        compiler_params=params(),
        cost_estimate=cost(3),
        name="slots",
    )(
        first_expert.reshape(1),
        expert_ids.T,
        route_order[0].reshape(length, TOPK).T,
    )
    places = jnp.pad(
        pos.transpose(0, 2, 1).reshape(length, SUBLANES), ((0, 0), (0, LANES - SUBLANES))
    )
    ends = ends[:, : chunks + 1]
    pieces = (me - jnp.arange(ny, dtype=jnp.int32)) % ny
    lane_expert = jnp.arange(LANES, dtype=jnp.int32)
    turned_expert = (me - lane_expert // experts) % ny * experts + lane_expert % experts
    turned_expert = jnp.where(lane_expert < all_experts, turned_expert, -1)
    members = jnp.any(expert_ids[:, :, None] == turned_expert[None, None, :], axis=1)
    members = members.astype(F32).reshape(chunks, CHUNK, LANES)
    own_ids = lax.dynamic_slice_in_dim(expert_ids, first_row, rows, 0)
    own_members = jnp.any(own_ids[:, :, None] == turned_expert[None, None, :], axis=1).astype(F32)

    inputs = tokens.astype(F32)
    scale_one = lax.rsqrt(jnp.mean(inputs * inputs, axis=1, keepdims=True) + EPS)
    normed_one = (inputs * scale_one * attn_gain[None, :]).astype(BF16)
    normed_one_t = normed_one.T
    cosine, sine = rope_tiles(first_row, rows)
    labels = jnp.concatenate([jnp.full((SEGMAX,), -1, jnp.int32), segment_ids[0]])
    labels = lax.dynamic_slice_in_dim(labels, first_row, rows + SEGMAX, 0)
    position = jnp.arange(rows + SEGMAX, dtype=jnp.int32)
    bias = jnp.stack(
        [
            jnp.where(
                (labels[s : s + 2 * SEGMAX, None] == labels[None, s + SEGMAX : s + 2 * SEGMAX])
                & (
                    position[s : s + 2 * SEGMAX, None]
                    <= position[None, s + SEGMAX : s + 2 * SEGMAX]
                ),
                0.0,
                MASKED,
            ).astype(F32)
            for s in range(0, rows, SEGMAX)
        ]
    )
    grouped = query_key_value_weight.reshape(depth, groups, QUERIES_PER_GROUP + 2, HEAD_WIDTH)
    own_joined = jnp.concatenate(
        [
            jnp.pad(
                grouped[:, :, :QUERIES_PER_GROUP].reshape(depth, heads_width), ((0, 0), (0, spare))
            ),
            grouped[:, :, QUERIES_PER_GROUP:].reshape(depth, kv_width),
        ],
        axis=1,
    )
    own_out = jnp.pad(out_weight.T, ((0, 0), (0, spare)))
    own_router = jnp.pad(router_weight.T, ((0, 0), (0, LANES - experts)))
    gap = -(joined + LANES) % width
    own_weights = jnp.concatenate(
        [own_joined, own_router, jnp.zeros((depth, gap), BF16), own_out], axis=1
    )
    own_second = jnp.concatenate([own_out, own_router], axis=1)
    cut = experts * 2 // 5
    bounds = ((0, cut), (cut, experts))
    own_experts = [
        jnp.concatenate([expert_in[lo:hi], expert_out[lo:hi]], axis=2) for lo, hi in bounds
    ]
    first_weights = lax.all_gather(own_weights, "gx", axis=0)
    line_joined = after(direct_gather(own_joined, ny), *own_experts)
    own_second = after(own_second, line_joined)
    line_second = direct_gather(own_second, ny)
    ready = after(out_grad, line_second, bias, cosine, sine, normed_one)
    grad_steps = [gather_step((ready, ready), 0, ny)]
    rest_joined = lax.all_gather(line_joined, "gx", axis=0)
    rest_second = lax.all_gather(line_second, "gx", axis=0)
    wide = []
    for own in own_experts:
        wide.append(lax.all_gather(own, "gx", axis=1, tiled=True))


    out_column = (joined + LANES + gap) // width
    rest_block = lambda b: (0, jnp.maximum(b - 1, 0), 0, 0)
    joined_specs = [
        pl.BlockSpec((nx, depth, joined), lambda b: (0, 0, 0)),
        pl.BlockSpec((nx, pl.Squeezed(), depth, joined), rest_block),
    ]
    out_specs = [
        pl.BlockSpec((nx, depth, width), lambda b: (0, 0, out_column)),
        pl.BlockSpec((nx, pl.Squeezed(), depth, width), rest_block),
    ]
    held_joined = pltpu.VMEM((D, joined), BF16)
    held_out = pltpu.VMEM((D, width), BF16)
    query, kv = pl.pallas_call(
        project_kernel,
        grid=(ny,),
        in_specs=[
            whole((rows, D)),
            *joined_specs,
            whole((rows, LANES)),
            whole((rows, LANES)),
        ],
        out_specs=[
            pl.BlockSpec((rows, width), lambda b: (0, b)),
            pl.BlockSpec((rows, kv_width), lambda b: (0, b)),
        ],
        out_shape=[
            jax.ShapeDtypeStruct((rows, ny * width), BF16),
            jax.ShapeDtypeStruct((rows, ny * kv_width), BF16),
        ],
        scratch_shapes=[held_joined],
        compiler_params=params(),
        cost_estimate=cost(10),
        name="project",
    )(after(normed_one, bias), first_weights, rest_joined, cosine, sine)
    halo = lax.ppermute(kv[rows - SEGMAX :], "gy", [(s, s + 1) for s in range(ny - 1)])
    halves = rows // SEGMAX
    half_rows = lambda n, w: pl.BlockSpec((SEGMAX, w), lambda b: (n, b))
    whole_half = lambda n, w: pl.BlockSpec((SEGMAX, w), lambda b: (n, 0))
    below_rows = pl.BlockSpec((SEGMAX, kv_width), lambda b: (0, (b + ny - 1) % ny))
    bias_half = lambda n: pl.BlockSpec((pl.Squeezed(), 2 * SEGMAX, SEGMAX), lambda b: (n, 0, 0))

    def window(n):
        if n == 0:
            return [half_rows(0, kv_width), below_rows], (kv, halo)
        return [half_rows(n, kv_width), half_rows(n - 1, kv_width)], (kv, kv)

    mixed = [None] * halves
    for n in reversed(range(halves)):
        specs, arrays = window(n)
        mixed[n] = pl.pallas_call(
            attend_kernel,
            grid=(ny,),
            in_specs=[half_rows(n, width), *specs, bias_half(n)],
            out_specs=half_rows(0, width),
            out_shape=jax.ShapeDtypeStruct((SEGMAX, ny * width), BF16),
            compiler_params=params(),
            cost_estimate=cost(8),
            name="attend",
        )(query, *arrays, bias)
    for step in range(1, ny - 2):
        grad_steps.append(gather_step(grad_steps[-1], step, ny, mixed[-1]))
    middle, *normed_chunks = pl.pallas_call(
        functools.partial(branch_kernel, halves),
        grid=(1,),
        in_specs=[whole((SEGMAX, ny * width))] * halves
        + [
            out_specs[0],
            pl.BlockSpec((nx, ny - 1, depth, width), lambda _: (0, 0, 0, 0)),
            whole((rows, D)),
            whole((1, D)),
        ],
        out_specs=[whole((rows, D))] + [whole((CHUNK, D))] * own_chunks,
        out_shape=[jax.ShapeDtypeStruct((rows, D), F32)]
        + [jax.ShapeDtypeStruct((CHUNK, D), BF16)] * own_chunks,
        compiler_params=params(),
        cost_estimate=cost(7),
        name="branch",
    )(*mixed, first_weights, rest_second, tokens, moe_gain[None, :])

    router = jnp.concatenate(
        [
            first_weights[:, None, :, joined : joined + experts],
            rest_second[:, :, :, width : width + experts],
        ],
        axis=1,
    )
    router = router.transpose(0, 2, 1, 3).reshape(D, all_experts)
    router = jnp.pad(router, ((0, 0), (0, LANES - all_experts)))
    normed_two = jnp.concatenate(normed_chunks, axis=0)
    normed_steps = []
    for part in normed_chunks:
        part = after(part, grad_steps[-1])
        normed_steps.append([(part, part)])
    for step in range(ny - 1):
        for steps in normed_steps:
            steps.append(gather_step(steps[-1], step, ny))
    grad_steps.append(
        gather_step(grad_steps[-1], ny - 2, ny, *[steps[-1] for steps in normed_steps])
    )
    normed_pieces = []
    for part, steps in zip(normed_chunks, normed_steps):
        normed_pieces += [part] + [up for up, _ in steps[1:]] + [down for _, down in steps[1:]]
    grad_pieces = [out_grad] + [up for up, _ in grad_steps] + [down for _, down in grad_steps]
    smem = pl.BlockSpec(memory_space=pltpu.SMEM)
    vmem = pl.BlockSpec(memory_space=pltpu.VMEM)
    slot_rows = jax.ShapeDtypeStruct((experts, SLOTS, D), BF16)
    slot_lanes = lambda kind: jax.ShapeDtypeStruct((experts, SLOTS, LANES), kind)
    dispatch_scratch = lambda parts: [
        pltpu.VMEM((experts * SHORT_WINDOW, CHUNK), BF16),
        pltpu.VMEM((ny, rows, D), BF16),
        pltpu.SemaphoreType.DMA((ny, parts)),
    ]
    hbm = pl.BlockSpec(memory_space=pl.ANY)
    slot_grads = pl.pallas_call(
        functools.partial(dispatch_kernel, False, experts, ny),
        in_specs=[smem, smem] + [hbm] * (2 * ny - 1) + [vmem],
        out_specs=vmem,
        out_shape=slot_rows,
        scratch_shapes=dispatch_scratch(1),
        compiler_params=params(),
        cost_estimate=cost(26),
        name="dispatch_grads",
    )(pieces, ends, *grad_pieces, pos)
    dispatched, slot_gates = pl.pallas_call(
        functools.partial(dispatch_kernel, True, experts, ny),
        in_specs=[smem, smem] + [hbm] * len(normed_pieces) + [vmem] * 3,
        out_specs=[vmem, vmem],
        out_shape=[slot_rows, slot_lanes(F32)],
        scratch_shapes=dispatch_scratch(own_chunks),
        compiler_params=params(),
        cost_estimate=cost(31),
        name="dispatch_rows",
    )(pieces, ends, *normed_pieces, pos, router, members)

    half = (lax.axis_index("gx") % 2).reshape(1)
    y_rows, z_rows, slot_pairs, weight_terms = [], [], [], []
    for n, (lo, hi) in enumerate(bounds):
        outer = lambda *shape: pl.BlockSpec((1,) + shape, lambda e, lo=lo: (lo + e, 0, 0))
        inner = lambda *shape: pl.BlockSpec((1,) + shape, lambda e: (e, 0, 0))
        parts = n + 1
        slices = pl.BlockSpec((nx // parts, pl.Squeezed(), depth, 3 * FF), lambda e: (0, e, 0, 0))
        y, z, pair, *terms = pl.pallas_call(
            functools.partial(expert_kernel, lo, experts),
            grid=(hi - lo,),
            in_specs=[
                smem,
                outer(SLOTS, D),
                outer(SLOTS, D),
                outer(SLOTS, LANES),
                inner(D, 3 * FF),
            ],
            out_specs=[inner(SLOTS, D), inner(SLOTS, D), inner(SLOTS, LANES)]
            + [slices] * parts,
            out_shape=[
                jax.ShapeDtypeStruct((hi - lo, SLOTS, D), BF16),
                jax.ShapeDtypeStruct((hi - lo, SLOTS, D), BF16),
                jax.ShapeDtypeStruct((hi - lo, SLOTS, LANES), BF16),
            ]
            + [jax.ShapeDtypeStruct((nx // parts, hi - lo, depth, 3 * FF), BF16)] * parts,
            compiler_params=params(),
            cost_estimate=cost(9 * (hi - lo)),
            name="experts",
        )(half, dispatched, slot_grads, slot_gates, wide[n])
        y_rows.append(y)
        z_rows.append(z)
        slot_pairs.append(pair)
        weight_terms.append(terms)
    def combine(rows_in, which, pairs=None):
        held = pltpu.VMEM((3, experts * WINDOW, D), BF16)
        sems = pltpu.SemaphoreType.DMA((3, experts))
        hot_t = pltpu.VMEM((CHUNK, experts * WINDOW), BF16)
        total = pltpu.VMEM((CHUNK, D), F32)
        more = pairs is not None
        columns = D + LANES * more
        halves = chunks // ny
        here = pieces[jnp.array(which)]

        def place_map(c, piece_ref):
            return (piece_ref[c // halves] * halves + c % halves, 0)

        visits = 1 if more else halves

        def out_map(n):
            return lambda c, piece_ref: (jnp.clip(c - n * visits, 0, visits - 1), 0)

        return pl.pallas_call(
            functools.partial(combine_kernel, more, tuple(hi - lo for lo, hi in bounds), which),
            grid_spec=pltpu.PrefetchScalarGridSpec(
                num_scalar_prefetch=1,
                grid=(halves * len(which),),
                in_specs=[smem, pl.BlockSpec((CHUNK, LANES), place_map)]
                + [hbm] * len(bounds)
                + [once((hi - lo, SLOTS, LANES)) for lo, hi in bounds] * more,
                out_specs=[
                    pl.BlockSpec((CHUNK, columns), out_map(n))
                    for n in range(len(which) * halves // visits)
                ],
                scratch_shapes=[held, sems, hot_t, total]
                + [
                    pltpu.VMEM((experts * WINDOW, LANES), BF16),
                    pltpu.VMEM((CHUNK, LANES), F32),
                ]
                * more,
            ),
            out_shape=[jax.ShapeDtypeStruct((CHUNK * visits, columns), BF16)]
            * (len(which) * halves // visits),
            compiler_params=params(),
            cost_estimate=cost(16),
            name="combine_grads" if more else "combine_rows",
        )(here, ends, places, *rows_in, *(pairs if more else []))

    outer_pieces = sorted({1, ny - 1})
    inner_pieces = [k for k in range(ny) if k not in outer_pieces]
    order = outer_pieces + inner_pieces
    token_sum = combine(z_rows, order, slot_pairs)
    token_sum = [
        [token_sum[order.index(k) * own_chunks + n] for k in range(ny)] for n in range(own_chunks)
    ]
    token_steps = [[] for _ in token_sum]
    for step in range(1, ny):
        for parts, steps in zip(token_sum, token_steps):
            steps.append(sum_step(parts, steps[-1] if steps else None, step, ny))
    own_logits = jnp.where(own_members > 0.5, dot_nn(normed_two, router), MASKED)
    own_raised = jnp.exp(own_logits)
    own_gates = own_raised / jnp.sum(own_raised, axis=1, keepdims=True)
    source = lane_expert // (2 * experts) * experts + lane_expert % experts
    source = jnp.where(lane_expert < 2 * all_experts, source, -1)
    select = (source[:, None] == lane_expert[None, :]).astype(BF16)
    weight_sums = [
        lax.psum_scatter(weight_terms[0][0], "gx", scatter_dimension=0, tiled=True)[0],
        pair_scatter(*weight_terms[1], nx, token_sum[0][0]),
    ]
    combined = combine([after(y, [steps[-2] for steps in token_steps]) for y in y_rows], order)
    combined = [combined[order.index(k)] for k in range(ny)]
    row_block = lambda w: pl.BlockSpec((LANES, w), lambda r: (r, 0))
    later_block = lambda n, w: pl.BlockSpec((LANES, w), lambda r: (r + n * CHUNK // LANES, 0))
    backs = []
    for n, (parts, steps) in enumerate(zip(token_sum, token_steps)):
        backs.append(
            pl.pallas_call(
                middle_back_kernel,
                grid=(CHUNK // LANES,),
                in_specs=[row_block(D + LANES)] * 3
                + [later_block(n, LANES), whole((LANES, LANES)), whole((D, LANES))]
                + [later_block(n, D), whole((1, D)), later_block(n, D)],
                out_specs=[row_block(D), row_block(D), row_block(LANES), row_block(LANES)]
                + [whole((1, D))],
                out_shape=[
                    jax.ShapeDtypeStruct((CHUNK, D), F32),
                    jax.ShapeDtypeStruct((CHUNK, D), BF16),
                    jax.ShapeDtypeStruct((CHUNK, LANES), BF16),
                    jax.ShapeDtypeStruct((CHUNK, LANES), BF16),
                    jax.ShapeDtypeStruct((1, D), F32),
                ],
                compiler_params=params(),
                cost_estimate=cost(4),
                name="middle_back",
            )(after(parts[0], *combined), *steps[-1], own_gates, select, router, middle,
              moe_gain[None, :], out_grad)
        )
    middle_grads, branch_grads, highs, lows, moe_gain_grads = zip(*backs)
    moe_gain_grad = sum(moe_gain_grads)

    combined_steps = [sum_step(combined, None, 1, ny)]

    dquery, dkv, dbefore = [], [], []
    for n in range(halves):
        specs, arrays = window(n)
        outs = pl.pallas_call(
            attend_back_kernel,
            grid=(ny,),
            in_specs=[
                half_rows(n, width),
                *specs,
                bias_half(n),
                *out_specs,
                whole((SEGMAX, D)),
                whole_half(n, LANES),
                whole_half(n, LANES),
            ],
            out_specs=[half_rows(0, width), half_rows(0, kv_width), half_rows(0, kv_width)],
            out_shape=[
                jax.ShapeDtypeStruct((SEGMAX, ny * width), BF16),
                jax.ShapeDtypeStruct((SEGMAX, ny * kv_width), F32),
                jax.ShapeDtypeStruct((SEGMAX, ny * kv_width), F32 if n else BF16),
            ],
            scratch_shapes=[pltpu.VMEM((SEGMAX, width), F32), held_out],
            compiler_params=params(),
            cost_estimate=cost(17),
            name="attend_back",
        )(query, *arrays, bias, first_weights, rest_second, after(branch_grads[n], *combined, *dbefore),
          cosine, sine)
        for kept, out in zip((dquery, dkv, dbefore), outs):
            kept.append(out)
    halo_grad = lax.ppermute(dbefore[0], "gy", [(s + 1, s) for s in range(ny - 1)])
    second_term = pl.pallas_call(
        functools.partial(branch_weights_kernel, experts, halves),
        grid=(ny,),
        in_specs=[whole((D, rows))]
        + [whole((CHUNK, D))] * halves
        + [whole((CHUNK, LANES))] * (2 * halves)
        + [half_rows(0, width)] * halves,
        out_specs=pl.BlockSpec((nx, pl.Squeezed(), depth, width + LANES), lambda b: (0, b, 0, 0)),
        out_shape=jax.ShapeDtypeStruct((nx, ny, depth, width + LANES), BF16),
        scratch_shapes=[pltpu.VMEM((D, rows), BF16), pltpu.VMEM((D, LANES), F32)],
        compiler_params=params(),
        cost_estimate=cost(9),
        name="branch_weights",
    )(normed_two.T, *branch_grads, *highs, *lows, *mixed)
    combined_steps.append(sum_step(combined, combined_steps[-1], 2, ny, halo_grad))
    next_rows = pl.BlockSpec((SEGMAX, kv_width), lambda b: (0, (b + 1) % ny))
    joined_term, normed_one_grad = pl.pallas_call(
        functools.partial(project_back_kernel, halves),
        grid=(ny,),
        in_specs=[half_rows(0, width)] * halves
        + [half_rows(0, kv_width)] * (2 * halves - 1)
        + [
            next_rows,
            whole((D, rows)),
            *joined_specs,
            whole((rows, LANES)),
            whole((rows, LANES)),
        ],
        out_specs=[
            pl.BlockSpec((nx, pl.Squeezed(), depth, joined), lambda b: (0, b, 0, 0)),
            whole((rows, D)),
        ],
        out_shape=[
            jax.ShapeDtypeStruct((nx, ny, depth, joined), BF16),
            jax.ShapeDtypeStruct((rows, D), F32),
        ],
        scratch_shapes=[held_joined],
        compiler_params=params(),
        cost_estimate=cost(22),
        name="project_back",
    )(*dquery, *dkv, *dbefore[1:], halo_grad, normed_one_t, first_weights, rest_joined, cosine, sine)
    in_grad, down_grad = [], []
    for part in after(tuple(weight_sums), joined_term):
        in_grad.append(part[..., : 2 * FF].astype(F32))
        down_grad.append(part[..., 2 * FF :].astype(F32))
    in_grad, down_grad = jnp.concatenate(in_grad), jnp.concatenate(down_grad)
    input_grad, attn_gain_grad = pl.pallas_call(
        input_back_kernel,
        grid=(rows // LANES,),
        in_specs=[row_block(D), row_block(D), whole((1, D)), row_block(D)],
        out_specs=[row_block(D), whole((1, D))],
        out_shape=[
            jax.ShapeDtypeStruct((rows, D), F32),
            jax.ShapeDtypeStruct((1, D), F32),
        ],
        compiler_params=params(),
        cost_estimate=cost(6),
        name="input_back",
    )(tokens, normed_one_grad, attn_gain[None, :], after(jnp.concatenate(middle_grads), in_grad, down_grad))

    second_sum = lax.psum_scatter(
        after(second_term, weight_sums[0]), "gx", scatter_dimension=0, tiled=True
    )
    second_sum = lax.optimization_barrier(second_sum)[0]
    joined_sum = lax.psum_scatter(
        after(joined_term, second_sum, combined_steps[1], *weight_sums), "gx", scatter_dimension=0, tiled=True
    )
    joined_sum = lax.optimization_barrier(joined_sum)[0]
    gain_sums = jnp.concatenate([attn_gain_grad, moe_gain_grad])
    bit = 1
    while bit < nx:
        pairs = [(s, s ^ bit) for s in range(nx)]
        gain_sums = gain_sums + lax.ppermute(gain_sums, "gx", pairs)
        bit = 2 * bit
    high = gain_sums.astype(BF16)
    low = (gain_sums - high.astype(F32)).astype(BF16)
    gains = jnp.stack([high, low]).reshape(-1)
    gain_rows = -(-gains.shape[0] // joined)
    gain_rows += -gain_rows % SUBLANES
    gains = jnp.pad(gains, (0, gain_rows * joined - gains.shape[0])).reshape(gain_rows, joined)
    second_sum = direct_sum(second_sum, ny)
    out_weight_grad = second_sum[:, :heads_width].T
    router_grad = second_sum[:, width : width + experts].T
    for step in range(3, ny):
        gates = (gains, out_weight_grad, router_grad) if step == 3 else ()
        combined_steps.append(sum_step(combined, combined_steps[-1], step, ny, *gates))
    layer_out = (middle + summed(combined, combined_steps)).astype(BF16)
    joined_parts, gain_parts = [joined_sum[0]], [gains]
    for k in range(1, ny):
        part = jnp.concatenate([joined_sum[k], gains], axis=0)
        part = lax.ppermute(part, "gy", [(s, (s - k) % ny) for s in range(ny)])
        joined_parts.append(part)
        gain_parts.append(part[depth:])
    qkv_grad = pl.pallas_call(
        functools.partial(joined_sum_kernel, groups),
        out_shape=jax.ShapeDtypeStruct(query_key_value_weight.shape, F32),
        compiler_params=params(),
        cost_estimate=cost(2),
        name="joined_sum",
    )(*joined_parts)
    gain_sums = jnp.roll(jnp.stack(gain_parts), me, axis=0).astype(F32)
    gain_sums = gain_sums.reshape(ny, -1)[:, : 4 * D].reshape(ny, 2, 2, D)
    gain_sums = jnp.sum(gain_sums, axis=(0, 1))
    return (
        layer_out,
        input_grad,
        gain_sums[0],
        qkv_grad,
        out_weight_grad,
        gain_sums[1],
        router_grad,
        in_grad,
        down_grad,
    )


def solution(mesh):
    in_specs = (
        P(("gx", "gy"), None),
        P(),
        P("gx", "gy"),
        P("gy", "gx"),
        P(),
        P("gy", "gx"),
        P("gy", "gx", None),
        P("gy", "gx", None),
        P("gx", None),
        P("gx", None),
        P("gx", None),
        P(("gx", "gy"), None),
    )
    out_specs = (
        P(("gx", "gy"), None),
        P(("gx", "gy"), None),
        P(),
        P("gx", "gy"),
        P("gy", "gx"),
        P(),
        P("gy", "gx"),
        P("gy", "gx", None),
        P("gy", "gx", None),
    )
    body = functools.partial(shards, mesh.shape["gx"], mesh.shape["gy"])
    return jax.shard_map(body, mesh=mesh, in_specs=in_specs, out_specs=out_specs, check_vma=False)
```

```python
import functools

import jax
import jax.numpy as jnp
from jax import lax
from jax.experimental import pallas as pl
from jax.experimental.pallas import tpu as pltpu
from jax.sharding import PartitionSpec as P

D = 1536
HEAD_WIDTH = 64
FF = 512
TOPK = 8
SEGMAX = 256
QUERIES_PER_GROUP = 3
CAP = 460
SLOTS = 464
WINDOW = 128
SHORT_WINDOW = 96
CHUNK = 256
LANES = 128
SUBLANES = 16

EPS = 1e-05
MASKED = -1e30
SCORE_SCALE = HEAD_WIDTH ** (-0.5)
VMEM_BYTES = 60 * 1024 * 1024
F32 = jnp.float32
BF16 = jnp.bfloat16


def dot_nn(a, b):
    return lax.dot_general(a, b, (((1,), (0,)), ((), ())), preferred_element_type=F32)


def dot_nt(a, b):
    return lax.dot_general(a, b, (((1,), (1,)), ((), ())), preferred_element_type=F32)


def dot_tn(a, b):
    return lax.dot_general(a, b, (((0,), (0,)), ((), ())), preferred_element_type=F32)


def params(**more):
    return pltpu.CompilerParams(vmem_limit_bytes=VMEM_BYTES, **more)


def cost(micros):
    return pl.CostEstimate(
        flops=int(micros * 1.1e9), bytes_accessed=int(micros * 3.6e6), transcendentals=0
    )


def store_halves(half_ref, mine_ref, other_ref, columns, value):
    slices, depth, _ = mine_ref.shape
    for parity in range(2):
        own = half_ref[0] == parity
        for ref, taken in ((mine_ref, own), (other_ref, jnp.logical_not(own))):

            @pl.when(taken)
            def _(ref=ref, parity=parity):
                for n in range(slices):
                    at = (2 * n + parity) * depth
                    ref[n, :, columns] = value[at : at + depth]


def whole(shape):
    return pl.BlockSpec(shape, lambda *_: (0,) * len(shape))


def once(shape):
    return pl.BlockSpec(shape, lambda *_: (0,) * len(shape), pipeline_mode=pl.Buffered(1))


def rope_tiles(first_row, rows):
    half = HEAD_WIDTH // 2
    freq = jnp.exp(jnp.arange(half, dtype=F32) * (-2.0 * jnp.log(10000.0) / HEAD_WIDTH))
    position = (first_row + jnp.arange(rows, dtype=jnp.int32)).astype(F32)
    angle = position[:, None] * freq[None, :]
    cosine, sine = jnp.cos(angle), jnp.sin(angle)
    return (
        jnp.concatenate([cosine] * 4, axis=1),
        jnp.concatenate([-sine, sine, -sine, sine], axis=1),
    )


def swap_halves(tile):
    lane = lax.broadcasted_iota(jnp.int32, tile.shape, 1)
    half = HEAD_WIDTH // 2
    return jnp.where(
        lane % HEAD_WIDTH < half,
        pltpu.roll(tile, LANES - half, axis=1),
        pltpu.roll(tile, half, axis=1),
    )


def rotate_tile(tile, cosine, sine, sign):
    return tile * cosine + sign * swap_halves(tile) * sine


def key_tables(cosine, sine):
    lane = lax.broadcasted_iota(jnp.int32, cosine.shape, 1)
    is_key = lane < HEAD_WIDTH
    return jnp.where(is_key, cosine, 1.0), jnp.where(is_key, sine, 0.0)


def hold_weight(first_ref, rest_ref, held_ref):
    @pl.when(pl.program_id(0) == 0)
    def _():
        held_ref[...] = first_ref[...].reshape(held_ref.shape)

    @pl.when(pl.program_id(0) > 0)
    def _():
        held_ref[...] = rest_ref[...].reshape(held_ref.shape)


def project_kernel(
    normed_ref, first_ref, rest_ref, cos_ref, sin_ref, query_ref, kv_ref, held_ref
):
    hold_weight(first_ref, rest_ref, held_ref)
    project = dot_nn(normed_ref[...], held_ref[...])
    cosine, sine = cos_ref[...], sin_ref[...]
    key_cos, key_sin = key_tables(cosine, sine)
    for col in range(0, query_ref.shape[1], LANES):
        tile = rotate_tile(project[:, col : col + LANES], cosine, sine, 1.0)
        query_ref[:, col : col + LANES] = tile.astype(BF16)
    for col in range(0, kv_ref.shape[1], LANES):
        at = query_ref.shape[1] + col
        tile = rotate_tile(project[:, at : at + LANES], key_cos, key_sin, 1.0)
        kv_ref[:, col : col + LANES] = tile.astype(BF16)


def group_windows(before, own, group):
    col = group * 2 * HEAD_WIDTH
    return [
        jnp.concatenate([before[:, at : at + HEAD_WIDTH], own[:, at : at + HEAD_WIDTH]], axis=0)
        for at in (col, col + HEAD_WIDTH)
    ]


def stack_heads(block, group):
    at = group * QUERIES_PER_GROUP * HEAD_WIDTH
    return jnp.concatenate(
        [
            block[:, at + i * HEAD_WIDTH : at + (i + 1) * HEAD_WIDTH]
            for i in range(QUERIES_PER_GROUP)
        ],
        axis=0,
    )


def store_heads(ref, group, value_t):
    at = group * QUERIES_PER_GROUP * HEAD_WIDTH
    for i in range(QUERIES_PER_GROUP):
        part = value_t[:, i * SEGMAX : (i + 1) * SEGMAX].T
        ref[:, at + i * HEAD_WIDTH : at + (i + 1) * HEAD_WIDTH] = part.astype(ref.dtype)


def clear_spare(ref, groups):
    used = groups * QUERIES_PER_GROUP * HEAD_WIDTH
    if used < ref.shape[1]:
        ref[:, used:] = jnp.zeros((ref.shape[0], ref.shape[1] - used), ref.dtype)


def probs_of(keys, queries, bias):
    scores = dot_nt(keys, queries) * SCORE_SCALE
    scores = scores + jnp.concatenate([bias] * QUERIES_PER_GROUP, axis=1)
    top = jnp.max(scores, axis=0, keepdims=True)
    weights = jnp.exp(scores - top)
    total = jnp.sum(weights, axis=0, keepdims=True)
    return weights * (1.0 / total)


def attend_kernel(query_ref, own_ref, before_ref, bias_ref, mixed_ref):
    groups = own_ref.shape[1] // (2 * HEAD_WIDTH)
    query, own, before, bias = query_ref[...], own_ref[...], before_ref[...], bias_ref[...]
    clear_spare(mixed_ref, groups)
    for group in range(groups):
        keys, values = group_windows(before, own, group)
        probs = probs_of(keys, stack_heads(query, group), bias).astype(BF16)
        store_heads(mixed_ref, group, dot_nn(values.T, probs))


def attend_back_kernel(
    query_ref, own_ref, before_ref, bias_ref, first_ref, rest_ref, branch_ref, cos_ref, sin_ref,
    dquery_ref, down_ref, dbefore_ref, raw_ref, held_ref,
):
    groups = own_ref.shape[1] // (2 * HEAD_WIDTH)
    hold_weight(first_ref, rest_ref, held_ref)
    mixed_grad = dot_nn(branch_ref[...], held_ref[...]).astype(BF16)
    query, own, before, bias = query_ref[...], own_ref[...], before_ref[...], bias_ref[...]
    clear_spare(raw_ref, groups)
    for group in range(groups):
        keys, values = group_windows(before, own, group)
        queries, grads = stack_heads(query, group), stack_heads(mixed_grad, group)
        probs = probs_of(keys, queries, bias)
        prob_grad = dot_nt(values, grads)
        inner = jnp.sum(probs * prob_grad, axis=0, keepdims=True)
        score_grad = (SCORE_SCALE * probs * (prob_grad - inner)).astype(BF16)
        store_heads(raw_ref, group, dot_nn(keys.T, score_grad))
        col = group * 2 * HEAD_WIDTH
        for at, part in (
            (col, dot_nn(score_grad, queries)),
            (col + HEAD_WIDTH, dot_nn(probs.astype(BF16), grads)),
        ):
            dbefore_ref[:, at : at + HEAD_WIDTH] = part[:SEGMAX].astype(dbefore_ref.dtype)
            down_ref[:, at : at + HEAD_WIDTH] = part[SEGMAX:]
    cosine, sine = cos_ref[...], sin_ref[...]
    for col in range(0, query_ref.shape[1], LANES):
        tile = rotate_tile(raw_ref[:, col : col + LANES], cosine, sine, -1.0)
        dquery_ref[:, col : col + LANES] = tile.astype(BF16)


def branch_weights_kernel(experts, halves, normed_t_ref, *refs):
    branch_refs, refs = refs[:halves], refs[halves:]
    high_refs, low_refs, refs = refs[:halves], refs[halves : 2 * halves], refs[2 * halves :]
    *mixed_refs, term_ref, turned_ref, router_ref = refs
    block = pl.program_id(0)
    width = mixed_refs[0].shape[1]

    @pl.when(block == 0)
    def _():
        turned_ref[...] = jnp.concatenate([ref[...].T for ref in branch_refs], axis=1)
        high, low = (
            jnp.concatenate([ref[...] for ref in part], axis=0) for part in (high_refs, low_refs)
        )
        normed_t = normed_t_ref[...]
        router_ref[...] = dot_nn(normed_t, high) + dot_nn(normed_t, low)

    mixed = jnp.concatenate([ref[...] for ref in mixed_refs], axis=0)
    out_grad = dot_nn(turned_ref[...], mixed).astype(BF16)
    slices, depth, _ = term_ref.shape
    term_ref[:, :, :width] = out_grad.reshape(slices, depth, width)
    router = pltpu.roll(router_ref[...], (LANES - block * experts) % LANES, axis=1)
    term_ref[:, :, width:] = router.astype(BF16).reshape(slices, depth, LANES)


def branch_kernel(halves, *refs):
    mixed_refs = refs[:halves]
    first_ref, rest_ref, inputs_ref, gain_ref, middle_ref, *normed_refs = refs[halves:]
    width = first_ref.shape[-1]
    blocks = [first_ref[...].reshape(D, width)]
    blocks += [rest_ref[:, n].reshape(D, width) for n in range(rest_ref.shape[1])]
    weight = jnp.concatenate(blocks, axis=1)
    mixed = jnp.concatenate([ref[...] for ref in mixed_refs], axis=0)
    middle = inputs_ref[...].astype(F32) + dot_nt(mixed, weight)
    scale = lax.rsqrt(jnp.mean(middle * middle, axis=1, keepdims=True) + EPS)
    middle_ref[...] = middle
    normed = (middle * scale * gain_ref[...]).astype(BF16)
    for n, ref in enumerate(normed_refs):
        ref[...] = normed[n * CHUNK : (n + 1) * CHUNK]


def middle_back_kernel(
    own_ref, up_ref, down_ref, gates_ref, select_ref, router_ref, middle_ref, gain_ref, grad_ref,
    middle_grad_ref, branch_ref, high_ref, low_ref, gain_grad_ref,
):
    grad = own_ref[...].astype(F32) + up_ref[...].astype(F32) + down_ref[...].astype(F32)
    pairs = dot_nn(grad[:, D:].astype(BF16), select_ref[...])
    gates, router = gates_ref[...], router_ref[...]
    logit_grad = gates * (pairs - jnp.sum(gates * pairs, axis=1, keepdims=True))
    high = logit_grad.astype(BF16)
    low = (logit_grad - high.astype(F32)).astype(BF16)
    high_ref[...] = high
    low_ref[...] = low
    grad = grad[:, :D] + dot_nt(high, router) + dot_nt(low, router)
    back, gain_grad = norm_back(middle_ref[...], gain_ref[...], grad)
    middle_grad = grad_ref[...].astype(F32) + back
    middle_grad_ref[...] = middle_grad
    branch_ref[...] = middle_grad.astype(BF16)

    @pl.when(pl.program_id(0) == 0)
    def _():
        gain_grad_ref[...] = gain_grad

    @pl.when(pl.program_id(0) > 0)
    def _():
        gain_grad_ref[...] += gain_grad


def project_back_kernel(halves, *refs):
    dquery_refs, refs = refs[:halves], refs[halves:]
    own_refs, refs = refs[:halves], refs[halves:]
    next_refs, refs = refs[:halves], refs[halves:]
    (half_ref, normed_t_ref, first_ref, rest_ref, cos_ref, sin_ref, mine_ref, other_ref, total_ref,
     held_ref) = refs
    block = pl.program_id(0)
    key_cos, key_sin = key_tables(cos_ref[...], sin_ref[...])
    tiles = [jnp.concatenate([ref[...] for ref in dquery_refs], axis=0)]
    for col in range(0, own_refs[0].shape[1], LANES):
        cols = slice(col, col + LANES)
        tile = jnp.concatenate(
            [own[:, cols] + after_[:, cols].astype(F32) for own, after_ in zip(own_refs, next_refs)],
            axis=0,
        )
        tiles.append(rotate_tile(tile, key_cos, key_sin, -1.0).astype(BF16))
    grads = jnp.concatenate(tiles, axis=1)
    hold_weight(first_ref, rest_ref, held_ref)
    dweight = dot_nn(normed_t_ref[...], grads).astype(BF16)
    store_halves(half_ref, mine_ref, other_ref, slice(0, grads.shape[1]), dweight)
    part = dot_nt(grads, held_ref[...])

    @pl.when(block == 0)
    def _():
        total_ref[...] = part

    @pl.when(block > 0)
    def _():
        total_ref[...] += part


def input_back_kernel(
    inputs_ref, total_ref, gain_ref, middle_grad_ref, input_grad_ref, gain_grad_ref
):
    back, gain_grad = norm_back(inputs_ref[...].astype(F32), gain_ref[...], total_ref[...])
    input_grad_ref[...] = middle_grad_ref[...] + back

    @pl.when(pl.program_id(0) == 0)
    def _():
        gain_grad_ref[...] = gain_grad

    @pl.when(pl.program_id(0) > 0)
    def _():
        gain_grad_ref[...] += gain_grad


def joined_sum_kernel(groups, *refs):
    *part_refs, out_ref = refs
    rows = out_ref.shape[0]
    total = part_refs[0][...].astype(F32)
    for ref in part_refs[1:]:
        total = total + ref[:rows, :].astype(F32)
    queries = QUERIES_PER_GROUP * HEAD_WIDTH
    span = queries + 2 * HEAD_WIDTH
    width = total.shape[1] - groups * 2 * HEAD_WIDTH
    for group in range(groups):
        at = group * span
        out_ref[:, at : at + queries] = total[:, group * queries : (group + 1) * queries]
        col = width + group * 2 * HEAD_WIDTH
        out_ref[:, at + queries : at + span] = total[:, col : col + 2 * HEAD_WIDTH]


def norm_back(resid, gain, grad):
    scale = lax.rsqrt(jnp.mean(resid * resid, axis=1, keepdims=True) + EPS)
    gain_grad = jnp.sum(grad * resid * scale, axis=0, keepdims=True)
    scaled = grad * gain
    inner = jnp.sum(scaled * resid, axis=1, keepdims=True)
    return scale * scaled - resid * (scale * scale * scale * inner / D), gain_grad


def slots_kernel(experts, first_ref, ids_ref, rank_ref, pos_ref, ends_ref):
    length = ids_ref.shape[1]
    row = lax.broadcasted_iota(jnp.int32, (SUBLANES, length), 0)
    wanted = jnp.where(row < experts, row + first_ref[0], -1)
    rank = jnp.full((SUBLANES, length), 1 << 30, jnp.int32)
    for k in range(TOPK):
        rank = jnp.where(ids_ref[k : k + 1, :] == wanted, rank_ref[k : k + 1, :], rank)
    limit = jnp.zeros((SUBLANES, 1), jnp.int32)
    for bit in reversed(range((length * TOPK).bit_length())):
        higher = limit + (1 << bit)
        count = jnp.sum(jnp.where(rank < higher, 1.0, 0.0), axis=1, keepdims=True)
        limit = jnp.where(count <= CAP, higher, limit)
    kept = jnp.where(rank < limit, 1.0, 0.0)
    before = jnp.where(
        lax.broadcasted_iota(jnp.int32, (CHUNK, CHUNK), 0)
        < lax.broadcasted_iota(jnp.int32, (CHUNK, CHUNK), 1),
        1.0,
        0.0,
    ).astype(BF16)
    lane = lax.broadcasted_iota(jnp.int32, ends_ref.shape, 1)
    so_far = jnp.zeros((SUBLANES, 1), F32)
    ends = jnp.zeros(ends_ref.shape, F32)
    for n in range(length // CHUNK):
        part = kept[:, n * CHUNK : (n + 1) * CHUNK]
        place = dot_nn(part.astype(BF16), before) + so_far
        pos_ref[n] = jnp.where(part > 0.5, place, -1.0).astype(jnp.int32)
        so_far = so_far + jnp.sum(part, axis=1, keepdims=True)
        ends = jnp.where(lane == n + 1, so_far, ends)
    ends_ref[...] = ends.astype(jnp.int32)


def slot_windows(ends_ref, experts, chunk, window):
    firsts = [ends_ref[e, chunk] // SUBLANES * SUBLANES for e in range(experts)]
    ends = [ends_ref[e, chunk + 1] for e in range(experts)]
    count = jnp.int32(0)
    for first, end in zip(firsts, ends):
        count = jnp.maximum(count, (end - first + window - 1) // window)
    return firsts, ends, count


def window_start(first, n_window, window):
    return pl.multiple_of(jnp.minimum(first + n_window * window, SLOTS - window), SUBLANES)


def dispatch_kernel(with_gates, experts, size, *refs):
    shard_ref, ends_ref, *refs = refs
    if with_gates:
        *x_refs, pos_ref, router_ref, member_ref, out_ref, gate_ref, hot_ref, held_ref, sems = refs
    else:
        *x_refs, pos_ref, out_ref, hot_ref, held_ref, sems = refs
    window = hot_ref.shape[0] // experts
    span = 2 * size - 1
    parts = len(x_refs) // span
    part_rows = held_ref.shape[1] // parts

    def fetch(n, part, source):
        rows = pl.ds(part * part_rows, part_rows)
        return pltpu.make_async_copy(
            x_refs[part * span + source], held_ref.at[n, rows, :], sems.at[n, part]
        )

    for n in range(size):
        for part in range(parts):
            if n == 0:
                fetch(n, part, 0).start()
            else:
                below = shard_ref[0] >= n

                @pl.when(below)
                def _(n=n, part=part):
                    fetch(n, part, n).start()

                @pl.when(jnp.logical_not(below))
                def _(n=n, part=part):
                    fetch(n, part, span - n).start()

    out_ref[...] = jnp.zeros(out_ref.shape, BF16)
    if with_gates:
        gate_ref[...] = jnp.zeros(gate_ref.shape, F32)
    row = lax.broadcasted_iota(jnp.int32, (window, CHUNK), 0)
    halves = held_ref.shape[1] // CHUNK
    for n in range(size):
        for part in range(parts):
            fetch(n, part, 0).wait()
        for half in range(halves):
            chunk = shard_ref[n] * halves + half
            x = held_ref[n, half * CHUNK : (half + 1) * CHUNK, :]
            pos = pos_ref[chunk]
            firsts, ends, count = slot_windows(ends_ref, experts, chunk, window)
            if with_gates:
                logits = jnp.where(member_ref[chunk] > 0.5, dot_nn(x, router_ref[...]), MASKED)
                raised = jnp.exp(logits)
                gates = raised / jnp.sum(raised, axis=1, keepdims=True)
                lane = lax.broadcasted_iota(jnp.int32, gates.shape, 1)
                gates = jnp.where(lane < SUBLANES, gates, 0.0)
                high = gates.astype(BF16).astype(F32)
                gates = (high + pltpu.roll(gates - high, SUBLANES, axis=1)).astype(BF16)

            def body(n_window, _):
                for e in range(experts):
                    start = firsts[e] + n_window * window
                    at = window_start(firsts[e], n_window, window)
                    place = pos[e : e + 1, :]
                    place = jnp.where(place >= start, place - at, -1)
                    hot_ref[e * window : (e + 1) * window, :] = jnp.where(
                        row == place, 1.0, 0.0
                    ).astype(BF16)
                hot = hot_ref[...]
                rows = dot_nn(hot, x)
                if with_gates:
                    gate_rows = dot_nn(hot, gates)
                for e in range(experts):
                    start = firsts[e] + n_window * window
                    at = window_start(firsts[e], n_window, window)
                    part = slice(e * window, (e + 1) * window)

                    @pl.when(start < ends[e])
                    def _():
                        out_ref[e, pl.ds(at, window), :] += rows[part].astype(BF16)
                        if with_gates:
                            gate_ref[e, pl.ds(at, window), :] += gate_rows[part]

                return 0

            lax.fori_loop(0, count, body, 0)


def combine_kernel(with_pairs, sizes, order, *refs):
    piece_ref, ends_ref, place_ref, *refs = refs
    rows_refs, refs = refs[: len(sizes)], refs[len(sizes) :]
    if with_pairs:
        pair_refs, refs = refs[: len(sizes)], refs[len(sizes) :]
        *out_refs, held_ref, sems, hot_ref, total_ref, held_pair_ref, pair_total_ref = refs
    else:
        *out_refs, held_ref, sems, hot_ref, total_ref = refs
    experts = sum(sizes)
    count_out = len(out_refs)
    home = [(n, e) for n, size in enumerate(sizes) for e in range(size)]
    step, steps = pl.program_id(0), pl.num_programs(0)
    halves = steps // len(order)
    visits = steps // count_out

    def chunk_of(at_step):
        return piece_ref[at_step // halves] * halves + at_step % halves

    def copies(chunk, n_window, slot):
        firsts = slot_windows(ends_ref, experts, chunk, WINDOW)[0]
        return [
            pltpu.make_async_copy(
                rows_refs[n].at[own, pl.ds(window_start(firsts[e], n_window, WINDOW), WINDOW), :],
                held_ref.at[slot, pl.ds(e * WINDOW, WINDOW), :],
                sems.at[slot, e],
            )
            for e, (n, own) in enumerate(home)
        ]

    @pl.when(step == 0)
    def _():
        for copy in copies(chunk_of(step), 0, 0):
            copy.start()

    @pl.when(step + 1 < steps)
    def _():
        for copy in copies(chunk_of(step + 1), 0, (step + 1) % 2):
            copy.start()

    chunk = chunk_of(step)
    firsts, ends, count = slot_windows(ends_ref, experts, chunk, WINDOW)
    lane = lax.broadcasted_iota(jnp.int32, (CHUNK, WINDOW), 1)
    places = place_ref[...]

    def mark(n_window):
        for e, (n, own) in enumerate(home):
            start = firsts[e] + n_window * WINDOW
            at = window_start(firsts[e], n_window, WINDOW)
            place = places[:, e : e + 1]
            place = jnp.where(place >= start, place - at, -1)
            cols = slice(e * WINDOW, (e + 1) * WINDOW)
            hot_ref[:, cols] = jnp.where(lane == place, 1.0, 0.0).astype(BF16)
            if with_pairs:
                held_pair_ref[cols, :] = pair_refs[n][own, pl.ds(at, WINDOW), :]

    mark(0)
    for copy in copies(chunk, 0, step % 2):
        copy.wait()
    total_ref[...] = dot_nn(hot_ref[...], held_ref[step % 2])
    if with_pairs:
        pair_total_ref[...] = dot_nn(hot_ref[...], held_pair_ref[...])

    def body(n_window, _):
        more = copies(chunk, n_window, 2)
        for copy in more:
            copy.start()
        mark(n_window)
        for copy in more:
            copy.wait()
        total_ref[...] += dot_nn(hot_ref[...], held_ref[2])
        if with_pairs:
            pair_total_ref[...] += dot_nn(hot_ref[...], held_pair_ref[...])
        return 0

    lax.fori_loop(1, count, body, 0)
    for n, out_ref in enumerate(out_refs):

        @pl.when(step // visits == n)
        def _(n=n * visits // halves, out_ref=out_ref):
            out_ref[:, :D] = total_ref[...].astype(BF16)
            if with_pairs:
                place = -order[n] % len(order) * 2 * experts
                out_ref[:, D:] = pltpu.roll(pair_total_ref[...], place, axis=1).astype(BF16)


def expert_kernel(
    first, experts, half_ref, x_ref, grad_ref, gate_ref, weight_ref, y_ref, z_ref, pair_ref, *term_refs,
):
    e = first + pl.program_id(0)
    x, slot_grad = x_ref[0], grad_ref[0]
    w_in, w_out = weight_ref[0, :, : 2 * FF], weight_ref[0, :, 2 * FF :]
    lane = lax.broadcasted_iota(jnp.int32, gate_ref.shape[1:], 1)
    gate = jnp.sum(
        jnp.where((lane == e) | (lane == e + SUBLANES), gate_ref[0], 0.0), axis=1, keepdims=True
    )
    gate_up = dot_nn(x, w_in)
    gate_part, up_part = gate_up[:, :FF], gate_up[:, FF:]
    sigmoid = jax.nn.sigmoid(gate_part)
    silu = gate_part * sigmoid
    hidden = (silu * up_part).astype(BF16)
    raw = dot_nn(slot_grad, w_out)
    pair = jnp.sum(hidden.astype(F32) * raw, axis=1, keepdims=True)
    high = pair.astype(BF16).astype(F32)
    pair_ref[0] = jnp.where(
        lane == e, high, jnp.where(lane == e + experts, pair - high, 0.0)
    ).astype(BF16)
    hidden_grad = gate * raw
    gate_up_grad = jnp.concatenate(
        [
            (hidden_grad * up_part * sigmoid * (1.0 + gate_part * (1.0 - sigmoid))).astype(BF16),
            (hidden_grad * silu).astype(BF16),
        ],
        axis=1,
    )
    z_ref[0] = dot_nt(gate_up_grad, w_in).astype(BF16)
    y_ref[0] = (gate * dot_nt(hidden, w_out)).astype(BF16)
    rows_grad = (gate * slot_grad.astype(F32)).astype(BF16)
    in_term = dot_tn(x, gate_up_grad).astype(BF16)
    out_term = dot_tn(rows_grad, hidden).astype(BF16)
    if len(term_refs) == 2:
        store_halves(half_ref, *term_refs, slice(0, 2 * FF), in_term)
        store_halves(half_ref, *term_refs, slice(2 * FF, 3 * FF), out_term)
    else:
        term_ref = term_refs[0]
        slices, depth, _ = term_ref.shape
        term_ref[:, :, : 2 * FF] = in_term.reshape(slices, depth, 2 * FF)
        term_ref[:, :, 2 * FF :] = out_term.reshape(slices, depth, FF)


def after(value, *others):
    return lax.optimization_barrier((value,) + others)[0]


def pair_scatter(mine, other, size, *gates):
    taken = after(lax.ppermute(other, "gx", [(s, s ^ 1) for s in range(size)]), *gates)
    mine = (mine.astype(F32) + taken.astype(F32)).astype(mine.dtype)
    groups = [list(range(0, size, 2)), list(range(1, size, 2))]
    total = lax.psum_scatter(mine, "gx", scatter_dimension=0, tiled=True, axis_index_groups=groups)
    return lax.optimization_barrier(total)[0]


def direct_gather(part, size):
    return jnp.stack(
        [
            lax.ppermute(part, "gy", [(s, (s + k) % size) for s in range(size)])
            for k in range(1, size)
        ]
    )


def gather_step(pair, step, size, *gates):
    up, down = (after(part, *gates) if gates else part for part in pair)
    return (
        lax.ppermute(up, "gy", [(s, s + 1) for s in range(step, size - 1)]),
        lax.ppermute(down, "gy", [(s + 1, s) for s in range(0, size - 1 - step)]),
    )


def sum_step(parts, pair, step, size, *gates):
    above, below = parts[step], parts[size - step]
    if gates:
        pair = tuple(after(part, *gates) for part in pair)
    if pair is not None:
        above, below = (
            (a.astype(F32) + b.astype(F32)).astype(a.dtype)
            for a, b in zip((above, below), pair)
        )
    return (
        lax.ppermute(above, "gy", [(s, s + 1) for s in range(step)]),
        lax.ppermute(below, "gy", [(size - 1 - s, size - 2 - s) for s in range(step)]),
    )


def sum_steps_of(parts, size, gates):
    steps, pair = [], None
    for step in range(1, size):
        pair = sum_step(parts, pair, step, size, *gates.get(step, ()))
        steps.append(pair)
    return steps


def direct_sum(parts, size):
    total = parts[0].astype(F32)
    for k in range(1, size):
        total = total + lax.ppermute(
            parts[k], "gy", [(s, (s - k) % size) for s in range(size)]
        ).astype(F32)
    return total


def summed(parts, steps):
    return parts[0].astype(F32) + steps[-1][0].astype(F32) + steps[-1][1].astype(F32)


def shards(
    nx,
    ny,
    tokens,
    attn_gain,
    query_key_value_weight,
    out_weight,
    moe_gain,
    router_weight,
    expert_in,
    expert_out,
    expert_ids,
    route_order,
    segment_ids,
    out_grad,
):
    rows = tokens.shape[0]
    length = segment_ids.shape[1]
    depth = out_weight.shape[1]
    heads_width = out_weight.shape[0]
    groups = heads_width // (HEAD_WIDTH * QUERIES_PER_GROUP)
    spare = -heads_width % LANES
    width = heads_width + spare
    kv_width = groups * 2 * HEAD_WIDTH
    joined = width + kv_width
    experts = router_weight.shape[0]
    all_experts = experts * ny
    chunks = length // CHUNK
    own_chunks = rows // CHUNK
    me = lax.axis_index("gy")
    first_expert = me * experts
    first_row = me * rows
    both = ("gx", "gy")

    pos, ends = pl.pallas_call(
        functools.partial(slots_kernel, experts),
        in_specs=[
            pl.BlockSpec(memory_space=pltpu.SMEM),
            pl.BlockSpec(memory_space=pltpu.VMEM),
            pl.BlockSpec(memory_space=pltpu.VMEM),
        ],
        out_shape=[
            jax.ShapeDtypeStruct((chunks, SUBLANES, CHUNK), jnp.int32),
            jax.ShapeDtypeStruct((SUBLANES, LANES), jnp.int32),
        ],
        compiler_params=params(),
        cost_estimate=cost(3),
        name="slots",
    )(
        first_expert.reshape(1),
        expert_ids.T,
        route_order[0].reshape(length, TOPK).T,
    )
    places = jnp.pad(
        pos.transpose(0, 2, 1).reshape(length, SUBLANES), ((0, 0), (0, LANES - SUBLANES))
    )
    ends = ends[:, : chunks + 1]
    pieces = (me - jnp.arange(ny, dtype=jnp.int32)) % ny
    lane_expert = jnp.arange(LANES, dtype=jnp.int32)
    turned_expert = (me - lane_expert // experts) % ny * experts + lane_expert % experts
    turned_expert = jnp.where(lane_expert < all_experts, turned_expert, -1)
    members = jnp.any(expert_ids[:, :, None] == turned_expert[None, None, :], axis=1)
    members = members.astype(F32).reshape(chunks, CHUNK, LANES)
    own_ids = lax.dynamic_slice_in_dim(expert_ids, first_row, rows, 0)
    own_members = jnp.any(own_ids[:, :, None] == turned_expert[None, None, :], axis=1).astype(F32)

    inputs = tokens.astype(F32)
    scale_one = lax.rsqrt(jnp.mean(inputs * inputs, axis=1, keepdims=True) + EPS)
    normed_one = (inputs * scale_one * attn_gain[None, :]).astype(BF16)
    normed_one_t = normed_one.T
    cosine, sine = rope_tiles(first_row, rows)
    labels = jnp.concatenate([jnp.full((SEGMAX,), -1, jnp.int32), segment_ids[0]])
    labels = lax.dynamic_slice_in_dim(labels, first_row, rows + SEGMAX, 0)
    position = jnp.arange(rows + SEGMAX, dtype=jnp.int32)
    bias = jnp.stack(
        [
            jnp.where(
                (labels[s : s + 2 * SEGMAX, None] == labels[None, s + SEGMAX : s + 2 * SEGMAX])
                & (
                    position[s : s + 2 * SEGMAX, None]
                    <= position[None, s + SEGMAX : s + 2 * SEGMAX]
                ),
                0.0,
                MASKED,
            ).astype(F32)
            for s in range(0, rows, SEGMAX)
        ]
    )
    grouped = query_key_value_weight.reshape(depth, groups, QUERIES_PER_GROUP + 2, HEAD_WIDTH)
    own_joined = jnp.concatenate(
        [
            jnp.pad(
                grouped[:, :, :QUERIES_PER_GROUP].reshape(depth, heads_width), ((0, 0), (0, spare))
            ),
            grouped[:, :, QUERIES_PER_GROUP:].reshape(depth, kv_width),
        ],
        axis=1,
    )
    own_out = jnp.pad(out_weight.T, ((0, 0), (0, spare)))
    own_router = jnp.pad(router_weight.T, ((0, 0), (0, LANES - experts)))
    gap = -(joined + LANES) % width
    own_weights = jnp.concatenate(
        [own_joined, own_router, jnp.zeros((depth, gap), BF16), own_out], axis=1
    )
    own_second = jnp.concatenate([own_out, own_router], axis=1)
    cut = experts * 2 // 5
    bounds = ((0, cut), (cut, experts))
    own_experts = [
        jnp.concatenate([expert_in[lo:hi], expert_out[lo:hi]], axis=2) for lo, hi in bounds
    ]
    first_weights = lax.all_gather(own_weights, "gx", axis=0)
    line_joined = after(direct_gather(own_joined, ny), *own_experts)
    own_second = after(own_second, line_joined)
    line_second = direct_gather(own_second, ny)
    ready = after(out_grad, line_second, bias, cosine, sine, normed_one)
    grad_steps = [gather_step((ready, ready), 0, ny)]
    rest_joined = lax.all_gather(line_joined, "gx", axis=0)
    rest_second = lax.all_gather(line_second, "gx", axis=0)
    wide = []
    for own in own_experts:
        wide.append(lax.all_gather(own, "gx", axis=1, tiled=True))


    out_column = (joined + LANES + gap) // width
    rest_block = lambda b: (0, jnp.maximum(b - 1, 0), 0, 0)
    joined_specs = [
        pl.BlockSpec((nx, depth, joined), lambda b: (0, 0, 0)),
        pl.BlockSpec((nx, pl.Squeezed(), depth, joined), rest_block),
    ]
    out_specs = [
        pl.BlockSpec((nx, depth, width), lambda b: (0, 0, out_column)),
        pl.BlockSpec((nx, pl.Squeezed(), depth, width), rest_block),
    ]
    held_joined = pltpu.VMEM((D, joined), BF16)
    held_out = pltpu.VMEM((D, width), BF16)
    query, kv = pl.pallas_call(
        project_kernel,
        grid=(ny,),
        in_specs=[
            whole((rows, D)),
            *joined_specs,
            whole((rows, LANES)),
            whole((rows, LANES)),
        ],
        out_specs=[
            pl.BlockSpec((rows, width), lambda b: (0, b)),
            pl.BlockSpec((rows, kv_width), lambda b: (0, b)),
        ],
        out_shape=[
            jax.ShapeDtypeStruct((rows, ny * width), BF16),
            jax.ShapeDtypeStruct((rows, ny * kv_width), BF16),
        ],
        scratch_shapes=[held_joined],
        compiler_params=params(),
        cost_estimate=cost(10),
        name="project",
    )(after(normed_one, bias), first_weights, rest_joined, cosine, sine)
    halo = lax.ppermute(kv[rows - SEGMAX :], "gy", [(s, s + 1) for s in range(ny - 1)])
    halves = rows // SEGMAX
    half_rows = lambda n, w: pl.BlockSpec((SEGMAX, w), lambda b: (n, b))
    whole_half = lambda n, w: pl.BlockSpec((SEGMAX, w), lambda b: (n, 0))
    below_rows = pl.BlockSpec((SEGMAX, kv_width), lambda b: (0, (b + ny - 1) % ny))
    bias_half = lambda n: pl.BlockSpec((pl.Squeezed(), 2 * SEGMAX, SEGMAX), lambda b: (n, 0, 0))

    def window(n):
        if n == 0:
            return [half_rows(0, kv_width), below_rows], (kv, halo)
        return [half_rows(n, kv_width), half_rows(n - 1, kv_width)], (kv, kv)

    mixed = [None] * halves
    for n in reversed(range(halves)):
        specs, arrays = window(n)
        mixed[n] = pl.pallas_call(
            attend_kernel,
            grid=(ny,),
            in_specs=[half_rows(n, width), *specs, bias_half(n)],
            out_specs=half_rows(0, width),
            out_shape=jax.ShapeDtypeStruct((SEGMAX, ny * width), BF16),
            compiler_params=params(),
            cost_estimate=cost(8),
            name="attend",
        )(query, *arrays, bias)
    for step in range(1, ny - 2):
        grad_steps.append(gather_step(grad_steps[-1], step, ny, mixed[-1]))
    middle, *normed_chunks = pl.pallas_call(
        functools.partial(branch_kernel, halves),
        grid=(1,),
        in_specs=[whole((SEGMAX, ny * width))] * halves
        + [
            out_specs[0],
            pl.BlockSpec((nx, ny - 1, depth, width), lambda _: (0, 0, 0, 0)),
            whole((rows, D)),
            whole((1, D)),
        ],
        out_specs=[whole((rows, D))] + [whole((CHUNK, D))] * own_chunks,
        out_shape=[jax.ShapeDtypeStruct((rows, D), F32)]
        + [jax.ShapeDtypeStruct((CHUNK, D), BF16)] * own_chunks,
        compiler_params=params(),
        cost_estimate=cost(7),
        name="branch",
    )(*mixed, first_weights, rest_second, tokens, moe_gain[None, :])

    router = jnp.concatenate(
        [
            first_weights[:, None, :, joined : joined + experts],
            rest_second[:, :, :, width : width + experts],
        ],
        axis=1,
    )
    router = router.transpose(0, 2, 1, 3).reshape(D, all_experts)
    router = jnp.pad(router, ((0, 0), (0, LANES - all_experts)))
    normed_two = jnp.concatenate(normed_chunks, axis=0)
    normed_steps = []
    for part in normed_chunks:
        part = after(part, grad_steps[-1])
        normed_steps.append([(part, part)])
    for step in range(ny - 1):
        for steps in normed_steps:
            steps.append(gather_step(steps[-1], step, ny))
    grad_steps.append(
        gather_step(grad_steps[-1], ny - 2, ny, *[steps[-1] for steps in normed_steps])
    )
    normed_pieces = []
    for part, steps in zip(normed_chunks, normed_steps):
        normed_pieces += [part] + [up for up, _ in steps[1:]] + [down for _, down in steps[1:]]
    grad_pieces = [out_grad] + [up for up, _ in grad_steps] + [down for _, down in grad_steps]
    smem = pl.BlockSpec(memory_space=pltpu.SMEM)
    vmem = pl.BlockSpec(memory_space=pltpu.VMEM)
    slot_rows = jax.ShapeDtypeStruct((experts, SLOTS, D), BF16)
    slot_lanes = lambda kind: jax.ShapeDtypeStruct((experts, SLOTS, LANES), kind)
    dispatch_scratch = lambda parts: [
        pltpu.VMEM((experts * SHORT_WINDOW, CHUNK), BF16),
        pltpu.VMEM((ny, rows, D), BF16),
        pltpu.SemaphoreType.DMA((ny, parts)),
    ]
    hbm = pl.BlockSpec(memory_space=pl.ANY)
    slot_grads = pl.pallas_call(
        functools.partial(dispatch_kernel, False, experts, ny),
        in_specs=[smem, smem] + [hbm] * (2 * ny - 1) + [vmem],
        out_specs=vmem,
        out_shape=slot_rows,
        scratch_shapes=dispatch_scratch(1),
        compiler_params=params(),
        cost_estimate=cost(26),
        name="dispatch_grads",
    )(pieces, ends, *grad_pieces, pos)
    dispatched, slot_gates = pl.pallas_call(
        functools.partial(dispatch_kernel, True, experts, ny),
        in_specs=[smem, smem] + [hbm] * len(normed_pieces) + [vmem] * 3,
        out_specs=[vmem, vmem],
        out_shape=[slot_rows, slot_lanes(F32)],
        scratch_shapes=dispatch_scratch(own_chunks),
        compiler_params=params(),
        cost_estimate=cost(31),
        name="dispatch_rows",
    )(pieces, ends, *normed_pieces, pos, router, members)

    half = (lax.axis_index("gx") % 2).reshape(1)
    y_rows, z_rows, slot_pairs, weight_terms = [], [], [], []
    for n, (lo, hi) in enumerate(bounds):
        outer = lambda *shape: pl.BlockSpec((1,) + shape, lambda e, lo=lo: (lo + e, 0, 0))
        inner = lambda *shape: pl.BlockSpec((1,) + shape, lambda e: (e, 0, 0))
        parts = n + 1
        slices = pl.BlockSpec((nx // parts, pl.Squeezed(), depth, 3 * FF), lambda e: (0, e, 0, 0))
        y, z, pair, *terms = pl.pallas_call(
            functools.partial(expert_kernel, lo, experts),
            grid=(hi - lo,),
            in_specs=[
                smem,
                outer(SLOTS, D),
                outer(SLOTS, D),
                outer(SLOTS, LANES),
                inner(D, 3 * FF),
            ],
            out_specs=[inner(SLOTS, D), inner(SLOTS, D), inner(SLOTS, LANES)]
            + [slices] * parts,
            out_shape=[
                jax.ShapeDtypeStruct((hi - lo, SLOTS, D), BF16),
                jax.ShapeDtypeStruct((hi - lo, SLOTS, D), BF16),
                jax.ShapeDtypeStruct((hi - lo, SLOTS, LANES), BF16),
            ]
            + [jax.ShapeDtypeStruct((nx // parts, hi - lo, depth, 3 * FF), BF16)] * parts,
            compiler_params=params(),
            cost_estimate=cost(9 * (hi - lo)),
            name="experts",
        )(half, dispatched, slot_grads, slot_gates, wide[n])
        y_rows.append(y)
        z_rows.append(z)
        slot_pairs.append(pair)
        weight_terms.append(terms)
    def combine(rows_in, which, pairs=None):
        held = pltpu.VMEM((3, experts * WINDOW, D), BF16)
        sems = pltpu.SemaphoreType.DMA((3, experts))
        hot_t = pltpu.VMEM((CHUNK, experts * WINDOW), BF16)
        total = pltpu.VMEM((CHUNK, D), F32)
        more = pairs is not None
        columns = D + LANES * more
        halves = chunks // ny
        here = pieces[jnp.array(which)]

        def place_map(c, piece_ref):
            return (piece_ref[c // halves] * halves + c % halves, 0)

        visits = 1 if more else halves

        def out_map(n):
            return lambda c, piece_ref: (jnp.clip(c - n * visits, 0, visits - 1), 0)

        return pl.pallas_call(
            functools.partial(combine_kernel, more, tuple(hi - lo for lo, hi in bounds), which),
            grid_spec=pltpu.PrefetchScalarGridSpec(
                num_scalar_prefetch=1,
                grid=(halves * len(which),),
                in_specs=[smem, pl.BlockSpec((CHUNK, LANES), place_map)]
                + [hbm] * len(bounds)
                + [once((hi - lo, SLOTS, LANES)) for lo, hi in bounds] * more,
                out_specs=[
                    pl.BlockSpec((CHUNK, columns), out_map(n))
                    for n in range(len(which) * halves // visits)
                ],
                scratch_shapes=[held, sems, hot_t, total]
                + [
                    pltpu.VMEM((experts * WINDOW, LANES), BF16),
                    pltpu.VMEM((CHUNK, LANES), F32),
                ]
                * more,
            ),
            out_shape=[jax.ShapeDtypeStruct((CHUNK * visits, columns), BF16)]
            * (len(which) * halves // visits),
            compiler_params=params(),
            cost_estimate=cost(16),
            name="combine_grads" if more else "combine_rows",
        )(here, ends, places, *rows_in, *(pairs if more else []))

    outer_pieces = sorted({1, ny - 1})
    inner_pieces = [k for k in range(ny) if k not in outer_pieces]
    order = outer_pieces + inner_pieces
    token_sum = combine(z_rows, order, slot_pairs)
    token_sum = [
        [token_sum[order.index(k) * own_chunks + n] for k in range(ny)] for n in range(own_chunks)
    ]
    token_steps = [[] for _ in token_sum]
    for step in range(1, ny):
        for parts, steps in zip(token_sum, token_steps):
            steps.append(sum_step(parts, steps[-1] if steps else None, step, ny))
    own_logits = jnp.where(own_members > 0.5, dot_nn(normed_two, router), MASKED)
    own_raised = jnp.exp(own_logits)
    own_gates = own_raised / jnp.sum(own_raised, axis=1, keepdims=True)
    source = lane_expert // (2 * experts) * experts + lane_expert % experts
    source = jnp.where(lane_expert < 2 * all_experts, source, -1)
    select = (source[:, None] == lane_expert[None, :]).astype(BF16)
    weight_sums = [
        lax.psum_scatter(weight_terms[0][0], "gx", scatter_dimension=0, tiled=True)[0],
        pair_scatter(*weight_terms[1], nx, token_sum[0][0]),
    ]
    combined = combine([after(y, [steps[-2] for steps in token_steps]) for y in y_rows], order)
    combined = [combined[order.index(k)] for k in range(ny)]
    row_block = lambda w: pl.BlockSpec((LANES, w), lambda r: (r, 0))
    later_block = lambda n, w: pl.BlockSpec((LANES, w), lambda r: (r + n * CHUNK // LANES, 0))
    backs = []
    for n, (parts, steps) in enumerate(zip(token_sum, token_steps)):
        backs.append(
            pl.pallas_call(
                middle_back_kernel,
                grid=(CHUNK // LANES,),
                in_specs=[row_block(D + LANES)] * 3
                + [later_block(n, LANES), whole((LANES, LANES)), whole((D, LANES))]
                + [later_block(n, D), whole((1, D)), later_block(n, D)],
                out_specs=[row_block(D), row_block(D), row_block(LANES), row_block(LANES)]
                + [whole((1, D))],
                out_shape=[
                    jax.ShapeDtypeStruct((CHUNK, D), F32),
                    jax.ShapeDtypeStruct((CHUNK, D), BF16),
                    jax.ShapeDtypeStruct((CHUNK, LANES), BF16),
                    jax.ShapeDtypeStruct((CHUNK, LANES), BF16),
                    jax.ShapeDtypeStruct((1, D), F32),
                ],
                compiler_params=params(),
                cost_estimate=cost(4),
                name="middle_back",
            )(after(parts[0], *combined), *steps[-1], own_gates, select, router, middle,
              moe_gain[None, :], out_grad)
        )
    middle_grads, branch_grads, highs, lows, moe_gain_grads = zip(*backs)
    moe_gain_grad = sum(moe_gain_grads)

    combined_steps = [sum_step(combined, None, 1, ny)]

    dquery, dkv, dbefore = [], [], []
    for n in range(halves):
        specs, arrays = window(n)
        outs = pl.pallas_call(
            attend_back_kernel,
            grid=(ny,),
            in_specs=[
                half_rows(n, width),
                *specs,
                bias_half(n),
                *out_specs,
                whole((SEGMAX, D)),
                whole_half(n, LANES),
                whole_half(n, LANES),
            ],
            out_specs=[half_rows(0, width), half_rows(0, kv_width), half_rows(0, kv_width)],
            out_shape=[
                jax.ShapeDtypeStruct((SEGMAX, ny * width), BF16),
                jax.ShapeDtypeStruct((SEGMAX, ny * kv_width), F32),
                jax.ShapeDtypeStruct((SEGMAX, ny * kv_width), F32 if n else BF16),
            ],
            scratch_shapes=[pltpu.VMEM((SEGMAX, width), F32), held_out],
            compiler_params=params(),
            cost_estimate=cost(17),
            name="attend_back",
        )(query, *arrays, bias, first_weights, rest_second, after(branch_grads[n], *combined, *dbefore),
          cosine, sine)
        for kept, out in zip((dquery, dkv, dbefore), outs):
            kept.append(out)
    halo_grad = lax.ppermute(dbefore[0], "gy", [(s + 1, s) for s in range(ny - 1)])
    second_term = pl.pallas_call(
        functools.partial(branch_weights_kernel, experts, halves),
        grid=(ny,),
        in_specs=[whole((D, rows))]
        + [whole((CHUNK, D))] * halves
        + [whole((CHUNK, LANES))] * (2 * halves)
        + [half_rows(0, width)] * halves,
        out_specs=pl.BlockSpec((nx, pl.Squeezed(), depth, width + LANES), lambda b: (0, b, 0, 0)),
        out_shape=jax.ShapeDtypeStruct((nx, ny, depth, width + LANES), BF16),
        scratch_shapes=[pltpu.VMEM((D, rows), BF16), pltpu.VMEM((D, LANES), F32)],
        compiler_params=params(),
        cost_estimate=cost(9),
        name="branch_weights",
    )(normed_two.T, *branch_grads, *highs, *lows, *mixed)
    for step in range(2, ny):
        gates = (halo_grad,) if step == 2 else ()
        combined_steps.append(sum_step(combined, combined_steps[-1], step, ny, *gates))
    next_rows = pl.BlockSpec((SEGMAX, kv_width), lambda b: (0, (b + 1) % ny))
    *joined_terms, normed_one_grad = pl.pallas_call(
        functools.partial(project_back_kernel, halves),
        grid=(ny,),
        in_specs=[half_rows(0, width)] * halves
        + [half_rows(0, kv_width)] * (2 * halves - 1)
        + [
            next_rows,
            smem,
            whole((D, rows)),
            *joined_specs,
            whole((rows, LANES)),
            whole((rows, LANES)),
        ],
        out_specs=[pl.BlockSpec((nx // 2, pl.Squeezed(), depth, joined), lambda b: (0, b, 0, 0))] * 2
        + [whole((rows, D))],
        out_shape=[jax.ShapeDtypeStruct((nx // 2, ny, depth, joined), BF16)] * 2
        + [jax.ShapeDtypeStruct((rows, D), F32)],
        scratch_shapes=[held_joined],
        compiler_params=params(),
        cost_estimate=cost(22),
        name="project_back",
    )(*dquery, *dkv, *dbefore[1:], halo_grad, half, normed_one_t, first_weights, rest_joined, cosine,
      sine)
    in_grad, down_grad = [], []
    for part in after(tuple(weight_sums), joined_terms):
        in_grad.append(part[..., : 2 * FF].astype(F32))
        down_grad.append(part[..., 2 * FF :].astype(F32))
    in_grad, down_grad = jnp.concatenate(in_grad), jnp.concatenate(down_grad)
    input_grad, attn_gain_grad = pl.pallas_call(
        input_back_kernel,
        grid=(rows // LANES,),
        in_specs=[row_block(D), row_block(D), whole((1, D)), row_block(D)],
        out_specs=[row_block(D), whole((1, D))],
        out_shape=[
            jax.ShapeDtypeStruct((rows, D), F32),
            jax.ShapeDtypeStruct((1, D), F32),
        ],
        compiler_params=params(),
        cost_estimate=cost(6),
        name="input_back",
    )(tokens, normed_one_grad, attn_gain[None, :], after(jnp.concatenate(middle_grads), in_grad, down_grad))

    second_sum = lax.psum_scatter(
        after(second_term, weight_sums[0]), "gx", scatter_dimension=0, tiled=True
    )
    second_sum = lax.optimization_barrier(second_sum)[0]
    mine, other = joined_terms
    other = after(other, combined_steps[1])
    joined_sum = pair_scatter(mine, other, nx, second_sum, *weight_sums)
    gain_sums = jnp.concatenate([attn_gain_grad, moe_gain_grad])
    bit = 1
    while bit < nx:
        pairs = [(s, s ^ bit) for s in range(nx)]
        gain_sums = gain_sums + lax.ppermute(gain_sums, "gx", pairs)
        bit = 2 * bit
    high = gain_sums.astype(BF16)
    low = (gain_sums - high.astype(F32)).astype(BF16)
    gains = jnp.stack([high, low]).reshape(-1)
    gain_rows = -(-gains.shape[0] // joined)
    gain_rows += -gain_rows % SUBLANES
    gains = jnp.pad(gains, (0, gain_rows * joined - gains.shape[0])).reshape(gain_rows, joined)
    second_sum = direct_sum(second_sum, ny)
    out_weight_grad = second_sum[:, :heads_width].T
    router_grad = second_sum[:, width : width + experts].T
    joined_sum = after(joined_sum, gains)
    last = tuple(after(part, joined_sum) for part in combined_steps[-1])
    layer_out = (middle + summed(combined, [last])).astype(BF16)
    joined_parts, gain_parts = [joined_sum[0]], [gains]
    for k in range(1, ny):
        part = jnp.concatenate([joined_sum[k], gains], axis=0)
        part = lax.ppermute(part, "gy", [(s, (s - k) % ny) for s in range(ny)])
        joined_parts.append(part)
        gain_parts.append(part[depth:])
    qkv_grad = pl.pallas_call(
        functools.partial(joined_sum_kernel, groups),
        out_shape=jax.ShapeDtypeStruct(query_key_value_weight.shape, F32),
        compiler_params=params(),
        cost_estimate=cost(2),
        name="joined_sum",
    )(*joined_parts)
    gain_sums = jnp.roll(jnp.stack(gain_parts), me, axis=0).astype(F32)
    gain_sums = gain_sums.reshape(ny, -1)[:, : 4 * D].reshape(ny, 2, 2, D)
    gain_sums = jnp.sum(gain_sums, axis=(0, 1))
    return (
        layer_out,
        input_grad,
        gain_sums[0],
        qkv_grad,
        out_weight_grad,
        gain_sums[1],
        router_grad,
        in_grad,
        down_grad,
    )


def solution(mesh):
    in_specs = (
        P(("gx", "gy"), None),
        P(),
        P("gx", "gy"),
        P("gy", "gx"),
        P(),
        P("gy", "gx"),
        P("gy", "gx", None),
        P("gy", "gx", None),
        P("gx", None),
        P("gx", None),
        P("gx", None),
        P(("gx", "gy"), None),
    )
    out_specs = (
        P(("gx", "gy"), None),
        P(("gx", "gy"), None),
        P(),
        P("gx", "gy"),
        P("gy", "gx"),
        P(),
        P("gy", "gx"),
        P("gy", "gx", None),
        P("gy", "gx", None),
    )
    body = functools.partial(shards, mesh.shape["gx"], mesh.shape["gy"])
    return jax.shard_map(body, mesh=mesh, in_specs=in_specs, out_specs=out_specs, check_vma=False)
```

```python
import functools

import jax
import jax.numpy as jnp
from jax import lax
from jax.experimental import pallas as pl
from jax.experimental.pallas import tpu as pltpu
from jax.sharding import PartitionSpec as P

D = 1536
HEAD_WIDTH = 64
FF = 512
TOPK = 8
SEGMAX = 256
QUERIES_PER_GROUP = 3
CAP = 460
SLOTS = 464
WINDOW = 128
SHORT_WINDOW = 96
CHUNK = 256
LANES = 128
SUBLANES = 16

EPS = 1e-05
MASKED = -1e30
SCORE_SCALE = HEAD_WIDTH ** (-0.5)
VMEM_BYTES = 60 * 1024 * 1024
F32 = jnp.float32
BF16 = jnp.bfloat16


def dot_nn(a, b):
    return lax.dot_general(a, b, (((1,), (0,)), ((), ())), preferred_element_type=F32)


def dot_nt(a, b):
    return lax.dot_general(a, b, (((1,), (1,)), ((), ())), preferred_element_type=F32)


def dot_tn(a, b):
    return lax.dot_general(a, b, (((0,), (0,)), ((), ())), preferred_element_type=F32)


def params(**more):
    return pltpu.CompilerParams(vmem_limit_bytes=VMEM_BYTES, **more)


def cost(micros):
    return pl.CostEstimate(
        flops=int(micros * 1.1e9), bytes_accessed=int(micros * 3.6e6), transcendentals=0
    )


def store_halves(half_ref, mine_ref, other_ref, columns, value):
    slices, depth, _ = mine_ref.shape
    for parity in range(2):
        own = half_ref[0] == parity
        for ref, taken in ((mine_ref, own), (other_ref, jnp.logical_not(own))):

            @pl.when(taken)
            def _(ref=ref, parity=parity):
                for n in range(slices):
                    at = (2 * n + parity) * depth
                    ref[n, :, columns] = value[at : at + depth]


def whole(shape):
    return pl.BlockSpec(shape, lambda *_: (0,) * len(shape))


def once(shape):
    return pl.BlockSpec(shape, lambda *_: (0,) * len(shape), pipeline_mode=pl.Buffered(1))


def rope_tiles(first_row, rows):
    half = HEAD_WIDTH // 2
    freq = jnp.exp(jnp.arange(half, dtype=F32) * (-2.0 * jnp.log(10000.0) / HEAD_WIDTH))
    position = (first_row + jnp.arange(rows, dtype=jnp.int32)).astype(F32)
    angle = position[:, None] * freq[None, :]
    cosine, sine = jnp.cos(angle), jnp.sin(angle)
    return (
        jnp.concatenate([cosine] * 4, axis=1),
        jnp.concatenate([-sine, sine, -sine, sine], axis=1),
    )


def swap_halves(tile):
    lane = lax.broadcasted_iota(jnp.int32, tile.shape, 1)
    half = HEAD_WIDTH // 2
    return jnp.where(
        lane % HEAD_WIDTH < half,
        pltpu.roll(tile, LANES - half, axis=1),
        pltpu.roll(tile, half, axis=1),
    )


def rotate_tile(tile, cosine, sine, sign):
    return tile * cosine + sign * swap_halves(tile) * sine


def key_tables(cosine, sine):
    lane = lax.broadcasted_iota(jnp.int32, cosine.shape, 1)
    is_key = lane < HEAD_WIDTH
    return jnp.where(is_key, cosine, 1.0), jnp.where(is_key, sine, 0.0)


def hold_weight(first_ref, rest_ref, held_ref):
    @pl.when(pl.program_id(0) == 0)
    def _():
        held_ref[...] = first_ref[...].reshape(held_ref.shape)

    @pl.when(pl.program_id(0) > 0)
    def _():
        held_ref[...] = rest_ref[...].reshape(held_ref.shape)


def project_kernel(
    normed_ref, first_ref, rest_ref, cos_ref, sin_ref, query_ref, kv_ref, held_ref
):
    hold_weight(first_ref, rest_ref, held_ref)
    project = dot_nn(normed_ref[...], held_ref[...])
    cosine, sine = cos_ref[...], sin_ref[...]
    key_cos, key_sin = key_tables(cosine, sine)
    for col in range(0, query_ref.shape[1], LANES):
        tile = rotate_tile(project[:, col : col + LANES], cosine, sine, 1.0)
        query_ref[:, col : col + LANES] = tile.astype(BF16)
    for col in range(0, kv_ref.shape[1], LANES):
        at = query_ref.shape[1] + col
        tile = rotate_tile(project[:, at : at + LANES], key_cos, key_sin, 1.0)
        kv_ref[:, col : col + LANES] = tile.astype(BF16)


def group_windows(before, own, group):
    col = group * 2 * HEAD_WIDTH
    return [
        jnp.concatenate([before[:, at : at + HEAD_WIDTH], own[:, at : at + HEAD_WIDTH]], axis=0)
        for at in (col, col + HEAD_WIDTH)
    ]


def stack_heads(block, group):
    at = group * QUERIES_PER_GROUP * HEAD_WIDTH
    return jnp.concatenate(
        [
            block[:, at + i * HEAD_WIDTH : at + (i + 1) * HEAD_WIDTH]
            for i in range(QUERIES_PER_GROUP)
        ],
        axis=0,
    )


def store_heads(ref, group, value_t):
    at = group * QUERIES_PER_GROUP * HEAD_WIDTH
    for i in range(QUERIES_PER_GROUP):
        part = value_t[:, i * SEGMAX : (i + 1) * SEGMAX].T
        ref[:, at + i * HEAD_WIDTH : at + (i + 1) * HEAD_WIDTH] = part.astype(ref.dtype)


def clear_spare(ref, groups):
    used = groups * QUERIES_PER_GROUP * HEAD_WIDTH
    if used < ref.shape[1]:
        ref[:, used:] = jnp.zeros((ref.shape[0], ref.shape[1] - used), ref.dtype)


def probs_of(keys, queries, bias):
    scores = dot_nt(keys, queries) * SCORE_SCALE
    scores = scores + jnp.concatenate([bias] * QUERIES_PER_GROUP, axis=1)
    top = jnp.max(scores, axis=0, keepdims=True)
    weights = jnp.exp(scores - top)
    total = jnp.sum(weights, axis=0, keepdims=True)
    return weights * (1.0 / total)


def attend_kernel(query_ref, own_ref, before_ref, bias_ref, mixed_ref):
    groups = own_ref.shape[1] // (2 * HEAD_WIDTH)
    query, own, before, bias = query_ref[...], own_ref[...], before_ref[...], bias_ref[...]
    clear_spare(mixed_ref, groups)
    for group in range(groups):
        keys, values = group_windows(before, own, group)
        probs = probs_of(keys, stack_heads(query, group), bias).astype(BF16)
        store_heads(mixed_ref, group, dot_nn(values.T, probs))


def attend_back_kernel(
    query_ref, own_ref, before_ref, bias_ref, first_ref, rest_ref, branch_ref, cos_ref, sin_ref,
    dquery_ref, down_ref, dbefore_ref, raw_ref, held_ref,
):
    groups = own_ref.shape[1] // (2 * HEAD_WIDTH)
    hold_weight(first_ref, rest_ref, held_ref)
    mixed_grad = dot_nn(branch_ref[...], held_ref[...]).astype(BF16)
    query, own, before, bias = query_ref[...], own_ref[...], before_ref[...], bias_ref[...]
    clear_spare(raw_ref, groups)
    for group in range(groups):
        keys, values = group_windows(before, own, group)
        queries, grads = stack_heads(query, group), stack_heads(mixed_grad, group)
        probs = probs_of(keys, queries, bias)
        prob_grad = dot_nt(values, grads)
        inner = jnp.sum(probs * prob_grad, axis=0, keepdims=True)
        score_grad = (SCORE_SCALE * probs * (prob_grad - inner)).astype(BF16)
        store_heads(raw_ref, group, dot_nn(keys.T, score_grad))
        col = group * 2 * HEAD_WIDTH
        for at, part in (
            (col, dot_nn(score_grad, queries)),
            (col + HEAD_WIDTH, dot_nn(probs.astype(BF16), grads)),
        ):
            dbefore_ref[:, at : at + HEAD_WIDTH] = part[:SEGMAX].astype(dbefore_ref.dtype)
            down_ref[:, at : at + HEAD_WIDTH] = part[SEGMAX:]
    cosine, sine = cos_ref[...], sin_ref[...]
    for col in range(0, query_ref.shape[1], LANES):
        tile = rotate_tile(raw_ref[:, col : col + LANES], cosine, sine, -1.0)
        dquery_ref[:, col : col + LANES] = tile.astype(BF16)


def branch_weights_kernel(experts, halves, normed_t_ref, *refs):
    branch_refs, refs = refs[:halves], refs[halves:]
    high_refs, low_refs, refs = refs[:halves], refs[halves : 2 * halves], refs[2 * halves :]
    *mixed_refs, term_ref, turned_ref, router_ref = refs
    block = pl.program_id(0)
    width = mixed_refs[0].shape[1]

    @pl.when(block == 0)
    def _():
        turned_ref[...] = jnp.concatenate([ref[...].T for ref in branch_refs], axis=1)
        high, low = (
            jnp.concatenate([ref[...] for ref in part], axis=0) for part in (high_refs, low_refs)
        )
        normed_t = normed_t_ref[...]
        router_ref[...] = dot_nn(normed_t, high) + dot_nn(normed_t, low)

    mixed = jnp.concatenate([ref[...] for ref in mixed_refs], axis=0)
    out_grad = dot_nn(turned_ref[...], mixed).astype(BF16)
    slices, depth, _ = term_ref.shape
    term_ref[:, :, :width] = out_grad.reshape(slices, depth, width)
    router = pltpu.roll(router_ref[...], (LANES - block * experts) % LANES, axis=1)
    term_ref[:, :, width:] = router.astype(BF16).reshape(slices, depth, LANES)


def branch_kernel(halves, *refs):
    mixed_refs = refs[:halves]
    first_ref, rest_ref, inputs_ref, gain_ref, middle_ref, *normed_refs = refs[halves:]
    width = first_ref.shape[-1]
    blocks = [first_ref[...].reshape(D, width)]
    blocks += [rest_ref[:, n].reshape(D, width) for n in range(rest_ref.shape[1])]
    weight = jnp.concatenate(blocks, axis=1)
    mixed = jnp.concatenate([ref[...] for ref in mixed_refs], axis=0)
    middle = inputs_ref[...].astype(F32) + dot_nt(mixed, weight)
    scale = lax.rsqrt(jnp.mean(middle * middle, axis=1, keepdims=True) + EPS)
    middle_ref[...] = middle
    normed = (middle * scale * gain_ref[...]).astype(BF16)
    for n, ref in enumerate(normed_refs):
        ref[...] = normed[n * CHUNK : (n + 1) * CHUNK]


def middle_back_kernel(
    own_ref, up_ref, down_ref, gates_ref, select_ref, router_ref, middle_ref, gain_ref, grad_ref,
    middle_grad_ref, branch_ref, high_ref, low_ref, gain_grad_ref,
):
    grad = own_ref[...].astype(F32) + up_ref[...].astype(F32) + down_ref[...].astype(F32)
    pairs = dot_nn(grad[:, D:].astype(BF16), select_ref[...])
    gates, router = gates_ref[...], router_ref[...]
    logit_grad = gates * (pairs - jnp.sum(gates * pairs, axis=1, keepdims=True))
    high = logit_grad.astype(BF16)
    low = (logit_grad - high.astype(F32)).astype(BF16)
    high_ref[...] = high
    low_ref[...] = low
    grad = grad[:, :D] + dot_nt(high, router) + dot_nt(low, router)
    back, gain_grad = norm_back(middle_ref[...], gain_ref[...], grad)
    middle_grad = grad_ref[...].astype(F32) + back
    middle_grad_ref[...] = middle_grad
    branch_ref[...] = middle_grad.astype(BF16)

    @pl.when(pl.program_id(0) == 0)
    def _():
        gain_grad_ref[...] = gain_grad

    @pl.when(pl.program_id(0) > 0)
    def _():
        gain_grad_ref[...] += gain_grad


def project_back_kernel(halves, *refs):
    dquery_refs, refs = refs[:halves], refs[halves:]
    own_refs, refs = refs[:halves], refs[halves:]
    next_refs, refs = refs[:halves], refs[halves:]
    (half_ref, normed_t_ref, first_ref, rest_ref, cos_ref, sin_ref, mine_ref, other_ref, total_ref,
     held_ref) = refs
    block = pl.program_id(0)
    key_cos, key_sin = key_tables(cos_ref[...], sin_ref[...])
    tiles = [jnp.concatenate([ref[...] for ref in dquery_refs], axis=0)]
    for col in range(0, own_refs[0].shape[1], LANES):
        cols = slice(col, col + LANES)
        tile = jnp.concatenate(
            [own[:, cols] + after_[:, cols].astype(F32) for own, after_ in zip(own_refs, next_refs)],
            axis=0,
        )
        tiles.append(rotate_tile(tile, key_cos, key_sin, -1.0).astype(BF16))
    grads = jnp.concatenate(tiles, axis=1)
    hold_weight(first_ref, rest_ref, held_ref)
    dweight = dot_nn(normed_t_ref[...], grads).astype(BF16)
    store_halves(half_ref, mine_ref, other_ref, slice(0, grads.shape[1]), dweight)
    part = dot_nt(grads, held_ref[...])

    @pl.when(block == 0)
    def _():
        total_ref[...] = part

    @pl.when(block > 0)
    def _():
        total_ref[...] += part


def input_back_kernel(
    inputs_ref, total_ref, gain_ref, middle_grad_ref, input_grad_ref, gain_grad_ref
):
    back, gain_grad = norm_back(inputs_ref[...].astype(F32), gain_ref[...], total_ref[...])
    input_grad_ref[...] = middle_grad_ref[...] + back

    @pl.when(pl.program_id(0) == 0)
    def _():
        gain_grad_ref[...] = gain_grad

    @pl.when(pl.program_id(0) > 0)
    def _():
        gain_grad_ref[...] += gain_grad


def joined_sum_kernel(groups, *refs):
    *part_refs, out_ref = refs
    rows = out_ref.shape[0]
    total = part_refs[0][...].astype(F32)
    for ref in part_refs[1:]:
        total = total + ref[:rows, :].astype(F32)
    queries = QUERIES_PER_GROUP * HEAD_WIDTH
    span = queries + 2 * HEAD_WIDTH
    width = total.shape[1] - groups * 2 * HEAD_WIDTH
    for group in range(groups):
        at = group * span
        out_ref[:, at : at + queries] = total[:, group * queries : (group + 1) * queries]
        col = width + group * 2 * HEAD_WIDTH
        out_ref[:, at + queries : at + span] = total[:, col : col + 2 * HEAD_WIDTH]


def norm_back(resid, gain, grad):
    scale = lax.rsqrt(jnp.mean(resid * resid, axis=1, keepdims=True) + EPS)
    gain_grad = jnp.sum(grad * resid * scale, axis=0, keepdims=True)
    scaled = grad * gain
    inner = jnp.sum(scaled * resid, axis=1, keepdims=True)
    return scale * scaled - resid * (scale * scale * scale * inner / D), gain_grad


def slots_kernel(experts, first_ref, ids_ref, rank_ref, pos_ref, ends_ref):
    length = ids_ref.shape[1]
    row = lax.broadcasted_iota(jnp.int32, (SUBLANES, length), 0)
    wanted = jnp.where(row < experts, row + first_ref[0], -1)
    rank = jnp.full((SUBLANES, length), 1 << 30, jnp.int32)
    for k in range(TOPK):
        rank = jnp.where(ids_ref[k : k + 1, :] == wanted, rank_ref[k : k + 1, :], rank)
    limit = jnp.zeros((SUBLANES, 1), jnp.int32)
    for bit in reversed(range((length * TOPK).bit_length())):
        higher = limit + (1 << bit)
        count = jnp.sum(jnp.where(rank < higher, 1.0, 0.0), axis=1, keepdims=True)
        limit = jnp.where(count <= CAP, higher, limit)
    kept = jnp.where(rank < limit, 1.0, 0.0)
    before = jnp.where(
        lax.broadcasted_iota(jnp.int32, (CHUNK, CHUNK), 0)
        < lax.broadcasted_iota(jnp.int32, (CHUNK, CHUNK), 1),
        1.0,
        0.0,
    ).astype(BF16)
    lane = lax.broadcasted_iota(jnp.int32, ends_ref.shape, 1)
    so_far = jnp.zeros((SUBLANES, 1), F32)
    ends = jnp.zeros(ends_ref.shape, F32)
    for n in range(length // CHUNK):
        part = kept[:, n * CHUNK : (n + 1) * CHUNK]
        place = dot_nn(part.astype(BF16), before) + so_far
        pos_ref[n] = jnp.where(part > 0.5, place, -1.0).astype(jnp.int32)
        so_far = so_far + jnp.sum(part, axis=1, keepdims=True)
        ends = jnp.where(lane == n + 1, so_far, ends)
    ends_ref[...] = ends.astype(jnp.int32)


def slot_windows(ends_ref, experts, chunk, window):
    firsts = [ends_ref[e, chunk] // SUBLANES * SUBLANES for e in range(experts)]
    ends = [ends_ref[e, chunk + 1] for e in range(experts)]
    count = jnp.int32(0)
    for first, end in zip(firsts, ends):
        count = jnp.maximum(count, (end - first + window - 1) // window)
    return firsts, ends, count


def window_start(first, n_window, window):
    return pl.multiple_of(jnp.minimum(first + n_window * window, SLOTS - window), SUBLANES)


def dispatch_kernel(with_gates, experts, size, *refs):
    shard_ref, ends_ref, *refs = refs
    if with_gates:
        *x_refs, pos_ref, router_ref, member_ref, out_ref, gate_ref, hot_ref, held_ref, sems = refs
    else:
        *x_refs, pos_ref, out_ref, hot_ref, held_ref, sems = refs
    window = hot_ref.shape[0] // experts
    span = 2 * size - 1
    parts = len(x_refs) // span
    part_rows = held_ref.shape[1] // parts

    def fetch(n, part, source):
        rows = pl.ds(part * part_rows, part_rows)
        return pltpu.make_async_copy(
            x_refs[part * span + source], held_ref.at[n, rows, :], sems.at[n, part]
        )

    for n in range(size):
        for part in range(parts):
            if n == 0:
                fetch(n, part, 0).start()
            else:
                below = shard_ref[0] >= n

                @pl.when(below)
                def _(n=n, part=part):
                    fetch(n, part, n).start()

                @pl.when(jnp.logical_not(below))
                def _(n=n, part=part):
                    fetch(n, part, span - n).start()

    out_ref[...] = jnp.zeros(out_ref.shape, BF16)
    if with_gates:
        gate_ref[...] = jnp.zeros(gate_ref.shape, F32)
    row = lax.broadcasted_iota(jnp.int32, (window, CHUNK), 0)
    halves = held_ref.shape[1] // CHUNK
    for n in range(size):
        for part in range(parts):
            fetch(n, part, 0).wait()
        for half in range(halves):
            chunk = shard_ref[n] * halves + half
            x = held_ref[n, half * CHUNK : (half + 1) * CHUNK, :]
            pos = pos_ref[chunk]
            firsts, ends, count = slot_windows(ends_ref, experts, chunk, window)
            if with_gates:
                logits = jnp.where(member_ref[chunk] > 0.5, dot_nn(x, router_ref[...]), MASKED)
                raised = jnp.exp(logits)
                gates = raised / jnp.sum(raised, axis=1, keepdims=True)
                lane = lax.broadcasted_iota(jnp.int32, gates.shape, 1)
                gates = jnp.where(lane < SUBLANES, gates, 0.0)
                high = gates.astype(BF16).astype(F32)
                gates = (high + pltpu.roll(gates - high, SUBLANES, axis=1)).astype(BF16)

            def body(n_window, _):
                for e in range(experts):
                    start = firsts[e] + n_window * window
                    at = window_start(firsts[e], n_window, window)
                    place = pos[e : e + 1, :]
                    place = jnp.where(place >= start, place - at, -1)
                    hot_ref[e * window : (e + 1) * window, :] = jnp.where(
                        row == place, 1.0, 0.0
                    ).astype(BF16)
                hot = hot_ref[...]
                rows = dot_nn(hot, x)
                if with_gates:
                    gate_rows = dot_nn(hot, gates)
                for e in range(experts):
                    start = firsts[e] + n_window * window
                    at = window_start(firsts[e], n_window, window)
                    part = slice(e * window, (e + 1) * window)

                    @pl.when(start < ends[e])
                    def _():
                        out_ref[e, pl.ds(at, window), :] += rows[part].astype(BF16)
                        if with_gates:
                            gate_ref[e, pl.ds(at, window), :] += gate_rows[part]

                return 0

            lax.fori_loop(0, count, body, 0)


def combine_kernel(with_pairs, sizes, order, *refs):
    piece_ref, ends_ref, place_ref, *refs = refs
    rows_refs, refs = refs[: len(sizes)], refs[len(sizes) :]
    if with_pairs:
        pair_refs, refs = refs[: len(sizes)], refs[len(sizes) :]
        *out_refs, held_ref, sems, hot_ref, total_ref, held_pair_ref, pair_total_ref = refs
    else:
        *out_refs, held_ref, sems, hot_ref, total_ref = refs
    experts = sum(sizes)
    count_out = len(out_refs)
    home = [(n, e) for n, size in enumerate(sizes) for e in range(size)]
    step, steps = pl.program_id(0), pl.num_programs(0)
    halves = steps // len(order)
    visits = steps // count_out

    def chunk_of(at_step):
        return piece_ref[at_step // halves] * halves + at_step % halves

    def copies(chunk, n_window, slot):
        firsts = slot_windows(ends_ref, experts, chunk, WINDOW)[0]
        return [
            pltpu.make_async_copy(
                rows_refs[n].at[own, pl.ds(window_start(firsts[e], n_window, WINDOW), WINDOW), :],
                held_ref.at[slot, pl.ds(e * WINDOW, WINDOW), :],
                sems.at[slot, e],
            )
            for e, (n, own) in enumerate(home)
        ]

    @pl.when(step == 0)
    def _():
        for copy in copies(chunk_of(step), 0, 0):
            copy.start()

    @pl.when(step + 1 < steps)
    def _():
        for copy in copies(chunk_of(step + 1), 0, (step + 1) % 2):
            copy.start()

    chunk = chunk_of(step)
    firsts, ends, count = slot_windows(ends_ref, experts, chunk, WINDOW)
    lane = lax.broadcasted_iota(jnp.int32, (CHUNK, WINDOW), 1)
    places = place_ref[...]

    def mark(n_window):
        for e, (n, own) in enumerate(home):
            start = firsts[e] + n_window * WINDOW
            at = window_start(firsts[e], n_window, WINDOW)
            place = places[:, e : e + 1]
            place = jnp.where(place >= start, place - at, -1)
            cols = slice(e * WINDOW, (e + 1) * WINDOW)
            hot_ref[:, cols] = jnp.where(lane == place, 1.0, 0.0).astype(BF16)
            if with_pairs:
                held_pair_ref[cols, :] = pair_refs[n][own, pl.ds(at, WINDOW), :]

    mark(0)
    for copy in copies(chunk, 0, step % 2):
        copy.wait()
    total_ref[...] = dot_nn(hot_ref[...], held_ref[step % 2])
    if with_pairs:
        pair_total_ref[...] = dot_nn(hot_ref[...], held_pair_ref[...])

    def body(n_window, _):
        more = copies(chunk, n_window, 2)
        for copy in more:
            copy.start()
        mark(n_window)
        for copy in more:
            copy.wait()
        total_ref[...] += dot_nn(hot_ref[...], held_ref[2])
        if with_pairs:
            pair_total_ref[...] += dot_nn(hot_ref[...], held_pair_ref[...])
        return 0

    lax.fori_loop(1, count, body, 0)
    for n, out_ref in enumerate(out_refs):

        @pl.when(step // visits == n)
        def _(n=n * visits // halves, out_ref=out_ref):
            out_ref[:, :D] = total_ref[...].astype(BF16)
            if with_pairs:
                place = -order[n] % len(order) * 2 * experts
                out_ref[:, D:] = pltpu.roll(pair_total_ref[...], place, axis=1).astype(BF16)


def expert_kernel(
    first, experts, half_ref, x_ref, grad_ref, gate_ref, weight_ref, y_ref, z_ref, pair_ref, *term_refs,
):
    e = first + pl.program_id(0)
    x, slot_grad = x_ref[0], grad_ref[0]
    w_in, w_out = weight_ref[0, :, : 2 * FF], weight_ref[0, :, 2 * FF :]
    lane = lax.broadcasted_iota(jnp.int32, gate_ref.shape[1:], 1)
    gate = jnp.sum(
        jnp.where((lane == e) | (lane == e + SUBLANES), gate_ref[0], 0.0), axis=1, keepdims=True
    )
    gate_up = dot_nn(x, w_in)
    gate_part, up_part = gate_up[:, :FF], gate_up[:, FF:]
    sigmoid = jax.nn.sigmoid(gate_part)
    silu = gate_part * sigmoid
    hidden = (silu * up_part).astype(BF16)
    raw = dot_nn(slot_grad, w_out)
    pair = jnp.sum(hidden.astype(F32) * raw, axis=1, keepdims=True)
    high = pair.astype(BF16).astype(F32)
    pair_ref[0] = jnp.where(
        lane == e, high, jnp.where(lane == e + experts, pair - high, 0.0)
    ).astype(BF16)
    hidden_grad = gate * raw
    gate_up_grad = jnp.concatenate(
        [
            (hidden_grad * up_part * sigmoid * (1.0 + gate_part * (1.0 - sigmoid))).astype(BF16),
            (hidden_grad * silu).astype(BF16),
        ],
        axis=1,
    )
    z_ref[0] = dot_nt(gate_up_grad, w_in).astype(BF16)
    y_ref[0] = (gate * dot_nt(hidden, w_out)).astype(BF16)
    rows_grad = (gate * slot_grad.astype(F32)).astype(BF16)
    in_term = dot_tn(x, gate_up_grad).astype(BF16)
    out_term = dot_tn(rows_grad, hidden).astype(BF16)
    if len(term_refs) == 2:
        store_halves(half_ref, *term_refs, slice(0, 2 * FF), in_term)
        store_halves(half_ref, *term_refs, slice(2 * FF, 3 * FF), out_term)
    else:
        term_ref = term_refs[0]
        slices, depth, _ = term_ref.shape
        term_ref[:, :, : 2 * FF] = in_term.reshape(slices, depth, 2 * FF)
        term_ref[:, :, 2 * FF :] = out_term.reshape(slices, depth, FF)


def after(value, *others):
    return lax.optimization_barrier((value,) + others)[0]


def pair_scatter(mine, other, size, *gates):
    taken = after(lax.ppermute(other, "gx", [(s, s ^ 1) for s in range(size)]), *gates)
    mine = (mine.astype(F32) + taken.astype(F32)).astype(mine.dtype)
    groups = [list(range(0, size, 2)), list(range(1, size, 2))]
    total = lax.psum_scatter(mine, "gx", scatter_dimension=0, tiled=True, axis_index_groups=groups)
    return lax.optimization_barrier(total)[0]


def direct_gather(part, size):
    return jnp.stack(
        [
            lax.ppermute(part, "gy", [(s, (s + k) % size) for s in range(size)])
            for k in range(1, size)
        ]
    )


def gather_step(pair, step, size, *gates):
    up, down = (after(part, *gates) if gates else part for part in pair)
    return (
        lax.ppermute(up, "gy", [(s, s + 1) for s in range(step, size - 1)]),
        lax.ppermute(down, "gy", [(s + 1, s) for s in range(0, size - 1 - step)]),
    )


def sum_added(parts, pair, step, size, *gates):
    above, below = parts[step], parts[size - step]
    if gates:
        pair = tuple(after(part, *gates) for part in pair)
    if pair is not None:
        above, below = (
            (a.astype(F32) + b.astype(F32)).astype(a.dtype)
            for a, b in zip((above, below), pair)
        )
    return above, below


def sum_sent(added, step, size):
    above, below = added
    return (
        lax.ppermute(above, "gy", [(s, s + 1) for s in range(step)]),
        lax.ppermute(below, "gy", [(size - 1 - s, size - 2 - s) for s in range(step)]),
    )


def sum_step(parts, pair, step, size, *gates):
    return sum_sent(sum_added(parts, pair, step, size, *gates), step, size)


def sum_steps_of(parts, size, gates):
    steps, pair = [], None
    for step in range(1, size):
        pair = sum_step(parts, pair, step, size, *gates.get(step, ()))
        steps.append(pair)
    return steps


def direct_sum(parts, size, *gates):
    taken = [
        lax.ppermute(parts[k], "gy", [(s, (s - k) % size) for s in range(size)])
        for k in range(1, size)
    ]
    total = parts[0].astype(F32)
    for part in taken:
        total = total + after(part, *gates).astype(F32)
    return total


def summed(parts, steps):
    return parts[0].astype(F32) + steps[-1][0].astype(F32) + steps[-1][1].astype(F32)


def shards(
    nx,
    ny,
    tokens,
    attn_gain,
    query_key_value_weight,
    out_weight,
    moe_gain,
    router_weight,
    expert_in,
    expert_out,
    expert_ids,
    route_order,
    segment_ids,
    out_grad,
):
    rows = tokens.shape[0]
    length = segment_ids.shape[1]
    depth = out_weight.shape[1]
    heads_width = out_weight.shape[0]
    groups = heads_width // (HEAD_WIDTH * QUERIES_PER_GROUP)
    spare = -heads_width % LANES
    width = heads_width + spare
    kv_width = groups * 2 * HEAD_WIDTH
    joined = width + kv_width
    experts = router_weight.shape[0]
    all_experts = experts * ny
    chunks = length // CHUNK
    own_chunks = rows // CHUNK
    me = lax.axis_index("gy")
    first_expert = me * experts
    first_row = me * rows
    both = ("gx", "gy")

    pos, ends = pl.pallas_call(
        functools.partial(slots_kernel, experts),
        in_specs=[
            pl.BlockSpec(memory_space=pltpu.SMEM),
            pl.BlockSpec(memory_space=pltpu.VMEM),
            pl.BlockSpec(memory_space=pltpu.VMEM),
        ],
        out_shape=[
            jax.ShapeDtypeStruct((chunks, SUBLANES, CHUNK), jnp.int32),
            jax.ShapeDtypeStruct((SUBLANES, LANES), jnp.int32),
        ],
        compiler_params=params(),
        cost_estimate=cost(3),
        name="slots",
    )(
        first_expert.reshape(1),
        expert_ids.T,
        route_order[0].reshape(length, TOPK).T,
    )
    places = jnp.pad(
        pos.transpose(0, 2, 1).reshape(length, SUBLANES), ((0, 0), (0, LANES - SUBLANES))
    )
    ends = ends[:, : chunks + 1]
    pieces = (me - jnp.arange(ny, dtype=jnp.int32)) % ny
    lane_expert = jnp.arange(LANES, dtype=jnp.int32)
    turned_expert = (me - lane_expert // experts) % ny * experts + lane_expert % experts
    turned_expert = jnp.where(lane_expert < all_experts, turned_expert, -1)
    members = jnp.any(expert_ids[:, :, None] == turned_expert[None, None, :], axis=1)
    members = members.astype(F32).reshape(chunks, CHUNK, LANES)
    own_ids = lax.dynamic_slice_in_dim(expert_ids, first_row, rows, 0)
    own_members = jnp.any(own_ids[:, :, None] == turned_expert[None, None, :], axis=1).astype(F32)

    inputs = tokens.astype(F32)
    scale_one = lax.rsqrt(jnp.mean(inputs * inputs, axis=1, keepdims=True) + EPS)
    normed_one = (inputs * scale_one * attn_gain[None, :]).astype(BF16)
    normed_one_t = normed_one.T
    cosine, sine = rope_tiles(first_row, rows)
    labels = jnp.concatenate([jnp.full((SEGMAX,), -1, jnp.int32), segment_ids[0]])
    labels = lax.dynamic_slice_in_dim(labels, first_row, rows + SEGMAX, 0)
    position = jnp.arange(rows + SEGMAX, dtype=jnp.int32)
    bias = jnp.stack(
        [
            jnp.where(
                (labels[s : s + 2 * SEGMAX, None] == labels[None, s + SEGMAX : s + 2 * SEGMAX])
                & (
                    position[s : s + 2 * SEGMAX, None]
                    <= position[None, s + SEGMAX : s + 2 * SEGMAX]
                ),
                0.0,
                MASKED,
            ).astype(F32)
            for s in range(0, rows, SEGMAX)
        ]
    )
    grouped = query_key_value_weight.reshape(depth, groups, QUERIES_PER_GROUP + 2, HEAD_WIDTH)
    own_joined = jnp.concatenate(
        [
            jnp.pad(
                grouped[:, :, :QUERIES_PER_GROUP].reshape(depth, heads_width), ((0, 0), (0, spare))
            ),
            grouped[:, :, QUERIES_PER_GROUP:].reshape(depth, kv_width),
        ],
        axis=1,
    )
    own_out = jnp.pad(out_weight.T, ((0, 0), (0, spare)))
    own_router = jnp.pad(router_weight.T, ((0, 0), (0, LANES - experts)))
    gap = -(joined + LANES) % width
    own_weights = jnp.concatenate(
        [own_joined, own_router, jnp.zeros((depth, gap), BF16), own_out], axis=1
    )
    own_second = jnp.concatenate([own_out, own_router], axis=1)
    cut = experts * 2 // 5
    bounds = ((0, cut), (cut, experts))
    own_experts = [
        jnp.concatenate([expert_in[lo:hi], expert_out[lo:hi]], axis=2) for lo, hi in bounds
    ]
    first_weights = lax.all_gather(own_weights, "gx", axis=0)
    line_joined = after(direct_gather(own_joined, ny), *own_experts)
    own_second = after(own_second, line_joined)
    line_second = direct_gather(own_second, ny)
    ready = after(out_grad, line_second, bias, cosine, sine, normed_one)
    grad_steps = [gather_step((ready, ready), 0, ny)]
    rest_joined = lax.all_gather(line_joined, "gx", axis=0)
    rest_second = lax.all_gather(line_second, "gx", axis=0)
    wide = []
    for own in own_experts:
        wide.append(lax.all_gather(own, "gx", axis=1, tiled=True))


    out_column = (joined + LANES + gap) // width
    rest_block = lambda b: (0, jnp.maximum(b - 1, 0), 0, 0)
    joined_specs = [
        pl.BlockSpec((nx, depth, joined), lambda b: (0, 0, 0)),
        pl.BlockSpec((nx, pl.Squeezed(), depth, joined), rest_block),
    ]
    out_specs = [
        pl.BlockSpec((nx, depth, width), lambda b: (0, 0, out_column)),
        pl.BlockSpec((nx, pl.Squeezed(), depth, width), rest_block),
    ]
    held_joined = pltpu.VMEM((D, joined), BF16)
    held_out = pltpu.VMEM((D, width), BF16)
    query, kv = pl.pallas_call(
        project_kernel,
        grid=(ny,),
        in_specs=[
            whole((rows, D)),
            *joined_specs,
            whole((rows, LANES)),
            whole((rows, LANES)),
        ],
        out_specs=[
            pl.BlockSpec((rows, width), lambda b: (0, b)),
            pl.BlockSpec((rows, kv_width), lambda b: (0, b)),
        ],
        out_shape=[
            jax.ShapeDtypeStruct((rows, ny * width), BF16),
            jax.ShapeDtypeStruct((rows, ny * kv_width), BF16),
        ],
        scratch_shapes=[held_joined],
        compiler_params=params(),
        cost_estimate=cost(10),
        name="project",
    )(after(normed_one, bias), first_weights, rest_joined, cosine, sine)
    halo = lax.ppermute(kv[rows - SEGMAX :], "gy", [(s, s + 1) for s in range(ny - 1)])
    halves = rows // SEGMAX
    half_rows = lambda n, w: pl.BlockSpec((SEGMAX, w), lambda b: (n, b))
    whole_half = lambda n, w: pl.BlockSpec((SEGMAX, w), lambda b: (n, 0))
    below_rows = pl.BlockSpec((SEGMAX, kv_width), lambda b: (0, (b + ny - 1) % ny))
    bias_half = lambda n: pl.BlockSpec((pl.Squeezed(), 2 * SEGMAX, SEGMAX), lambda b: (n, 0, 0))

    def window(n):
        if n == 0:
            return [half_rows(0, kv_width), below_rows], (kv, halo)
        return [half_rows(n, kv_width), half_rows(n - 1, kv_width)], (kv, kv)

    mixed = [None] * halves
    for n in reversed(range(halves)):
        specs, arrays = window(n)
        mixed[n] = pl.pallas_call(
            attend_kernel,
            grid=(ny,),
            in_specs=[half_rows(n, width), *specs, bias_half(n)],
            out_specs=half_rows(0, width),
            out_shape=jax.ShapeDtypeStruct((SEGMAX, ny * width), BF16),
            compiler_params=params(),
            cost_estimate=cost(8),
            name="attend",
        )(query, *arrays, bias)
    for step in range(1, ny - 2):
        grad_steps.append(gather_step(grad_steps[-1], step, ny, mixed[-1]))
    middle, *normed_chunks = pl.pallas_call(
        functools.partial(branch_kernel, halves),
        grid=(1,),
        in_specs=[whole((SEGMAX, ny * width))] * halves
        + [
            out_specs[0],
            pl.BlockSpec((nx, ny - 1, depth, width), lambda _: (0, 0, 0, 0)),
            whole((rows, D)),
            whole((1, D)),
        ],
        out_specs=[whole((rows, D))] + [whole((CHUNK, D))] * own_chunks,
        out_shape=[jax.ShapeDtypeStruct((rows, D), F32)]
        + [jax.ShapeDtypeStruct((CHUNK, D), BF16)] * own_chunks,
        compiler_params=params(),
        cost_estimate=cost(7),
        name="branch",
    )(*mixed, first_weights, rest_second, tokens, moe_gain[None, :])

    router = jnp.concatenate(
        [
            first_weights[:, None, :, joined : joined + experts],
            rest_second[:, :, :, width : width + experts],
        ],
        axis=1,
    )
    router = router.transpose(0, 2, 1, 3).reshape(D, all_experts)
    router = jnp.pad(router, ((0, 0), (0, LANES - all_experts)))
    normed_two = jnp.concatenate(normed_chunks, axis=0)
    normed_steps = []
    for part in normed_chunks:
        part = after(part, grad_steps[-1])
        normed_steps.append([(part, part)])
    for step in range(ny - 1):
        for steps in normed_steps:
            steps.append(gather_step(steps[-1], step, ny))
    grad_steps.append(
        gather_step(grad_steps[-1], ny - 2, ny, *[steps[-1] for steps in normed_steps])
    )
    normed_pieces = []
    for part, steps in zip(normed_chunks, normed_steps):
        normed_pieces += [part] + [up for up, _ in steps[1:]] + [down for _, down in steps[1:]]
    grad_pieces = [out_grad] + [up for up, _ in grad_steps] + [down for _, down in grad_steps]
    smem = pl.BlockSpec(memory_space=pltpu.SMEM)
    vmem = pl.BlockSpec(memory_space=pltpu.VMEM)
    slot_rows = jax.ShapeDtypeStruct((experts, SLOTS, D), BF16)
    slot_lanes = lambda kind: jax.ShapeDtypeStruct((experts, SLOTS, LANES), kind)
    dispatch_scratch = lambda parts: [
        pltpu.VMEM((experts * SHORT_WINDOW, CHUNK), BF16),
        pltpu.VMEM((ny, rows, D), BF16),
        pltpu.SemaphoreType.DMA((ny, parts)),
    ]
    hbm = pl.BlockSpec(memory_space=pl.ANY)
    slot_grads = pl.pallas_call(
        functools.partial(dispatch_kernel, False, experts, ny),
        in_specs=[smem, smem] + [hbm] * (2 * ny - 1) + [vmem],
        out_specs=vmem,
        out_shape=slot_rows,
        scratch_shapes=dispatch_scratch(1),
        compiler_params=params(),
        cost_estimate=cost(26),
        name="dispatch_grads",
    )(pieces, ends, *grad_pieces, pos)
    dispatched, slot_gates = pl.pallas_call(
        functools.partial(dispatch_kernel, True, experts, ny),
        in_specs=[smem, smem] + [hbm] * len(normed_pieces) + [vmem] * 3,
        out_specs=[vmem, vmem],
        out_shape=[slot_rows, slot_lanes(F32)],
        scratch_shapes=dispatch_scratch(own_chunks),
        compiler_params=params(),
        cost_estimate=cost(31),
        name="dispatch_rows",
    )(pieces, ends, *normed_pieces, pos, router, members)

    half = (lax.axis_index("gx") % 2).reshape(1)
    y_rows, z_rows, slot_pairs, weight_terms = [], [], [], []
    for n, (lo, hi) in enumerate(bounds):
        outer = lambda *shape: pl.BlockSpec((1,) + shape, lambda e, lo=lo: (lo + e, 0, 0))
        inner = lambda *shape: pl.BlockSpec((1,) + shape, lambda e: (e, 0, 0))
        parts = n + 1
        slices = pl.BlockSpec((nx // parts, pl.Squeezed(), depth, 3 * FF), lambda e: (0, e, 0, 0))
        y, z, pair, *terms = pl.pallas_call(
            functools.partial(expert_kernel, lo, experts),
            grid=(hi - lo,),
            in_specs=[
                smem,
                outer(SLOTS, D),
                outer(SLOTS, D),
                outer(SLOTS, LANES),
                inner(D, 3 * FF),
            ],
            out_specs=[inner(SLOTS, D), inner(SLOTS, D), inner(SLOTS, LANES)]
            + [slices] * parts,
            out_shape=[
                jax.ShapeDtypeStruct((hi - lo, SLOTS, D), BF16),
                jax.ShapeDtypeStruct((hi - lo, SLOTS, D), BF16),
                jax.ShapeDtypeStruct((hi - lo, SLOTS, LANES), BF16),
            ]
            + [jax.ShapeDtypeStruct((nx // parts, hi - lo, depth, 3 * FF), BF16)] * parts,
            compiler_params=params(),
            cost_estimate=cost(9 * (hi - lo)),
            name="experts",
        )(half, dispatched, slot_grads, slot_gates, wide[n])
        y_rows.append(y)
        z_rows.append(z)
        slot_pairs.append(pair)
        weight_terms.append(terms)
    def combine(rows_in, which, pairs=None):
        held = pltpu.VMEM((3, experts * WINDOW, D), BF16)
        sems = pltpu.SemaphoreType.DMA((3, experts))
        hot_t = pltpu.VMEM((CHUNK, experts * WINDOW), BF16)
        total = pltpu.VMEM((CHUNK, D), F32)
        more = pairs is not None
        columns = D + LANES * more
        halves = chunks // ny
        here = pieces[jnp.array(which)]

        def place_map(c, piece_ref):
            return (piece_ref[c // halves] * halves + c % halves, 0)

        visits = 1 if more else halves

        def out_map(n):
            return lambda c, piece_ref: (jnp.clip(c - n * visits, 0, visits - 1), 0)

        return pl.pallas_call(
            functools.partial(combine_kernel, more, tuple(hi - lo for lo, hi in bounds), which),
            grid_spec=pltpu.PrefetchScalarGridSpec(
                num_scalar_prefetch=1,
                grid=(halves * len(which),),
                in_specs=[smem, pl.BlockSpec((CHUNK, LANES), place_map)]
                + [hbm] * len(bounds)
                + [once((hi - lo, SLOTS, LANES)) for lo, hi in bounds] * more,
                out_specs=[
                    pl.BlockSpec((CHUNK, columns), out_map(n))
                    for n in range(len(which) * halves // visits)
                ],
                scratch_shapes=[held, sems, hot_t, total]
                + [
                    pltpu.VMEM((experts * WINDOW, LANES), BF16),
                    pltpu.VMEM((CHUNK, LANES), F32),
                ]
                * more,
            ),
            out_shape=[jax.ShapeDtypeStruct((CHUNK * visits, columns), BF16)]
            * (len(which) * halves // visits),
            compiler_params=params(),
            cost_estimate=cost(16),
            name="combine_grads" if more else "combine_rows",
        )(here, ends, places, *rows_in, *(pairs if more else []))

    outer_pieces = sorted({1, ny - 1})
    inner_pieces = [k for k in range(ny) if k not in outer_pieces]
    order = outer_pieces + inner_pieces
    token_sum = combine(z_rows, order, slot_pairs)
    token_sum = [
        [token_sum[order.index(k) * own_chunks + n] for k in range(ny)] for n in range(own_chunks)
    ]
    token_steps = [[] for _ in token_sum]
    for step in range(1, ny):
        for parts, steps in zip(token_sum, token_steps):
            steps.append(sum_step(parts, steps[-1] if steps else None, step, ny))
    own_logits = jnp.where(own_members > 0.5, dot_nn(normed_two, router), MASKED)
    own_raised = jnp.exp(own_logits)
    own_gates = own_raised / jnp.sum(own_raised, axis=1, keepdims=True)
    source = lane_expert // (2 * experts) * experts + lane_expert % experts
    source = jnp.where(lane_expert < 2 * all_experts, source, -1)
    select = (source[:, None] == lane_expert[None, :]).astype(BF16)
    weight_sums = [
        lax.psum_scatter(weight_terms[0][0], "gx", scatter_dimension=0, tiled=True)[0],
        pair_scatter(*weight_terms[1], nx, token_sum[0][0]),
    ]
    combined = combine([after(y, [steps[-2] for steps in token_steps]) for y in y_rows], order)
    combined = [combined[order.index(k)] for k in range(ny)]
    row_block = lambda w: pl.BlockSpec((LANES, w), lambda r: (r, 0))
    later_block = lambda n, w: pl.BlockSpec((LANES, w), lambda r: (r + n * CHUNK // LANES, 0))
    backs = []
    for n, (parts, steps) in enumerate(zip(token_sum, token_steps)):
        backs.append(
            pl.pallas_call(
                middle_back_kernel,
                grid=(CHUNK // LANES,),
                in_specs=[row_block(D + LANES)] * 3
                + [later_block(n, LANES), whole((LANES, LANES)), whole((D, LANES))]
                + [later_block(n, D), whole((1, D)), later_block(n, D)],
                out_specs=[row_block(D), row_block(D), row_block(LANES), row_block(LANES)]
                + [whole((1, D))],
                out_shape=[
                    jax.ShapeDtypeStruct((CHUNK, D), F32),
                    jax.ShapeDtypeStruct((CHUNK, D), BF16),
                    jax.ShapeDtypeStruct((CHUNK, LANES), BF16),
                    jax.ShapeDtypeStruct((CHUNK, LANES), BF16),
                    jax.ShapeDtypeStruct((1, D), F32),
                ],
                compiler_params=params(),
                cost_estimate=cost(4),
                name="middle_back",
            )(after(parts[0], *combined), *steps[-1], own_gates, select, router, middle,
              moe_gain[None, :], out_grad)
        )
    middle_grads, branch_grads, highs, lows, moe_gain_grads = zip(*backs)
    moe_gain_grad = sum(moe_gain_grads)

    combined_steps = [sum_step(combined, None, 1, ny)]

    dquery, dkv, dbefore = [], [], []
    for n in range(halves):
        specs, arrays = window(n)
        outs = pl.pallas_call(
            attend_back_kernel,
            grid=(ny,),
            in_specs=[
                half_rows(n, width),
                *specs,
                bias_half(n),
                *out_specs,
                whole((SEGMAX, D)),
                whole_half(n, LANES),
                whole_half(n, LANES),
            ],
            out_specs=[half_rows(0, width), half_rows(0, kv_width), half_rows(0, kv_width)],
            out_shape=[
                jax.ShapeDtypeStruct((SEGMAX, ny * width), BF16),
                jax.ShapeDtypeStruct((SEGMAX, ny * kv_width), F32),
                jax.ShapeDtypeStruct((SEGMAX, ny * kv_width), F32 if n else BF16),
            ],
            scratch_shapes=[pltpu.VMEM((SEGMAX, width), F32), held_out],
            compiler_params=params(),
            cost_estimate=cost(17),
            name="attend_back",
        )(query, *arrays, bias, first_weights, rest_second, after(branch_grads[n], *combined, *dbefore),
          cosine, sine)
        for kept, out in zip((dquery, dkv, dbefore), outs):
            kept.append(out)
    halo_grad = lax.ppermute(dbefore[0], "gy", [(s + 1, s) for s in range(ny - 1)])
    second_term = pl.pallas_call(
        functools.partial(branch_weights_kernel, experts, halves),
        grid=(ny,),
        in_specs=[whole((D, rows))]
        + [whole((CHUNK, D))] * halves
        + [whole((CHUNK, LANES))] * (2 * halves)
        + [half_rows(0, width)] * halves,
        out_specs=pl.BlockSpec((nx, pl.Squeezed(), depth, width + LANES), lambda b: (0, b, 0, 0)),
        out_shape=jax.ShapeDtypeStruct((nx, ny, depth, width + LANES), BF16),
        scratch_shapes=[pltpu.VMEM((D, rows), BF16), pltpu.VMEM((D, LANES), F32)],
        compiler_params=params(),
        cost_estimate=cost(9),
        name="branch_weights",
    )(normed_two.T, *branch_grads, *highs, *lows, *mixed)
    added = ()
    for step in range(2, ny):
        gates = (halo_grad,) if step == 2 else ()
        added = sum_added(combined, combined_steps[-1], step, ny, *gates)
        combined_steps.append(sum_sent(added, step, ny))
    next_rows = pl.BlockSpec((SEGMAX, kv_width), lambda b: (0, (b + 1) % ny))
    *joined_terms, normed_one_grad = pl.pallas_call(
        functools.partial(project_back_kernel, halves),
        grid=(ny,),
        in_specs=[half_rows(0, width)] * halves
        + [half_rows(0, kv_width)] * (2 * halves - 1)
        + [
            next_rows,
            smem,
            whole((D, rows)),
            *joined_specs,
            whole((rows, LANES)),
            whole((rows, LANES)),
        ],
        out_specs=[pl.BlockSpec((nx // 2, pl.Squeezed(), depth, joined), lambda b: (0, b, 0, 0))] * 2
        + [whole((rows, D))],
        out_shape=[jax.ShapeDtypeStruct((nx // 2, ny, depth, joined), BF16)] * 2
        + [jax.ShapeDtypeStruct((rows, D), F32)],
        scratch_shapes=[held_joined],
        compiler_params=params(),
        cost_estimate=cost(22),
        name="project_back",
    )(*dquery, *dkv, *dbefore[1:], halo_grad, half, normed_one_t, first_weights, rest_joined, cosine,
      sine)
    in_grad, down_grad = [], []
    for part in after(tuple(weight_sums), joined_terms):
        in_grad.append(part[..., : 2 * FF].astype(F32))
        down_grad.append(part[..., 2 * FF :].astype(F32))
    in_grad, down_grad = jnp.concatenate(in_grad), jnp.concatenate(down_grad)
    last = tuple(after(part, in_grad, down_grad) for part in combined_steps[-1])
    layer_out = (middle + summed(combined, [last])).astype(BF16)
    input_grad, attn_gain_grad = pl.pallas_call(
        input_back_kernel,
        grid=(rows // LANES,),
        in_specs=[row_block(D), row_block(D), whole((1, D)), row_block(D)],
        out_specs=[row_block(D), whole((1, D))],
        out_shape=[
            jax.ShapeDtypeStruct((rows, D), F32),
            jax.ShapeDtypeStruct((1, D), F32),
        ],
        compiler_params=params(),
        cost_estimate=cost(6),
        name="input_back",
    )(tokens, normed_one_grad, attn_gain[None, :], after(jnp.concatenate(middle_grads), layer_out))

    second_sum = lax.psum_scatter(
        after(second_term, weight_sums[0]), "gx", scatter_dimension=0, tiled=True
    )
    second_sum = lax.optimization_barrier(second_sum)[0]
    mine, other = joined_terms
    other = after(other, combined_steps[1])
    joined_sum = pair_scatter(mine, other, nx, second_sum, *added, *weight_sums)
    gain_sums = jnp.concatenate([attn_gain_grad, moe_gain_grad])
    bit = 1
    while bit < nx:
        pairs = [(s, s ^ bit) for s in range(nx)]
        gain_sums = gain_sums + lax.ppermute(gain_sums, "gx", pairs)
        bit = 2 * bit
    high = gain_sums.astype(BF16)
    low = (gain_sums - high.astype(F32)).astype(BF16)
    gains = jnp.stack([high, low]).reshape(-1)
    gain_rows = -(-gains.shape[0] // joined)
    gain_rows += -gain_rows % SUBLANES
    gains = jnp.pad(gains, (0, gain_rows * joined - gains.shape[0])).reshape(gain_rows, joined)
    joined_sum = after(joined_sum, gains)
    joined_parts, gain_parts = [joined_sum[0]], [gains]
    for k in range(1, ny):
        part = jnp.concatenate([joined_sum[k], gains], axis=0)
        part = lax.ppermute(part, "gy", [(s, (s - k) % ny) for s in range(ny)])
        joined_parts.append(part)
        gain_parts.append(part[depth:])
    second_sum = direct_sum(second_sum, ny, *joined_parts[1:])
    out_weight_grad = second_sum[:, :heads_width].T
    router_grad = second_sum[:, width : width + experts].T
    qkv_grad = pl.pallas_call(
        functools.partial(joined_sum_kernel, groups),
        out_shape=jax.ShapeDtypeStruct(query_key_value_weight.shape, F32),
        compiler_params=params(),
        cost_estimate=cost(2),
        name="joined_sum",
    )(*joined_parts)
    gain_sums = jnp.roll(jnp.stack(gain_parts), me, axis=0).astype(F32)
    gain_sums = gain_sums.reshape(ny, -1)[:, : 4 * D].reshape(ny, 2, 2, D)
    gain_sums = jnp.sum(gain_sums, axis=(0, 1))
    return (
        layer_out,
        input_grad,
        gain_sums[0],
        qkv_grad,
        out_weight_grad,
        gain_sums[1],
        router_grad,
        in_grad,
        down_grad,
    )


def solution(mesh):
    in_specs = (
        P(("gx", "gy"), None),
        P(),
        P("gx", "gy"),
        P("gy", "gx"),
        P(),
        P("gy", "gx"),
        P("gy", "gx", None),
        P("gy", "gx", None),
        P("gx", None),
        P("gx", None),
        P("gx", None),
        P(("gx", "gy"), None),
    )
    out_specs = (
        P(("gx", "gy"), None),
        P(("gx", "gy"), None),
        P(),
        P("gx", "gy"),
        P("gy", "gx"),
        P(),
        P("gy", "gx"),
        P("gy", "gx", None),
        P("gy", "gx", None),
    )
    body = functools.partial(shards, mesh.shape["gx"], mesh.shape["gy"])
    return jax.shard_map(body, mesh=mesh, in_specs=in_specs, out_specs=out_specs, check_vma=False)
```

```python
import functools

import jax
import jax.numpy as jnp
from jax import lax
from jax.experimental import pallas as pl
from jax.experimental.pallas import tpu as pltpu
from jax.sharding import PartitionSpec as P

D = 1536
HEAD_WIDTH = 64
FF = 512
TOPK = 8
SEGMAX = 256
QUERIES_PER_GROUP = 3
CAP = 460
SLOTS = 464
WINDOW = 128
SHORT_WINDOW = 96
CHUNK = 256
LANES = 128
SUBLANES = 16

EPS = 1e-05
MASKED = -1e30
SCORE_SCALE = HEAD_WIDTH ** (-0.5)
VMEM_BYTES = 60 * 1024 * 1024
F32 = jnp.float32
BF16 = jnp.bfloat16


def dot_nn(a, b):
    return lax.dot_general(a, b, (((1,), (0,)), ((), ())), preferred_element_type=F32)


def dot_nt(a, b):
    return lax.dot_general(a, b, (((1,), (1,)), ((), ())), preferred_element_type=F32)


def dot_tn(a, b):
    return lax.dot_general(a, b, (((0,), (0,)), ((), ())), preferred_element_type=F32)


def params(**more):
    return pltpu.CompilerParams(vmem_limit_bytes=VMEM_BYTES, **more)


def cost(micros):
    return pl.CostEstimate(
        flops=int(micros * 1.1e9), bytes_accessed=int(micros * 3.6e6), transcendentals=0
    )


def store_halves(half_ref, mine_ref, other_ref, columns, value):
    slices, depth, _ = mine_ref.shape
    for parity in range(2):
        own = half_ref[0] == parity
        for ref, taken in ((mine_ref, own), (other_ref, jnp.logical_not(own))):

            @pl.when(taken)
            def _(ref=ref, parity=parity):
                for n in range(slices):
                    at = (2 * n + parity) * depth
                    ref[n, :, columns] = value[at : at + depth]


def whole(shape):
    return pl.BlockSpec(shape, lambda *_: (0,) * len(shape))


def once(shape):
    return pl.BlockSpec(shape, lambda *_: (0,) * len(shape), pipeline_mode=pl.Buffered(1))


def rope_tiles(first_row, rows):
    half = HEAD_WIDTH // 2
    freq = jnp.exp(jnp.arange(half, dtype=F32) * (-2.0 * jnp.log(10000.0) / HEAD_WIDTH))
    position = (first_row + jnp.arange(rows, dtype=jnp.int32)).astype(F32)
    angle = position[:, None] * freq[None, :]
    cosine, sine = jnp.cos(angle), jnp.sin(angle)
    return (
        jnp.concatenate([cosine] * 4, axis=1),
        jnp.concatenate([-sine, sine, -sine, sine], axis=1),
    )


def swap_halves(tile):
    lane = lax.broadcasted_iota(jnp.int32, tile.shape, 1)
    half = HEAD_WIDTH // 2
    return jnp.where(
        lane % HEAD_WIDTH < half,
        pltpu.roll(tile, LANES - half, axis=1),
        pltpu.roll(tile, half, axis=1),
    )


def rotate_tile(tile, cosine, sine, sign):
    return tile * cosine + sign * swap_halves(tile) * sine


def key_tables(cosine, sine):
    lane = lax.broadcasted_iota(jnp.int32, cosine.shape, 1)
    is_key = lane < HEAD_WIDTH
    return jnp.where(is_key, cosine, 1.0), jnp.where(is_key, sine, 0.0)


def hold_weight(first_ref, rest_ref, held_ref):
    @pl.when(pl.program_id(0) == 0)
    def _():
        held_ref[...] = first_ref[...].reshape(held_ref.shape)

    @pl.when(pl.program_id(0) > 0)
    def _():
        held_ref[...] = rest_ref[...].reshape(held_ref.shape)


def project_kernel(
    normed_ref, first_ref, rest_ref, cos_ref, sin_ref, query_ref, kv_ref, held_ref
):
    hold_weight(first_ref, rest_ref, held_ref)
    project = dot_nn(normed_ref[...], held_ref[...])
    cosine, sine = cos_ref[...], sin_ref[...]
    key_cos, key_sin = key_tables(cosine, sine)
    for col in range(0, query_ref.shape[1], LANES):
        tile = rotate_tile(project[:, col : col + LANES], cosine, sine, 1.0)
        query_ref[:, col : col + LANES] = tile.astype(BF16)
    for col in range(0, kv_ref.shape[1], LANES):
        at = query_ref.shape[1] + col
        tile = rotate_tile(project[:, at : at + LANES], key_cos, key_sin, 1.0)
        kv_ref[:, col : col + LANES] = tile.astype(BF16)


def group_windows(before, own, group):
    col = group * 2 * HEAD_WIDTH
    return [
        jnp.concatenate([before[:, at : at + HEAD_WIDTH], own[:, at : at + HEAD_WIDTH]], axis=0)
        for at in (col, col + HEAD_WIDTH)
    ]


def stack_heads(block, group):
    at = group * QUERIES_PER_GROUP * HEAD_WIDTH
    return jnp.concatenate(
        [
            block[:, at + i * HEAD_WIDTH : at + (i + 1) * HEAD_WIDTH]
            for i in range(QUERIES_PER_GROUP)
        ],
        axis=0,
    )


def store_heads(ref, group, value_t):
    at = group * QUERIES_PER_GROUP * HEAD_WIDTH
    for i in range(QUERIES_PER_GROUP):
        part = value_t[:, i * SEGMAX : (i + 1) * SEGMAX].T
        ref[:, at + i * HEAD_WIDTH : at + (i + 1) * HEAD_WIDTH] = part.astype(ref.dtype)


def clear_spare(ref, groups):
    used = groups * QUERIES_PER_GROUP * HEAD_WIDTH
    if used < ref.shape[1]:
        ref[:, used:] = jnp.zeros((ref.shape[0], ref.shape[1] - used), ref.dtype)


def probs_of(keys, queries, bias):
    scores = dot_nt(keys, queries) * SCORE_SCALE
    scores = scores + jnp.concatenate([bias] * QUERIES_PER_GROUP, axis=1)
    top = jnp.max(scores, axis=0, keepdims=True)
    weights = jnp.exp(scores - top)
    total = jnp.sum(weights, axis=0, keepdims=True)
    return weights * (1.0 / total)


def attend_kernel(query_ref, own_ref, before_ref, bias_ref, mixed_ref):
    groups = own_ref.shape[1] // (2 * HEAD_WIDTH)
    query, own, before, bias = query_ref[...], own_ref[...], before_ref[...], bias_ref[...]
    clear_spare(mixed_ref, groups)
    for group in range(groups):
        keys, values = group_windows(before, own, group)
        probs = probs_of(keys, stack_heads(query, group), bias).astype(BF16)
        store_heads(mixed_ref, group, dot_nn(values.T, probs))


def attend_back_kernel(
    query_ref, own_ref, before_ref, bias_ref, first_ref, rest_ref, branch_ref, cos_ref, sin_ref,
    dquery_ref, down_ref, dbefore_ref, raw_ref, held_ref,
):
    groups = own_ref.shape[1] // (2 * HEAD_WIDTH)
    hold_weight(first_ref, rest_ref, held_ref)
    mixed_grad = dot_nn(branch_ref[...], held_ref[...]).astype(BF16)
    query, own, before, bias = query_ref[...], own_ref[...], before_ref[...], bias_ref[...]
    clear_spare(raw_ref, groups)
    for group in range(groups):
        keys, values = group_windows(before, own, group)
        queries, grads = stack_heads(query, group), stack_heads(mixed_grad, group)
        probs = probs_of(keys, queries, bias)
        prob_grad = dot_nt(values, grads)
        inner = jnp.sum(probs * prob_grad, axis=0, keepdims=True)
        score_grad = (SCORE_SCALE * probs * (prob_grad - inner)).astype(BF16)
        store_heads(raw_ref, group, dot_nn(keys.T, score_grad))
        col = group * 2 * HEAD_WIDTH
        for at, part in (
            (col, dot_nn(score_grad, queries)),
            (col + HEAD_WIDTH, dot_nn(probs.astype(BF16), grads)),
        ):
            dbefore_ref[:, at : at + HEAD_WIDTH] = part[:SEGMAX].astype(dbefore_ref.dtype)
            down_ref[:, at : at + HEAD_WIDTH] = part[SEGMAX:]
    cosine, sine = cos_ref[...], sin_ref[...]
    for col in range(0, query_ref.shape[1], LANES):
        tile = rotate_tile(raw_ref[:, col : col + LANES], cosine, sine, -1.0)
        dquery_ref[:, col : col + LANES] = tile.astype(BF16)


def branch_weights_kernel(experts, halves, normed_t_ref, *refs):
    branch_refs, refs = refs[:halves], refs[halves:]
    high_refs, low_refs, refs = refs[:halves], refs[halves : 2 * halves], refs[2 * halves :]
    *mixed_refs, term_ref, turned_ref, router_ref = refs
    block = pl.program_id(0)
    width = mixed_refs[0].shape[1]

    @pl.when(block == 0)
    def _():
        turned_ref[...] = jnp.concatenate([ref[...].T for ref in branch_refs], axis=1)
        high, low = (
            jnp.concatenate([ref[...] for ref in part], axis=0) for part in (high_refs, low_refs)
        )
        normed_t = normed_t_ref[...]
        router_ref[...] = dot_nn(normed_t, high) + dot_nn(normed_t, low)

    mixed = jnp.concatenate([ref[...] for ref in mixed_refs], axis=0)
    out_grad = dot_nn(turned_ref[...], mixed).astype(BF16)
    slices, depth, _ = term_ref.shape
    term_ref[:, :, :width] = out_grad.reshape(slices, depth, width)
    router = pltpu.roll(router_ref[...], (LANES - block * experts) % LANES, axis=1)
    term_ref[:, :, width:] = router.astype(BF16).reshape(slices, depth, LANES)


def branch_kernel(halves, *refs):
    mixed_refs = refs[:halves]
    first_ref, rest_ref, inputs_ref, gain_ref, middle_ref, *normed_refs = refs[halves:]
    width = first_ref.shape[-1]
    blocks = [first_ref[...].reshape(D, width)]
    blocks += [rest_ref[:, n].reshape(D, width) for n in range(rest_ref.shape[1])]
    weight = jnp.concatenate(blocks, axis=1)
    mixed = jnp.concatenate([ref[...] for ref in mixed_refs], axis=0)
    middle = inputs_ref[...].astype(F32) + dot_nt(mixed, weight)
    scale = lax.rsqrt(jnp.mean(middle * middle, axis=1, keepdims=True) + EPS)
    middle_ref[...] = middle
    normed = (middle * scale * gain_ref[...]).astype(BF16)
    for n, ref in enumerate(normed_refs):
        ref[...] = normed[n * CHUNK : (n + 1) * CHUNK]


def middle_back_kernel(
    own_ref, up_ref, down_ref, gates_ref, select_ref, router_ref, middle_ref, gain_ref, grad_ref,
    middle_grad_ref, branch_ref, high_ref, low_ref, gain_grad_ref,
):
    grad = own_ref[...].astype(F32) + up_ref[...].astype(F32) + down_ref[...].astype(F32)
    pairs = dot_nn(grad[:, D:].astype(BF16), select_ref[...])
    gates, router = gates_ref[...], router_ref[...]
    logit_grad = gates * (pairs - jnp.sum(gates * pairs, axis=1, keepdims=True))
    high = logit_grad.astype(BF16)
    low = (logit_grad - high.astype(F32)).astype(BF16)
    high_ref[...] = high
    low_ref[...] = low
    grad = grad[:, :D] + dot_nt(high, router) + dot_nt(low, router)
    back, gain_grad = norm_back(middle_ref[...], gain_ref[...], grad)
    middle_grad = grad_ref[...].astype(F32) + back
    middle_grad_ref[...] = middle_grad
    branch_ref[...] = middle_grad.astype(BF16)

    @pl.when(pl.program_id(0) == 0)
    def _():
        gain_grad_ref[...] = gain_grad

    @pl.when(pl.program_id(0) > 0)
    def _():
        gain_grad_ref[...] += gain_grad


def project_back_kernel(halves, *refs):
    dquery_refs, refs = refs[:halves], refs[halves:]
    own_refs, refs = refs[:halves], refs[halves:]
    next_refs, refs = refs[:halves], refs[halves:]
    (half_ref, normed_t_ref, first_ref, rest_ref, cos_ref, sin_ref, mine_ref, other_ref, total_ref,
     held_ref) = refs
    block = pl.program_id(0)
    key_cos, key_sin = key_tables(cos_ref[...], sin_ref[...])
    tiles = [jnp.concatenate([ref[...] for ref in dquery_refs], axis=0)]
    for col in range(0, own_refs[0].shape[1], LANES):
        cols = slice(col, col + LANES)
        tile = jnp.concatenate(
            [own[:, cols] + after_[:, cols].astype(F32) for own, after_ in zip(own_refs, next_refs)],
            axis=0,
        )
        tiles.append(rotate_tile(tile, key_cos, key_sin, -1.0).astype(BF16))
    grads = jnp.concatenate(tiles, axis=1)
    hold_weight(first_ref, rest_ref, held_ref)
    dweight = dot_nn(normed_t_ref[...], grads).astype(BF16)
    store_halves(half_ref, mine_ref, other_ref, slice(0, grads.shape[1]), dweight)
    part = dot_nt(grads, held_ref[...])

    @pl.when(block == 0)
    def _():
        total_ref[...] = part

    @pl.when(block > 0)
    def _():
        total_ref[...] += part


def input_back_kernel(
    inputs_ref, total_ref, gain_ref, middle_grad_ref, input_grad_ref, gain_grad_ref
):
    back, gain_grad = norm_back(inputs_ref[...].astype(F32), gain_ref[...], total_ref[...])
    input_grad_ref[...] = middle_grad_ref[...] + back

    @pl.when(pl.program_id(0) == 0)
    def _():
        gain_grad_ref[...] = gain_grad

    @pl.when(pl.program_id(0) > 0)
    def _():
        gain_grad_ref[...] += gain_grad


def joined_sum_kernel(groups, *refs):
    *part_refs, out_ref = refs
    rows = out_ref.shape[0]
    total = part_refs[0][...].astype(F32)
    for ref in part_refs[1:]:
        total = total + ref[:rows, :].astype(F32)
    queries = QUERIES_PER_GROUP * HEAD_WIDTH
    span = queries + 2 * HEAD_WIDTH
    width = total.shape[1] - groups * 2 * HEAD_WIDTH
    for group in range(groups):
        at = group * span
        out_ref[:, at : at + queries] = total[:, group * queries : (group + 1) * queries]
        col = width + group * 2 * HEAD_WIDTH
        out_ref[:, at + queries : at + span] = total[:, col : col + 2 * HEAD_WIDTH]


def norm_back(resid, gain, grad):
    scale = lax.rsqrt(jnp.mean(resid * resid, axis=1, keepdims=True) + EPS)
    gain_grad = jnp.sum(grad * resid * scale, axis=0, keepdims=True)
    scaled = grad * gain
    inner = jnp.sum(scaled * resid, axis=1, keepdims=True)
    return scale * scaled - resid * (scale * scale * scale * inner / D), gain_grad


def slots_kernel(experts, first_ref, ids_ref, rank_ref, pos_ref, ends_ref):
    length = ids_ref.shape[1]
    row = lax.broadcasted_iota(jnp.int32, (SUBLANES, length), 0)
    wanted = jnp.where(row < experts, row + first_ref[0], -1)
    rank = jnp.full((SUBLANES, length), 1 << 30, jnp.int32)
    for k in range(TOPK):
        rank = jnp.where(ids_ref[k : k + 1, :] == wanted, rank_ref[k : k + 1, :], rank)
    limit = jnp.zeros((SUBLANES, 1), jnp.int32)
    for bit in reversed(range((length * TOPK).bit_length())):
        higher = limit + (1 << bit)
        count = jnp.sum(jnp.where(rank < higher, 1.0, 0.0), axis=1, keepdims=True)
        limit = jnp.where(count <= CAP, higher, limit)
    kept = jnp.where(rank < limit, 1.0, 0.0)
    before = jnp.where(
        lax.broadcasted_iota(jnp.int32, (CHUNK, CHUNK), 0)
        < lax.broadcasted_iota(jnp.int32, (CHUNK, CHUNK), 1),
        1.0,
        0.0,
    ).astype(BF16)
    lane = lax.broadcasted_iota(jnp.int32, ends_ref.shape, 1)
    so_far = jnp.zeros((SUBLANES, 1), F32)
    ends = jnp.zeros(ends_ref.shape, F32)
    for n in range(length // CHUNK):
        part = kept[:, n * CHUNK : (n + 1) * CHUNK]
        place = dot_nn(part.astype(BF16), before) + so_far
        pos_ref[n] = jnp.where(part > 0.5, place, -1.0).astype(jnp.int32)
        so_far = so_far + jnp.sum(part, axis=1, keepdims=True)
        ends = jnp.where(lane == n + 1, so_far, ends)
    ends_ref[...] = ends.astype(jnp.int32)


def slot_windows(ends_ref, experts, chunk, window):
    firsts = [ends_ref[e, chunk] // SUBLANES * SUBLANES for e in range(experts)]
    ends = [ends_ref[e, chunk + 1] for e in range(experts)]
    count = jnp.int32(0)
    for first, end in zip(firsts, ends):
        count = jnp.maximum(count, (end - first + window - 1) // window)
    return firsts, ends, count


def window_start(first, n_window, window):
    return pl.multiple_of(jnp.minimum(first + n_window * window, SLOTS - window), SUBLANES)


def dispatch_kernel(with_gates, experts, size, *refs):
    shard_ref, ends_ref, *refs = refs
    if with_gates:
        *x_refs, pos_ref, router_ref, member_ref, out_ref, gate_ref, hot_ref, held_ref, sems = refs
    else:
        *x_refs, pos_ref, out_ref, hot_ref, held_ref, sems = refs
    window = hot_ref.shape[0] // experts
    span = 2 * size - 1
    parts = len(x_refs) // span
    part_rows = held_ref.shape[1] // parts

    def fetch(n, part, source):
        rows = pl.ds(part * part_rows, part_rows)
        return pltpu.make_async_copy(
            x_refs[part * span + source], held_ref.at[n, rows, :], sems.at[n, part]
        )

    for n in range(size):
        for part in range(parts):
            if n == 0:
                fetch(n, part, 0).start()
            else:
                below = shard_ref[0] >= n

                @pl.when(below)
                def _(n=n, part=part):
                    fetch(n, part, n).start()

                @pl.when(jnp.logical_not(below))
                def _(n=n, part=part):
                    fetch(n, part, span - n).start()

    out_ref[...] = jnp.zeros(out_ref.shape, BF16)
    if with_gates:
        gate_ref[...] = jnp.zeros(gate_ref.shape, F32)
    row = lax.broadcasted_iota(jnp.int32, (window, CHUNK), 0)
    halves = held_ref.shape[1] // CHUNK
    for n in range(size):
        for part in range(parts):
            fetch(n, part, 0).wait()
        for half in range(halves):
            chunk = shard_ref[n] * halves + half
            x = held_ref[n, half * CHUNK : (half + 1) * CHUNK, :]
            pos = pos_ref[chunk]
            firsts, ends, count = slot_windows(ends_ref, experts, chunk, window)
            if with_gates:
                logits = jnp.where(member_ref[chunk] > 0.5, dot_nn(x, router_ref[...]), MASKED)
                raised = jnp.exp(logits)
                gates = raised / jnp.sum(raised, axis=1, keepdims=True)
                lane = lax.broadcasted_iota(jnp.int32, gates.shape, 1)
                gates = jnp.where(lane < SUBLANES, gates, 0.0)
                high = gates.astype(BF16).astype(F32)
                gates = (high + pltpu.roll(gates - high, SUBLANES, axis=1)).astype(BF16)

            def body(n_window, _):
                for e in range(experts):
                    start = firsts[e] + n_window * window
                    at = window_start(firsts[e], n_window, window)
                    place = pos[e : e + 1, :]
                    place = jnp.where(place >= start, place - at, -1)
                    hot_ref[e * window : (e + 1) * window, :] = jnp.where(
                        row == place, 1.0, 0.0
                    ).astype(BF16)
                hot = hot_ref[...]
                rows = dot_nn(hot, x)
                if with_gates:
                    gate_rows = dot_nn(hot, gates)
                for e in range(experts):
                    start = firsts[e] + n_window * window
                    at = window_start(firsts[e], n_window, window)
                    part = slice(e * window, (e + 1) * window)

                    @pl.when(start < ends[e])
                    def _():
                        out_ref[e, pl.ds(at, window), :] += rows[part].astype(BF16)
                        if with_gates:
                            gate_ref[e, pl.ds(at, window), :] += gate_rows[part]

                return 0

            lax.fori_loop(0, count, body, 0)


def combine_kernel(with_pairs, sizes, order, *refs):
    piece_ref, ends_ref, place_ref, *refs = refs
    rows_refs, refs = refs[: len(sizes)], refs[len(sizes) :]
    if with_pairs:
        pair_refs, refs = refs[: len(sizes)], refs[len(sizes) :]
        *out_refs, held_ref, sems, hot_ref, total_ref, held_pair_ref, pair_total_ref = refs
    else:
        *out_refs, held_ref, sems, hot_ref, total_ref = refs
    experts = sum(sizes)
    count_out = len(out_refs)
    home = [(n, e) for n, size in enumerate(sizes) for e in range(size)]
    step, steps = pl.program_id(0), pl.num_programs(0)
    halves = steps // len(order)
    visits = steps // count_out

    def chunk_of(at_step):
        return piece_ref[at_step // halves] * halves + at_step % halves

    def copies(chunk, n_window, slot):
        firsts = slot_windows(ends_ref, experts, chunk, WINDOW)[0]
        return [
            pltpu.make_async_copy(
                rows_refs[n].at[own, pl.ds(window_start(firsts[e], n_window, WINDOW), WINDOW), :],
                held_ref.at[slot, pl.ds(e * WINDOW, WINDOW), :],
                sems.at[slot, e],
            )
            for e, (n, own) in enumerate(home)
        ]

    @pl.when(step == 0)
    def _():
        for copy in copies(chunk_of(step), 0, 0):
            copy.start()

    @pl.when(step + 1 < steps)
    def _():
        for copy in copies(chunk_of(step + 1), 0, (step + 1) % 2):
            copy.start()

    chunk = chunk_of(step)
    firsts, ends, count = slot_windows(ends_ref, experts, chunk, WINDOW)
    lane = lax.broadcasted_iota(jnp.int32, (CHUNK, WINDOW), 1)
    places = place_ref[...]

    def mark(n_window):
        for e, (n, own) in enumerate(home):
            start = firsts[e] + n_window * WINDOW
            at = window_start(firsts[e], n_window, WINDOW)
            place = places[:, e : e + 1]
            place = jnp.where(place >= start, place - at, -1)
            cols = slice(e * WINDOW, (e + 1) * WINDOW)
            hot_ref[:, cols] = jnp.where(lane == place, 1.0, 0.0).astype(BF16)
            if with_pairs:
                held_pair_ref[cols, :] = pair_refs[n][own, pl.ds(at, WINDOW), :]

    mark(0)
    for copy in copies(chunk, 0, step % 2):
        copy.wait()
    total_ref[...] = dot_nn(hot_ref[...], held_ref[step % 2])
    if with_pairs:
        pair_total_ref[...] = dot_nn(hot_ref[...], held_pair_ref[...])

    def body(n_window, _):
        more = copies(chunk, n_window, 2)
        for copy in more:
            copy.start()
        mark(n_window)
        for copy in more:
            copy.wait()
        total_ref[...] += dot_nn(hot_ref[...], held_ref[2])
        if with_pairs:
            pair_total_ref[...] += dot_nn(hot_ref[...], held_pair_ref[...])
        return 0

    lax.fori_loop(1, count, body, 0)
    for n, out_ref in enumerate(out_refs):

        @pl.when(step // visits == n)
        def _(n=n * visits // halves, out_ref=out_ref):
            out_ref[:, :D] = total_ref[...].astype(BF16)
            if with_pairs:
                place = -order[n] % len(order) * 2 * experts
                out_ref[:, D:] = pltpu.roll(pair_total_ref[...], place, axis=1).astype(BF16)


def expert_kernel(
    first, experts, half_ref, x_ref, grad_ref, gate_ref, weight_ref, y_ref, z_ref, pair_ref, *term_refs,
):
    e = first + pl.program_id(0)
    x, slot_grad = x_ref[0], grad_ref[0]
    w_in, w_out = weight_ref[0, :, : 2 * FF], weight_ref[0, :, 2 * FF :]
    lane = lax.broadcasted_iota(jnp.int32, gate_ref.shape[1:], 1)
    gate = jnp.sum(
        jnp.where((lane == e) | (lane == e + SUBLANES), gate_ref[0], 0.0), axis=1, keepdims=True
    )
    gate_up = dot_nn(x, w_in)
    gate_part, up_part = gate_up[:, :FF], gate_up[:, FF:]
    sigmoid = jax.nn.sigmoid(gate_part)
    silu = gate_part * sigmoid
    hidden = (silu * up_part).astype(BF16)
    raw = dot_nn(slot_grad, w_out)
    pair = jnp.sum(hidden.astype(F32) * raw, axis=1, keepdims=True)
    high = pair.astype(BF16).astype(F32)
    pair_ref[0] = jnp.where(
        lane == e, high, jnp.where(lane == e + experts, pair - high, 0.0)
    ).astype(BF16)
    hidden_grad = gate * raw
    gate_up_grad = jnp.concatenate(
        [
            (hidden_grad * up_part * sigmoid * (1.0 + gate_part * (1.0 - sigmoid))).astype(BF16),
            (hidden_grad * silu).astype(BF16),
        ],
        axis=1,
    )
    z_ref[0] = dot_nt(gate_up_grad, w_in).astype(BF16)
    y_ref[0] = (gate * dot_nt(hidden, w_out)).astype(BF16)
    rows_grad = (gate * slot_grad.astype(F32)).astype(BF16)
    in_term = dot_tn(x, gate_up_grad).astype(BF16)
    out_term = dot_tn(rows_grad, hidden).astype(BF16)
    if len(term_refs) == 2:
        store_halves(half_ref, *term_refs, slice(0, 2 * FF), in_term)
        store_halves(half_ref, *term_refs, slice(2 * FF, 3 * FF), out_term)
    else:
        term_ref = term_refs[0]
        slices, depth, _ = term_ref.shape
        term_ref[:, :, : 2 * FF] = in_term.reshape(slices, depth, 2 * FF)
        term_ref[:, :, 2 * FF :] = out_term.reshape(slices, depth, FF)


def after(value, *others):
    return lax.optimization_barrier((value,) + others)[0]


def pair_scatter(mine, other, size, *gates):
    taken = after(lax.ppermute(other, "gx", [(s, s ^ 1) for s in range(size)]), *gates)
    mine = (mine.astype(F32) + taken.astype(F32)).astype(mine.dtype)
    groups = [list(range(0, size, 2)), list(range(1, size, 2))]
    total = lax.psum_scatter(mine, "gx", scatter_dimension=0, tiled=True, axis_index_groups=groups)
    return lax.optimization_barrier(total)[0]


def direct_gather(part, size):
    return jnp.stack(
        [
            lax.ppermute(part, "gy", [(s, (s + k) % size) for s in range(size)])
            for k in range(1, size)
        ]
    )


def gather_step(pair, step, size, *gates):
    up, down = (after(part, *gates) if gates else part for part in pair)
    return (
        lax.ppermute(up, "gy", [(s, s + 1) for s in range(step, size - 1)]),
        lax.ppermute(down, "gy", [(s + 1, s) for s in range(0, size - 1 - step)]),
    )


def sum_added(parts, pair, step, size, *gates):
    above, below = parts[step], parts[size - step]
    if gates:
        pair = tuple(after(part, *gates) for part in pair)
    if pair is not None:
        above, below = (
            (a.astype(F32) + b.astype(F32)).astype(a.dtype)
            for a, b in zip((above, below), pair)
        )
    return above, below


def sum_sent(added, step, size):
    above, below = added
    return (
        lax.ppermute(above, "gy", [(s, s + 1) for s in range(step)]),
        lax.ppermute(below, "gy", [(size - 1 - s, size - 2 - s) for s in range(step)]),
    )


def sum_step(parts, pair, step, size, *gates):
    return sum_sent(sum_added(parts, pair, step, size, *gates), step, size)


def sum_steps_of(parts, size, gates):
    steps, pair = [], None
    for step in range(1, size):
        pair = sum_step(parts, pair, step, size, *gates.get(step, ()))
        steps.append(pair)
    return steps


def direct_sum(parts, size, *gates):
    taken = [
        lax.ppermute(parts[k], "gy", [(s, (s - k) % size) for s in range(size)])
        for k in range(1, size)
    ]
    total = parts[0].astype(F32)
    for part in taken:
        total = total + after(part, *gates).astype(F32)
    return total


def summed(parts, steps):
    return parts[0].astype(F32) + steps[-1][0].astype(F32) + steps[-1][1].astype(F32)


def shards(
    nx,
    ny,
    tokens,
    attn_gain,
    query_key_value_weight,
    out_weight,
    moe_gain,
    router_weight,
    expert_in,
    expert_out,
    expert_ids,
    route_order,
    segment_ids,
    out_grad,
):
    rows = tokens.shape[0]
    length = segment_ids.shape[1]
    depth = out_weight.shape[1]
    heads_width = out_weight.shape[0]
    groups = heads_width // (HEAD_WIDTH * QUERIES_PER_GROUP)
    spare = -heads_width % LANES
    width = heads_width + spare
    kv_width = groups * 2 * HEAD_WIDTH
    joined = width + kv_width
    experts = router_weight.shape[0]
    all_experts = experts * ny
    chunks = length // CHUNK
    own_chunks = rows // CHUNK
    me = lax.axis_index("gy")
    first_expert = me * experts
    first_row = me * rows
    both = ("gx", "gy")

    pos, ends = pl.pallas_call(
        functools.partial(slots_kernel, experts),
        in_specs=[
            pl.BlockSpec(memory_space=pltpu.SMEM),
            pl.BlockSpec(memory_space=pltpu.VMEM),
            pl.BlockSpec(memory_space=pltpu.VMEM),
        ],
        out_shape=[
            jax.ShapeDtypeStruct((chunks, SUBLANES, CHUNK), jnp.int32),
            jax.ShapeDtypeStruct((SUBLANES, LANES), jnp.int32),
        ],
        compiler_params=params(),
        cost_estimate=cost(3),
        name="slots",
    )(
        first_expert.reshape(1),
        expert_ids.T,
        route_order[0].reshape(length, TOPK).T,
    )
    places = jnp.pad(
        pos.transpose(0, 2, 1).reshape(length, SUBLANES), ((0, 0), (0, LANES - SUBLANES))
    )
    ends = ends[:, : chunks + 1]
    pieces = (me - jnp.arange(ny, dtype=jnp.int32)) % ny
    lane_expert = jnp.arange(LANES, dtype=jnp.int32)
    turned_expert = (me - lane_expert // experts) % ny * experts + lane_expert % experts
    turned_expert = jnp.where(lane_expert < all_experts, turned_expert, -1)
    members = jnp.any(expert_ids[:, :, None] == turned_expert[None, None, :], axis=1)
    members = members.astype(F32).reshape(chunks, CHUNK, LANES)
    own_ids = lax.dynamic_slice_in_dim(expert_ids, first_row, rows, 0)
    own_members = jnp.any(own_ids[:, :, None] == turned_expert[None, None, :], axis=1).astype(F32)

    inputs = tokens.astype(F32)
    scale_one = lax.rsqrt(jnp.mean(inputs * inputs, axis=1, keepdims=True) + EPS)
    normed_one = (inputs * scale_one * attn_gain[None, :]).astype(BF16)
    normed_one_t = normed_one.T
    cosine, sine = rope_tiles(first_row, rows)
    labels = jnp.concatenate([jnp.full((SEGMAX,), -1, jnp.int32), segment_ids[0]])
    labels = lax.dynamic_slice_in_dim(labels, first_row, rows + SEGMAX, 0)
    position = jnp.arange(rows + SEGMAX, dtype=jnp.int32)
    bias = jnp.stack(
        [
            jnp.where(
                (labels[s : s + 2 * SEGMAX, None] == labels[None, s + SEGMAX : s + 2 * SEGMAX])
                & (
                    position[s : s + 2 * SEGMAX, None]
                    <= position[None, s + SEGMAX : s + 2 * SEGMAX]
                ),
                0.0,
                MASKED,
            ).astype(F32)
            for s in range(0, rows, SEGMAX)
        ]
    )
    grouped = query_key_value_weight.reshape(depth, groups, QUERIES_PER_GROUP + 2, HEAD_WIDTH)
    own_joined = jnp.concatenate(
        [
            jnp.pad(
                grouped[:, :, :QUERIES_PER_GROUP].reshape(depth, heads_width), ((0, 0), (0, spare))
            ),
            grouped[:, :, QUERIES_PER_GROUP:].reshape(depth, kv_width),
        ],
        axis=1,
    )
    own_out = jnp.pad(out_weight.T, ((0, 0), (0, spare)))
    own_router = jnp.pad(router_weight.T, ((0, 0), (0, LANES - experts)))
    gap = -(joined + LANES) % width
    own_weights = jnp.concatenate(
        [own_joined, own_router, jnp.zeros((depth, gap), BF16), own_out], axis=1
    )
    own_second = jnp.concatenate([own_out, own_router], axis=1)
    cut = experts * 2 // 5
    bounds = ((0, cut), (cut, experts))
    own_experts = [
        jnp.concatenate([expert_in[lo:hi], expert_out[lo:hi]], axis=2) for lo, hi in bounds
    ]
    first_weights = lax.all_gather(own_weights, "gx", axis=0)
    line_joined = after(direct_gather(own_joined, ny), *own_experts)
    own_second = after(own_second, line_joined)
    line_second = direct_gather(own_second, ny)
    ready = after(out_grad, line_second, bias, cosine, sine, normed_one)
    grad_steps = [gather_step((ready, ready), 0, ny)]
    rest_joined = lax.all_gather(line_joined, "gx", axis=0)
    rest_second = lax.all_gather(line_second, "gx", axis=0)
    wide = []
    for own in own_experts:
        wide.append(lax.all_gather(own, "gx", axis=1, tiled=True))


    out_column = (joined + LANES + gap) // width
    rest_block = lambda b: (0, jnp.maximum(b - 1, 0), 0, 0)
    joined_specs = [
        pl.BlockSpec((nx, depth, joined), lambda b: (0, 0, 0)),
        pl.BlockSpec((nx, pl.Squeezed(), depth, joined), rest_block),
    ]
    out_specs = [
        pl.BlockSpec((nx, depth, width), lambda b: (0, 0, out_column)),
        pl.BlockSpec((nx, pl.Squeezed(), depth, width), rest_block),
    ]
    held_joined = pltpu.VMEM((D, joined), BF16)
    held_out = pltpu.VMEM((D, width), BF16)
    query, kv = pl.pallas_call(
        project_kernel,
        grid=(ny,),
        in_specs=[
            whole((rows, D)),
            *joined_specs,
            whole((rows, LANES)),
            whole((rows, LANES)),
        ],
        out_specs=[
            pl.BlockSpec((rows, width), lambda b: (0, b)),
            pl.BlockSpec((rows, kv_width), lambda b: (0, b)),
        ],
        out_shape=[
            jax.ShapeDtypeStruct((rows, ny * width), BF16),
            jax.ShapeDtypeStruct((rows, ny * kv_width), BF16),
        ],
        scratch_shapes=[held_joined],
        compiler_params=params(),
        cost_estimate=cost(10),
        name="project",
    )(after(normed_one, bias), first_weights, rest_joined, cosine, sine)
    halo = lax.ppermute(kv[rows - SEGMAX :], "gy", [(s, s + 1) for s in range(ny - 1)])
    halves = rows // SEGMAX
    half_rows = lambda n, w: pl.BlockSpec((SEGMAX, w), lambda b: (n, b))
    whole_half = lambda n, w: pl.BlockSpec((SEGMAX, w), lambda b: (n, 0))
    below_rows = pl.BlockSpec((SEGMAX, kv_width), lambda b: (0, (b + ny - 1) % ny))
    bias_half = lambda n: pl.BlockSpec((pl.Squeezed(), 2 * SEGMAX, SEGMAX), lambda b: (n, 0, 0))

    def window(n):
        if n == 0:
            return [half_rows(0, kv_width), below_rows], (kv, halo)
        return [half_rows(n, kv_width), half_rows(n - 1, kv_width)], (kv, kv)

    mixed = [None] * halves
    for n in reversed(range(halves)):
        specs, arrays = window(n)
        mixed[n] = pl.pallas_call(
            attend_kernel,
            grid=(ny,),
            in_specs=[half_rows(n, width), *specs, bias_half(n)],
            out_specs=half_rows(0, width),
            out_shape=jax.ShapeDtypeStruct((SEGMAX, ny * width), BF16),
            compiler_params=params(),
            cost_estimate=cost(8),
            name="attend",
        )(query, *arrays, bias)
    for step in range(1, ny - 2):
        grad_steps.append(gather_step(grad_steps[-1], step, ny, mixed[-1]))
    middle, *normed_chunks = pl.pallas_call(
        functools.partial(branch_kernel, halves),
        grid=(1,),
        in_specs=[whole((SEGMAX, ny * width))] * halves
        + [
            out_specs[0],
            pl.BlockSpec((nx, ny - 1, depth, width), lambda _: (0, 0, 0, 0)),
            whole((rows, D)),
            whole((1, D)),
        ],
        out_specs=[whole((rows, D))] + [whole((CHUNK, D))] * own_chunks,
        out_shape=[jax.ShapeDtypeStruct((rows, D), F32)]
        + [jax.ShapeDtypeStruct((CHUNK, D), BF16)] * own_chunks,
        compiler_params=params(),
        cost_estimate=cost(7),
        name="branch",
    )(*mixed, first_weights, rest_second, tokens, moe_gain[None, :])

    router = jnp.concatenate(
        [
            first_weights[:, None, :, joined : joined + experts],
            rest_second[:, :, :, width : width + experts],
        ],
        axis=1,
    )
    router = router.transpose(0, 2, 1, 3).reshape(D, all_experts)
    router = jnp.pad(router, ((0, 0), (0, LANES - all_experts)))
    normed_two = jnp.concatenate(normed_chunks, axis=0)
    normed_steps = []
    for part in normed_chunks:
        part = after(part, grad_steps[-1])
        normed_steps.append([(part, part)])
    for step in range(ny - 1):
        for steps in normed_steps:
            steps.append(gather_step(steps[-1], step, ny))
    grad_steps.append(
        gather_step(grad_steps[-1], ny - 2, ny, *[steps[-1] for steps in normed_steps])
    )
    normed_pieces = []
    for part, steps in zip(normed_chunks, normed_steps):
        normed_pieces += [part] + [up for up, _ in steps[1:]] + [down for _, down in steps[1:]]
    grad_pieces = [out_grad] + [up for up, _ in grad_steps] + [down for _, down in grad_steps]
    smem = pl.BlockSpec(memory_space=pltpu.SMEM)
    vmem = pl.BlockSpec(memory_space=pltpu.VMEM)
    slot_rows = jax.ShapeDtypeStruct((experts, SLOTS, D), BF16)
    slot_lanes = lambda kind: jax.ShapeDtypeStruct((experts, SLOTS, LANES), kind)
    dispatch_scratch = lambda parts: [
        pltpu.VMEM((experts * SHORT_WINDOW, CHUNK), BF16),
        pltpu.VMEM((ny, rows, D), BF16),
        pltpu.SemaphoreType.DMA((ny, parts)),
    ]
    hbm = pl.BlockSpec(memory_space=pl.ANY)
    slot_grads = pl.pallas_call(
        functools.partial(dispatch_kernel, False, experts, ny),
        in_specs=[smem, smem] + [hbm] * (2 * ny - 1) + [vmem],
        out_specs=vmem,
        out_shape=slot_rows,
        scratch_shapes=dispatch_scratch(1),
        compiler_params=params(),
        cost_estimate=cost(26),
        name="dispatch_grads",
    )(pieces, ends, *grad_pieces, pos)
    dispatched, slot_gates = pl.pallas_call(
        functools.partial(dispatch_kernel, True, experts, ny),
        in_specs=[smem, smem] + [hbm] * len(normed_pieces) + [vmem] * 3,
        out_specs=[vmem, vmem],
        out_shape=[slot_rows, slot_lanes(F32)],
        scratch_shapes=dispatch_scratch(own_chunks),
        compiler_params=params(),
        cost_estimate=cost(31),
        name="dispatch_rows",
    )(pieces, ends, *normed_pieces, pos, router, members)

    half = (lax.axis_index("gx") % 2).reshape(1)
    y_rows, z_rows, slot_pairs, weight_terms = [], [], [], []
    for n, (lo, hi) in enumerate(bounds):
        outer = lambda *shape: pl.BlockSpec((1,) + shape, lambda e, lo=lo: (lo + e, 0, 0))
        inner = lambda *shape: pl.BlockSpec((1,) + shape, lambda e: (e, 0, 0))
        parts = n + 1
        slices = pl.BlockSpec((nx // parts, pl.Squeezed(), depth, 3 * FF), lambda e: (0, e, 0, 0))
        y, z, pair, *terms = pl.pallas_call(
            functools.partial(expert_kernel, lo, experts),
            grid=(hi - lo,),
            in_specs=[
                smem,
                outer(SLOTS, D),
                outer(SLOTS, D),
                outer(SLOTS, LANES),
                inner(D, 3 * FF),
            ],
            out_specs=[inner(SLOTS, D), inner(SLOTS, D), inner(SLOTS, LANES)]
            + [slices] * parts,
            out_shape=[
                jax.ShapeDtypeStruct((hi - lo, SLOTS, D), BF16),
                jax.ShapeDtypeStruct((hi - lo, SLOTS, D), BF16),
                jax.ShapeDtypeStruct((hi - lo, SLOTS, LANES), BF16),
            ]
            + [jax.ShapeDtypeStruct((nx // parts, hi - lo, depth, 3 * FF), BF16)] * parts,
            compiler_params=params(),
            cost_estimate=cost(9 * (hi - lo)),
            name="experts",
        )(half, dispatched, slot_grads, slot_gates, wide[n])
        y_rows.append(y)
        z_rows.append(z)
        slot_pairs.append(pair)
        weight_terms.append(terms)
    def combine(rows_in, which, pairs=None):
        held = pltpu.VMEM((3, experts * WINDOW, D), BF16)
        sems = pltpu.SemaphoreType.DMA((3, experts))
        hot_t = pltpu.VMEM((CHUNK, experts * WINDOW), BF16)
        total = pltpu.VMEM((CHUNK, D), F32)
        more = pairs is not None
        columns = D + LANES * more
        halves = chunks // ny
        here = pieces[jnp.array(which)]

        def place_map(c, piece_ref):
            return (piece_ref[c // halves] * halves + c % halves, 0)

        visits = 1 if more else halves

        def out_map(n):
            return lambda c, piece_ref: (jnp.clip(c - n * visits, 0, visits - 1), 0)

        return pl.pallas_call(
            functools.partial(combine_kernel, more, tuple(hi - lo for lo, hi in bounds), which),
            grid_spec=pltpu.PrefetchScalarGridSpec(
                num_scalar_prefetch=1,
                grid=(halves * len(which),),
                in_specs=[smem, pl.BlockSpec((CHUNK, LANES), place_map)]
                + [hbm] * len(bounds)
                + [once((hi - lo, SLOTS, LANES)) for lo, hi in bounds] * more,
                out_specs=[
                    pl.BlockSpec((CHUNK, columns), out_map(n))
                    for n in range(len(which) * halves // visits)
                ],
                scratch_shapes=[held, sems, hot_t, total]
                + [
                    pltpu.VMEM((experts * WINDOW, LANES), BF16),
                    pltpu.VMEM((CHUNK, LANES), F32),
                ]
                * more,
            ),
            out_shape=[jax.ShapeDtypeStruct((CHUNK * visits, columns), BF16)]
            * (len(which) * halves // visits),
            compiler_params=params(),
            cost_estimate=cost(16),
            name="combine_grads" if more else "combine_rows",
        )(here, ends, places, *rows_in, *(pairs if more else []))

    outer_pieces = sorted({1, ny - 1})
    inner_pieces = [k for k in range(ny) if k not in outer_pieces]
    order = outer_pieces + inner_pieces
    token_sum = combine(z_rows, order, slot_pairs)
    token_sum = [
        [token_sum[order.index(k) * own_chunks + n] for k in range(ny)] for n in range(own_chunks)
    ]
    token_steps = [[] for _ in token_sum]
    for step in range(1, ny):
        for parts, steps in zip(token_sum, token_steps):
            steps.append(sum_step(parts, steps[-1] if steps else None, step, ny))
    own_logits = jnp.where(own_members > 0.5, dot_nn(normed_two, router), MASKED)
    own_raised = jnp.exp(own_logits)
    own_gates = own_raised / jnp.sum(own_raised, axis=1, keepdims=True)
    source = lane_expert // (2 * experts) * experts + lane_expert % experts
    source = jnp.where(lane_expert < 2 * all_experts, source, -1)
    select = (source[:, None] == lane_expert[None, :]).astype(BF16)
    weight_sums = [
        lax.psum_scatter(weight_terms[0][0], "gx", scatter_dimension=0, tiled=True)[0],
        pair_scatter(*weight_terms[1], nx, token_sum[0][0]),
    ]
    combined = combine([after(y, [steps[-2] for steps in token_steps]) for y in y_rows], order)
    combined = [combined[order.index(k)] for k in range(ny)]
    row_block = lambda w: pl.BlockSpec((LANES, w), lambda r: (r, 0))
    later_block = lambda n, w: pl.BlockSpec((LANES, w), lambda r: (r + n * CHUNK // LANES, 0))
    backs = []
    for n, (parts, steps) in enumerate(zip(token_sum, token_steps)):
        backs.append(
            pl.pallas_call(
                middle_back_kernel,
                grid=(CHUNK // LANES,),
                in_specs=[row_block(D + LANES)] * 3
                + [later_block(n, LANES), whole((LANES, LANES)), whole((D, LANES))]
                + [later_block(n, D), whole((1, D)), later_block(n, D)],
                out_specs=[row_block(D), row_block(D), row_block(LANES), row_block(LANES)]
                + [whole((1, D))],
                out_shape=[
                    jax.ShapeDtypeStruct((CHUNK, D), F32),
                    jax.ShapeDtypeStruct((CHUNK, D), BF16),
                    jax.ShapeDtypeStruct((CHUNK, LANES), BF16),
                    jax.ShapeDtypeStruct((CHUNK, LANES), BF16),
                    jax.ShapeDtypeStruct((1, D), F32),
                ],
                compiler_params=params(),
                cost_estimate=cost(4),
                name="middle_back",
            )(after(parts[0], *combined), *steps[-1], own_gates, select, router, middle,
              moe_gain[None, :], out_grad)
        )
    middle_grads, branch_grads, highs, lows, moe_gain_grads = zip(*backs)
    moe_gain_grad = sum(moe_gain_grads)

    combined_steps = [sum_step(combined, None, 1, ny)]

    dquery, dkv, dbefore = [], [], []
    for n in range(halves):
        specs, arrays = window(n)
        outs = pl.pallas_call(
            attend_back_kernel,
            grid=(ny,),
            in_specs=[
                half_rows(n, width),
                *specs,
                bias_half(n),
                *out_specs,
                whole((SEGMAX, D)),
                whole_half(n, LANES),
                whole_half(n, LANES),
            ],
            out_specs=[half_rows(0, width), half_rows(0, kv_width), half_rows(0, kv_width)],
            out_shape=[
                jax.ShapeDtypeStruct((SEGMAX, ny * width), BF16),
                jax.ShapeDtypeStruct((SEGMAX, ny * kv_width), F32),
                jax.ShapeDtypeStruct((SEGMAX, ny * kv_width), F32 if n else BF16),
            ],
            scratch_shapes=[pltpu.VMEM((SEGMAX, width), F32), held_out],
            compiler_params=params(),
            cost_estimate=cost(17),
            name="attend_back",
        )(query, *arrays, bias, first_weights, rest_second, after(branch_grads[n], *branch_grads, *combined, *dbefore),
          cosine, sine)
        for kept, out in zip((dquery, dkv, dbefore), outs):
            kept.append(out)
    halo_grad = lax.ppermute(dbefore[0], "gy", [(s + 1, s) for s in range(ny - 1)])
    second_term = pl.pallas_call(
        functools.partial(branch_weights_kernel, experts, halves),
        grid=(ny,),
        in_specs=[whole((D, rows))]
        + [whole((CHUNK, D))] * halves
        + [whole((CHUNK, LANES))] * (2 * halves)
        + [half_rows(0, width)] * halves,
        out_specs=pl.BlockSpec((nx, pl.Squeezed(), depth, width + LANES), lambda b: (0, b, 0, 0)),
        out_shape=jax.ShapeDtypeStruct((nx, ny, depth, width + LANES), BF16),
        scratch_shapes=[pltpu.VMEM((D, rows), BF16), pltpu.VMEM((D, LANES), F32)],
        compiler_params=params(),
        cost_estimate=cost(9),
        name="branch_weights",
    )(normed_two.T, *branch_grads, *highs, *lows, *mixed)
    added = ()
    for step in range(2, ny):
        gates = (halo_grad,) if step == 2 else ()
        added = sum_added(combined, combined_steps[-1], step, ny, *gates)
        combined_steps.append(sum_sent(added, step, ny))
    next_rows = pl.BlockSpec((SEGMAX, kv_width), lambda b: (0, (b + 1) % ny))
    *joined_terms, normed_one_grad = pl.pallas_call(
        functools.partial(project_back_kernel, halves),
        grid=(ny,),
        in_specs=[half_rows(0, width)] * halves
        + [half_rows(0, kv_width)] * (2 * halves - 1)
        + [
            next_rows,
            smem,
            whole((D, rows)),
            *joined_specs,
            whole((rows, LANES)),
            whole((rows, LANES)),
        ],
        out_specs=[pl.BlockSpec((nx // 2, pl.Squeezed(), depth, joined), lambda b: (0, b, 0, 0))] * 2
        + [whole((rows, D))],
        out_shape=[jax.ShapeDtypeStruct((nx // 2, ny, depth, joined), BF16)] * 2
        + [jax.ShapeDtypeStruct((rows, D), F32)],
        scratch_shapes=[held_joined],
        compiler_params=params(),
        cost_estimate=cost(22),
        name="project_back",
    )(*dquery, *dkv, *dbefore[1:], halo_grad, half, normed_one_t, first_weights, rest_joined, cosine,
      sine)
    in_grad, down_grad = [], []
    for part in after(tuple(weight_sums), joined_terms):
        in_grad.append(part[..., : 2 * FF].astype(F32))
        down_grad.append(part[..., 2 * FF :].astype(F32))
    in_grad, down_grad = jnp.concatenate(in_grad), jnp.concatenate(down_grad)
    last = tuple(after(part, in_grad, down_grad) for part in combined_steps[-1])
    layer_out = (middle + summed(combined, [last])).astype(BF16)
    input_grad, attn_gain_grad = pl.pallas_call(
        input_back_kernel,
        grid=(rows // LANES,),
        in_specs=[row_block(D), row_block(D), whole((1, D)), row_block(D)],
        out_specs=[row_block(D), whole((1, D))],
        out_shape=[
            jax.ShapeDtypeStruct((rows, D), F32),
            jax.ShapeDtypeStruct((1, D), F32),
        ],
        compiler_params=params(),
        cost_estimate=cost(6),
        name="input_back",
    )(tokens, normed_one_grad, attn_gain[None, :], jnp.concatenate(middle_grads))

    second_sum = lax.psum_scatter(
        after(second_term, weight_sums[0]), "gx", scatter_dimension=0, tiled=True
    )
    second_sum = lax.optimization_barrier(second_sum)[0]
    mine, other = joined_terms
    other = after(other, combined_steps[1], attn_gain_grad)
    joined_sum = pair_scatter(mine, other, nx, second_sum, *added, *weight_sums)
    gain_sums = after(jnp.concatenate([attn_gain_grad, moe_gain_grad]), layer_out)
    bit = 1
    while bit < nx:
        pairs = [(s, s ^ bit) for s in range(nx)]
        gain_sums = gain_sums + lax.ppermute(gain_sums, "gx", pairs)
        bit = 2 * bit
    high = gain_sums.astype(BF16)
    low = (gain_sums - high.astype(F32)).astype(BF16)
    gains = jnp.stack([high, low]).reshape(-1)
    gain_rows = -(-gains.shape[0] // joined)
    gain_rows += -gain_rows % SUBLANES
    gains = jnp.pad(gains, (0, gain_rows * joined - gains.shape[0])).reshape(gain_rows, joined)
    joined_sum = after(joined_sum, gains)
    joined_parts, gain_parts = [joined_sum[0]], [gains]
    for k in range(1, ny):
        part = jnp.concatenate([joined_sum[k], gains], axis=0)
        part = lax.ppermute(part, "gy", [(s, (s - k) % ny) for s in range(ny)])
        joined_parts.append(part)
        gain_parts.append(part[depth:])
    second_sum = direct_sum(second_sum, ny, *joined_parts[1:])
    out_weight_grad = second_sum[:, :heads_width].T
    router_grad = second_sum[:, width : width + experts].T
    qkv_grad = pl.pallas_call(
        functools.partial(joined_sum_kernel, groups),
        out_shape=jax.ShapeDtypeStruct(query_key_value_weight.shape, F32),
        compiler_params=params(),
        cost_estimate=cost(2),
        name="joined_sum",
    )(*joined_parts)
    gain_sums = jnp.roll(jnp.stack(gain_parts), me, axis=0).astype(F32)
    gain_sums = gain_sums.reshape(ny, -1)[:, : 4 * D].reshape(ny, 2, 2, D)
    gain_sums = jnp.sum(gain_sums, axis=(0, 1))
    return (
        layer_out,
        input_grad,
        gain_sums[0],
        qkv_grad,
        out_weight_grad,
        gain_sums[1],
        router_grad,
        in_grad,
        down_grad,
    )


def solution(mesh):
    in_specs = (
        P(("gx", "gy"), None),
        P(),
        P("gx", "gy"),
        P("gy", "gx"),
        P(),
        P("gy", "gx"),
        P("gy", "gx", None),
        P("gy", "gx", None),
        P("gx", None),
        P("gx", None),
        P("gx", None),
        P(("gx", "gy"), None),
    )
    out_specs = (
        P(("gx", "gy"), None),
        P(("gx", "gy"), None),
        P(),
        P("gx", "gy"),
        P("gy", "gx"),
        P(),
        P("gy", "gx"),
        P("gy", "gx", None),
        P("gy", "gx", None),
    )
    body = functools.partial(shards, mesh.shape["gx"], mesh.shape["gy"])
    return jax.shard_map(body, mesh=mesh, in_specs=in_specs, out_specs=out_specs, check_vma=False)
```

```python
import functools

import jax
import jax.numpy as jnp
from jax import lax
from jax.experimental import pallas as pl
from jax.experimental.pallas import tpu as pltpu
from jax.sharding import PartitionSpec as P

D = 1536
HEAD_WIDTH = 64
FF = 512
TOPK = 8
SEGMAX = 256
QUERIES_PER_GROUP = 3
CAP = 460
SLOTS = 464
WINDOW = 128
SHORT_WINDOW = 96
CHUNK = 256
LANES = 128
SUBLANES = 16

EPS = 1e-05
MASKED = -1e30
SCORE_SCALE = HEAD_WIDTH ** (-0.5)
VMEM_BYTES = 60 * 1024 * 1024
F32 = jnp.float32
BF16 = jnp.bfloat16


def dot_nn(a, b):
    return lax.dot_general(a, b, (((1,), (0,)), ((), ())), preferred_element_type=F32)


def dot_nt(a, b):
    return lax.dot_general(a, b, (((1,), (1,)), ((), ())), preferred_element_type=F32)


def dot_tn(a, b):
    return lax.dot_general(a, b, (((0,), (0,)), ((), ())), preferred_element_type=F32)


def params(**more):
    return pltpu.CompilerParams(vmem_limit_bytes=VMEM_BYTES, **more)


def cost(micros):
    return pl.CostEstimate(
        flops=int(micros * 1.1e9), bytes_accessed=int(micros * 3.6e6), transcendentals=0
    )


def store_halves(half_ref, mine_ref, other_ref, columns, value):
    slices, depth, _ = mine_ref.shape
    for parity in range(2):
        own = half_ref[0] == parity
        for ref, taken in ((mine_ref, own), (other_ref, jnp.logical_not(own))):

            @pl.when(taken)
            def _(ref=ref, parity=parity):
                for n in range(slices):
                    at = (2 * n + parity) * depth
                    ref[n, :, columns] = value[at : at + depth]


def whole(shape):
    return pl.BlockSpec(shape, lambda *_: (0,) * len(shape))


def once(shape):
    return pl.BlockSpec(shape, lambda *_: (0,) * len(shape), pipeline_mode=pl.Buffered(1))


def rope_tiles(first_row, rows):
    half = HEAD_WIDTH // 2
    freq = jnp.exp(jnp.arange(half, dtype=F32) * (-2.0 * jnp.log(10000.0) / HEAD_WIDTH))
    position = (first_row + jnp.arange(rows, dtype=jnp.int32)).astype(F32)
    angle = position[:, None] * freq[None, :]
    cosine, sine = jnp.cos(angle), jnp.sin(angle)
    return (
        jnp.concatenate([cosine] * 4, axis=1),
        jnp.concatenate([-sine, sine, -sine, sine], axis=1),
    )


def swap_halves(tile):
    lane = lax.broadcasted_iota(jnp.int32, tile.shape, 1)
    half = HEAD_WIDTH // 2
    return jnp.where(
        lane % HEAD_WIDTH < half,
        pltpu.roll(tile, LANES - half, axis=1),
        pltpu.roll(tile, half, axis=1),
    )


def rotate_tile(tile, cosine, sine, sign):
    return tile * cosine + sign * swap_halves(tile) * sine


def key_tables(cosine, sine):
    lane = lax.broadcasted_iota(jnp.int32, cosine.shape, 1)
    is_key = lane < HEAD_WIDTH
    return jnp.where(is_key, cosine, 1.0), jnp.where(is_key, sine, 0.0)


def hold_weight(first_ref, rest_ref, held_ref):
    @pl.when(pl.program_id(0) == 0)
    def _():
        held_ref[...] = first_ref[...].reshape(held_ref.shape)

    @pl.when(pl.program_id(0) > 0)
    def _():
        held_ref[...] = rest_ref[...].reshape(held_ref.shape)


def project_kernel(
    normed_ref, first_ref, rest_ref, cos_ref, sin_ref, query_ref, kv_ref, held_ref
):
    hold_weight(first_ref, rest_ref, held_ref)
    project = dot_nn(normed_ref[...], held_ref[...])
    cosine, sine = cos_ref[...], sin_ref[...]
    key_cos, key_sin = key_tables(cosine, sine)
    for col in range(0, query_ref.shape[1], LANES):
        tile = rotate_tile(project[:, col : col + LANES], cosine, sine, 1.0)
        query_ref[:, col : col + LANES] = tile.astype(BF16)
    for col in range(0, kv_ref.shape[1], LANES):
        at = query_ref.shape[1] + col
        tile = rotate_tile(project[:, at : at + LANES], key_cos, key_sin, 1.0)
        kv_ref[:, col : col + LANES] = tile.astype(BF16)


def group_windows(before, own, group):
    col = group * 2 * HEAD_WIDTH
    return [
        jnp.concatenate([before[:, at : at + HEAD_WIDTH], own[:, at : at + HEAD_WIDTH]], axis=0)
        for at in (col, col + HEAD_WIDTH)
    ]


def stack_heads(block, group):
    at = group * QUERIES_PER_GROUP * HEAD_WIDTH
    return jnp.concatenate(
        [
            block[:, at + i * HEAD_WIDTH : at + (i + 1) * HEAD_WIDTH]
            for i in range(QUERIES_PER_GROUP)
        ],
        axis=0,
    )


def store_heads(ref, group, value_t):
    at = group * QUERIES_PER_GROUP * HEAD_WIDTH
    for i in range(QUERIES_PER_GROUP):
        part = value_t[:, i * SEGMAX : (i + 1) * SEGMAX].T
        ref[:, at + i * HEAD_WIDTH : at + (i + 1) * HEAD_WIDTH] = part.astype(ref.dtype)


def clear_spare(ref, groups):
    used = groups * QUERIES_PER_GROUP * HEAD_WIDTH
    if used < ref.shape[1]:
        ref[:, used:] = jnp.zeros((ref.shape[0], ref.shape[1] - used), ref.dtype)


def probs_of(keys, queries, bias):
    scores = dot_nt(keys, queries) * SCORE_SCALE
    scores = scores + jnp.concatenate([bias] * QUERIES_PER_GROUP, axis=1)
    top = jnp.max(scores, axis=0, keepdims=True)
    weights = jnp.exp(scores - top)
    total = jnp.sum(weights, axis=0, keepdims=True)
    return weights * (1.0 / total)


def attend_kernel(query_ref, own_ref, before_ref, bias_ref, mixed_ref):
    groups = own_ref.shape[1] // (2 * HEAD_WIDTH)
    query, own, before, bias = query_ref[...], own_ref[...], before_ref[...], bias_ref[...]
    clear_spare(mixed_ref, groups)
    for group in range(groups):
        keys, values = group_windows(before, own, group)
        probs = probs_of(keys, stack_heads(query, group), bias).astype(BF16)
        store_heads(mixed_ref, group, dot_nn(values.T, probs))


def attend_back_kernel(
    query_ref, own_ref, before_ref, bias_ref, first_ref, rest_ref, branch_ref, cos_ref, sin_ref,
    dquery_ref, down_ref, dbefore_ref, raw_ref, held_ref,
):
    groups = own_ref.shape[1] // (2 * HEAD_WIDTH)
    hold_weight(first_ref, rest_ref, held_ref)
    mixed_grad = dot_nn(branch_ref[...], held_ref[...]).astype(BF16)
    query, own, before, bias = query_ref[...], own_ref[...], before_ref[...], bias_ref[...]
    clear_spare(raw_ref, groups)
    for group in range(groups):
        keys, values = group_windows(before, own, group)
        queries, grads = stack_heads(query, group), stack_heads(mixed_grad, group)
        probs = probs_of(keys, queries, bias)
        prob_grad = dot_nt(values, grads)
        inner = jnp.sum(probs * prob_grad, axis=0, keepdims=True)
        score_grad = (SCORE_SCALE * probs * (prob_grad - inner)).astype(BF16)
        store_heads(raw_ref, group, dot_nn(keys.T, score_grad))
        col = group * 2 * HEAD_WIDTH
        for at, part in (
            (col, dot_nn(score_grad, queries)),
            (col + HEAD_WIDTH, dot_nn(probs.astype(BF16), grads)),
        ):
            dbefore_ref[:, at : at + HEAD_WIDTH] = part[:SEGMAX].astype(dbefore_ref.dtype)
            down_ref[:, at : at + HEAD_WIDTH] = part[SEGMAX:]
    cosine, sine = cos_ref[...], sin_ref[...]
    for col in range(0, query_ref.shape[1], LANES):
        tile = rotate_tile(raw_ref[:, col : col + LANES], cosine, sine, -1.0)
        dquery_ref[:, col : col + LANES] = tile.astype(BF16)


def branch_weights_kernel(experts, halves, normed_t_ref, *refs):
    branch_refs, refs = refs[:halves], refs[halves:]
    high_refs, low_refs, refs = refs[:halves], refs[halves : 2 * halves], refs[2 * halves :]
    *mixed_refs, term_ref, turned_ref, router_ref = refs
    block = pl.program_id(0)
    width = mixed_refs[0].shape[1]

    @pl.when(block == 0)
    def _():
        turned_ref[...] = jnp.concatenate([ref[...].T for ref in branch_refs], axis=1)
        high, low = (
            jnp.concatenate([ref[...] for ref in part], axis=0) for part in (high_refs, low_refs)
        )
        normed_t = normed_t_ref[...]
        router_ref[...] = dot_nn(normed_t, high) + dot_nn(normed_t, low)

    mixed = jnp.concatenate([ref[...] for ref in mixed_refs], axis=0)
    out_grad = dot_nn(turned_ref[...], mixed).astype(BF16)
    slices, depth, _ = term_ref.shape
    term_ref[:, :, :width] = out_grad.reshape(slices, depth, width)
    router = pltpu.roll(router_ref[...], (LANES - block * experts) % LANES, axis=1)
    term_ref[:, :, width:] = router.astype(BF16).reshape(slices, depth, LANES)


def branch_kernel(halves, *refs):
    mixed_refs = refs[:halves]
    first_ref, rest_ref, inputs_ref, gain_ref, middle_ref, *normed_refs = refs[halves:]
    width = first_ref.shape[-1]
    blocks = [first_ref[...].reshape(D, width)]
    blocks += [rest_ref[:, n].reshape(D, width) for n in range(rest_ref.shape[1])]
    weight = jnp.concatenate(blocks, axis=1)
    mixed = jnp.concatenate([ref[...] for ref in mixed_refs], axis=0)
    middle = inputs_ref[...].astype(F32) + dot_nt(mixed, weight)
    scale = lax.rsqrt(jnp.mean(middle * middle, axis=1, keepdims=True) + EPS)
    middle_ref[...] = middle
    normed = (middle * scale * gain_ref[...]).astype(BF16)
    for n, ref in enumerate(normed_refs):
        ref[...] = normed[n * CHUNK : (n + 1) * CHUNK]


def middle_back_kernel(
    own_ref, up_ref, down_ref, gates_ref, select_ref, router_ref, middle_ref, gain_ref, grad_ref,
    middle_grad_ref, branch_ref, high_ref, low_ref, gain_grad_ref,
):
    grad = own_ref[...].astype(F32) + up_ref[...].astype(F32) + down_ref[...].astype(F32)
    pairs = dot_nn(grad[:, D:].astype(BF16), select_ref[...])
    gates, router = gates_ref[...], router_ref[...]
    logit_grad = gates * (pairs - jnp.sum(gates * pairs, axis=1, keepdims=True))
    high = logit_grad.astype(BF16)
    low = (logit_grad - high.astype(F32)).astype(BF16)
    high_ref[...] = high
    low_ref[...] = low
    grad = grad[:, :D] + dot_nt(high, router) + dot_nt(low, router)
    back, gain_grad = norm_back(middle_ref[...], gain_ref[...], grad)
    middle_grad = grad_ref[...].astype(F32) + back
    middle_grad_ref[...] = middle_grad
    branch_ref[...] = middle_grad.astype(BF16)

    @pl.when(pl.program_id(0) == 0)
    def _():
        gain_grad_ref[...] = gain_grad

    @pl.when(pl.program_id(0) > 0)
    def _():
        gain_grad_ref[...] += gain_grad


def project_back_kernel(halves, *refs):
    dquery_refs, refs = refs[:halves], refs[halves:]
    own_refs, refs = refs[:halves], refs[halves:]
    next_refs, refs = refs[:halves], refs[halves:]
    (half_ref, normed_t_ref, first_ref, rest_ref, cos_ref, sin_ref, mine_ref, other_ref, total_ref,
     held_ref) = refs
    block = pl.program_id(0)
    key_cos, key_sin = key_tables(cos_ref[...], sin_ref[...])
    tiles = [jnp.concatenate([ref[...] for ref in dquery_refs], axis=0)]
    for col in range(0, own_refs[0].shape[1], LANES):
        cols = slice(col, col + LANES)
        tile = jnp.concatenate(
            [own[:, cols] + after_[:, cols].astype(F32) for own, after_ in zip(own_refs, next_refs)],
            axis=0,
        )
        tiles.append(rotate_tile(tile, key_cos, key_sin, -1.0).astype(BF16))
    grads = jnp.concatenate(tiles, axis=1)
    hold_weight(first_ref, rest_ref, held_ref)
    dweight = dot_nn(normed_t_ref[...], grads).astype(BF16)
    store_halves(half_ref, mine_ref, other_ref, slice(0, grads.shape[1]), dweight)
    part = dot_nt(grads, held_ref[...])

    @pl.when(block == 0)
    def _():
        total_ref[...] = part

    @pl.when(block > 0)
    def _():
        total_ref[...] += part


def input_back_kernel(
    inputs_ref, total_ref, gain_ref, middle_grad_ref, input_grad_ref, gain_grad_ref
):
    back, gain_grad = norm_back(inputs_ref[...].astype(F32), gain_ref[...], total_ref[...])
    input_grad_ref[...] = middle_grad_ref[...] + back

    @pl.when(pl.program_id(0) == 0)
    def _():
        gain_grad_ref[...] = gain_grad

    @pl.when(pl.program_id(0) > 0)
    def _():
        gain_grad_ref[...] += gain_grad


def joined_sum_kernel(groups, *refs):
    *part_refs, out_ref = refs
    rows = out_ref.shape[0]
    total = part_refs[0][...].astype(F32)
    for ref in part_refs[1:]:
        total = total + ref[:rows, :].astype(F32)
    queries = QUERIES_PER_GROUP * HEAD_WIDTH
    span = queries + 2 * HEAD_WIDTH
    width = total.shape[1] - groups * 2 * HEAD_WIDTH
    for group in range(groups):
        at = group * span
        out_ref[:, at : at + queries] = total[:, group * queries : (group + 1) * queries]
        col = width + group * 2 * HEAD_WIDTH
        out_ref[:, at + queries : at + span] = total[:, col : col + 2 * HEAD_WIDTH]


def norm_back(resid, gain, grad):
    scale = lax.rsqrt(jnp.mean(resid * resid, axis=1, keepdims=True) + EPS)
    gain_grad = jnp.sum(grad * resid * scale, axis=0, keepdims=True)
    scaled = grad * gain
    inner = jnp.sum(scaled * resid, axis=1, keepdims=True)
    return scale * scaled - resid * (scale * scale * scale * inner / D), gain_grad


def slots_kernel(experts, first_ref, ids_ref, rank_ref, pos_ref, ends_ref):
    length = ids_ref.shape[1]
    row = lax.broadcasted_iota(jnp.int32, (SUBLANES, length), 0)
    wanted = jnp.where(row < experts, row + first_ref[0], -1)
    rank = jnp.full((SUBLANES, length), 1 << 30, jnp.int32)
    for k in range(TOPK):
        rank = jnp.where(ids_ref[k : k + 1, :] == wanted, rank_ref[k : k + 1, :], rank)
    limit = jnp.zeros((SUBLANES, 1), jnp.int32)
    for bit in reversed(range((length * TOPK).bit_length())):
        higher = limit + (1 << bit)
        count = jnp.sum(jnp.where(rank < higher, 1.0, 0.0), axis=1, keepdims=True)
        limit = jnp.where(count <= CAP, higher, limit)
    kept = jnp.where(rank < limit, 1.0, 0.0)
    before = jnp.where(
        lax.broadcasted_iota(jnp.int32, (CHUNK, CHUNK), 0)
        < lax.broadcasted_iota(jnp.int32, (CHUNK, CHUNK), 1),
        1.0,
        0.0,
    ).astype(BF16)
    lane = lax.broadcasted_iota(jnp.int32, ends_ref.shape, 1)
    so_far = jnp.zeros((SUBLANES, 1), F32)
    ends = jnp.zeros(ends_ref.shape, F32)
    for n in range(length // CHUNK):
        part = kept[:, n * CHUNK : (n + 1) * CHUNK]
        place = dot_nn(part.astype(BF16), before) + so_far
        pos_ref[n] = jnp.where(part > 0.5, place, -1.0).astype(jnp.int32)
        so_far = so_far + jnp.sum(part, axis=1, keepdims=True)
        ends = jnp.where(lane == n + 1, so_far, ends)
    ends_ref[...] = ends.astype(jnp.int32)


def slot_windows(ends_ref, experts, chunk, window):
    firsts = [ends_ref[e, chunk] // SUBLANES * SUBLANES for e in range(experts)]
    ends = [ends_ref[e, chunk + 1] for e in range(experts)]
    count = jnp.int32(0)
    for first, end in zip(firsts, ends):
        count = jnp.maximum(count, (end - first + window - 1) // window)
    return firsts, ends, count


def window_start(first, n_window, window):
    return pl.multiple_of(jnp.minimum(first + n_window * window, SLOTS - window), SUBLANES)


def dispatch_kernel(with_gates, experts, size, *refs):
    shard_ref, ends_ref, *refs = refs
    if with_gates:
        *x_refs, pos_ref, router_ref, member_ref, out_ref, gate_ref, hot_ref, held_ref, sems = refs
    else:
        *x_refs, pos_ref, out_ref, hot_ref, held_ref, sems = refs
    window = hot_ref.shape[0] // experts
    span = 2 * size - 1
    parts = len(x_refs) // span
    part_rows = held_ref.shape[1] // parts

    def fetch(n, part, source):
        rows = pl.ds(part * part_rows, part_rows)
        return pltpu.make_async_copy(
            x_refs[part * span + source], held_ref.at[n, rows, :], sems.at[n, part]
        )

    for n in range(size):
        for part in range(parts):
            if n == 0:
                fetch(n, part, 0).start()
            else:
                below = shard_ref[0] >= n

                @pl.when(below)
                def _(n=n, part=part):
                    fetch(n, part, n).start()

                @pl.when(jnp.logical_not(below))
                def _(n=n, part=part):
                    fetch(n, part, span - n).start()

    out_ref[...] = jnp.zeros(out_ref.shape, BF16)
    if with_gates:
        gate_ref[...] = jnp.zeros(gate_ref.shape, F32)
    row = lax.broadcasted_iota(jnp.int32, (window, CHUNK), 0)
    halves = held_ref.shape[1] // CHUNK
    for n in range(size):
        for part in range(parts):
            fetch(n, part, 0).wait()
        for half in range(halves):
            chunk = shard_ref[n] * halves + half
            x = held_ref[n, half * CHUNK : (half + 1) * CHUNK, :]
            pos = pos_ref[chunk]
            firsts, ends, count = slot_windows(ends_ref, experts, chunk, window)
            if with_gates:
                logits = jnp.where(member_ref[chunk] > 0.5, dot_nn(x, router_ref[...]), MASKED)
                raised = jnp.exp(logits)
                gates = raised / jnp.sum(raised, axis=1, keepdims=True)
                lane = lax.broadcasted_iota(jnp.int32, gates.shape, 1)
                gates = jnp.where(lane < SUBLANES, gates, 0.0)
                high = gates.astype(BF16).astype(F32)
                gates = (high + pltpu.roll(gates - high, SUBLANES, axis=1)).astype(BF16)

            def body(n_window, _):
                for e in range(experts):
                    start = firsts[e] + n_window * window
                    at = window_start(firsts[e], n_window, window)
                    place = pos[e : e + 1, :]
                    place = jnp.where(place >= start, place - at, -1)
                    hot_ref[e * window : (e + 1) * window, :] = jnp.where(
                        row == place, 1.0, 0.0
                    ).astype(BF16)
                hot = hot_ref[...]
                rows = dot_nn(hot, x)
                if with_gates:
                    gate_rows = dot_nn(hot, gates)
                for e in range(experts):
                    start = firsts[e] + n_window * window
                    at = window_start(firsts[e], n_window, window)
                    part = slice(e * window, (e + 1) * window)

                    @pl.when(start < ends[e])
                    def _():
                        out_ref[e, pl.ds(at, window), :] += rows[part].astype(BF16)
                        if with_gates:
                            gate_ref[e, pl.ds(at, window), :] += gate_rows[part]

                return 0

            lax.fori_loop(0, count, body, 0)


def combine_kernel(with_pairs, sizes, order, *refs):
    piece_ref, ends_ref, place_ref, *refs = refs
    rows_refs, refs = refs[: len(sizes)], refs[len(sizes) :]
    if with_pairs:
        pair_refs, refs = refs[: len(sizes)], refs[len(sizes) :]
        *out_refs, held_ref, sems, hot_ref, total_ref, held_pair_ref, pair_total_ref = refs
    else:
        *out_refs, held_ref, sems, hot_ref, total_ref = refs
    experts = sum(sizes)
    count_out = len(out_refs)
    home = [(n, e) for n, size in enumerate(sizes) for e in range(size)]
    step, steps = pl.program_id(0), pl.num_programs(0)
    halves = steps // len(order)
    visits = steps // count_out

    def chunk_of(at_step):
        return piece_ref[at_step // halves] * halves + at_step % halves

    def copies(chunk, n_window, slot):
        firsts = slot_windows(ends_ref, experts, chunk, WINDOW)[0]
        return [
            pltpu.make_async_copy(
                rows_refs[n].at[own, pl.ds(window_start(firsts[e], n_window, WINDOW), WINDOW), :],
                held_ref.at[slot, pl.ds(e * WINDOW, WINDOW), :],
                sems.at[slot, e],
            )
            for e, (n, own) in enumerate(home)
        ]

    @pl.when(step == 0)
    def _():
        for copy in copies(chunk_of(step), 0, 0):
            copy.start()

    @pl.when(step + 1 < steps)
    def _():
        for copy in copies(chunk_of(step + 1), 0, (step + 1) % 2):
            copy.start()

    chunk = chunk_of(step)
    firsts, ends, count = slot_windows(ends_ref, experts, chunk, WINDOW)
    lane = lax.broadcasted_iota(jnp.int32, (CHUNK, WINDOW), 1)
    places = place_ref[...]

    def mark(n_window):
        for e, (n, own) in enumerate(home):
            start = firsts[e] + n_window * WINDOW
            at = window_start(firsts[e], n_window, WINDOW)
            place = places[:, e : e + 1]
            place = jnp.where(place >= start, place - at, -1)
            cols = slice(e * WINDOW, (e + 1) * WINDOW)
            hot_ref[:, cols] = jnp.where(lane == place, 1.0, 0.0).astype(BF16)
            if with_pairs:
                held_pair_ref[cols, :] = pair_refs[n][own, pl.ds(at, WINDOW), :]

    mark(0)
    for copy in copies(chunk, 0, step % 2):
        copy.wait()
    total_ref[...] = dot_nn(hot_ref[...], held_ref[step % 2])
    if with_pairs:
        pair_total_ref[...] = dot_nn(hot_ref[...], held_pair_ref[...])

    def body(n_window, _):
        more = copies(chunk, n_window, 2)
        for copy in more:
            copy.start()
        mark(n_window)
        for copy in more:
            copy.wait()
        total_ref[...] += dot_nn(hot_ref[...], held_ref[2])
        if with_pairs:
            pair_total_ref[...] += dot_nn(hot_ref[...], held_pair_ref[...])
        return 0

    lax.fori_loop(1, count, body, 0)
    for n, out_ref in enumerate(out_refs):

        @pl.when(step // visits == n)
        def _(n=n * visits // halves, out_ref=out_ref):
            out_ref[:, :D] = total_ref[...].astype(BF16)
            if with_pairs:
                place = -order[n] % len(order) * 2 * experts
                out_ref[:, D:] = pltpu.roll(pair_total_ref[...], place, axis=1).astype(BF16)


def expert_kernel(
    first, experts, half_ref, x_ref, grad_ref, gate_ref, weight_ref, y_ref, z_ref, pair_ref, *term_refs,
):
    e = first + pl.program_id(0)
    x, slot_grad = x_ref[0], grad_ref[0]
    w_in, w_out = weight_ref[0, :, : 2 * FF], weight_ref[0, :, 2 * FF :]
    lane = lax.broadcasted_iota(jnp.int32, gate_ref.shape[1:], 1)
    gate = jnp.sum(
        jnp.where((lane == e) | (lane == e + SUBLANES), gate_ref[0], 0.0), axis=1, keepdims=True
    )
    gate_up = dot_nn(x, w_in)
    gate_part, up_part = gate_up[:, :FF], gate_up[:, FF:]
    sigmoid = jax.nn.sigmoid(gate_part)
    silu = gate_part * sigmoid
    hidden = (silu * up_part).astype(BF16)
    raw = dot_nn(slot_grad, w_out)
    pair = jnp.sum(hidden.astype(F32) * raw, axis=1, keepdims=True)
    high = pair.astype(BF16).astype(F32)
    pair_ref[0] = jnp.where(
        lane == e, high, jnp.where(lane == e + experts, pair - high, 0.0)
    ).astype(BF16)
    hidden_grad = gate * raw
    gate_up_grad = jnp.concatenate(
        [
            (hidden_grad * up_part * sigmoid * (1.0 + gate_part * (1.0 - sigmoid))).astype(BF16),
            (hidden_grad * silu).astype(BF16),
        ],
        axis=1,
    )
    z_ref[0] = dot_nt(gate_up_grad, w_in).astype(BF16)
    y_ref[0] = (gate * dot_nt(hidden, w_out)).astype(BF16)
    rows_grad = (gate * slot_grad.astype(F32)).astype(BF16)
    in_term = dot_tn(x, gate_up_grad).astype(BF16)
    out_term = dot_tn(rows_grad, hidden).astype(BF16)
    if len(term_refs) == 2:
        store_halves(half_ref, *term_refs, slice(0, 2 * FF), in_term)
        store_halves(half_ref, *term_refs, slice(2 * FF, 3 * FF), out_term)
    else:
        term_ref = term_refs[0]
        slices, depth, _ = term_ref.shape
        term_ref[:, :, : 2 * FF] = in_term.reshape(slices, depth, 2 * FF)
        term_ref[:, :, 2 * FF :] = out_term.reshape(slices, depth, FF)


def after(value, *others):
    return lax.optimization_barrier((value,) + others)[0]


def pair_scatter(mine, other, size, *gates):
    taken = after(lax.ppermute(other, "gx", [(s, s ^ 1) for s in range(size)]), *gates)
    mine = (mine.astype(F32) + taken.astype(F32)).astype(mine.dtype)
    groups = [list(range(0, size, 2)), list(range(1, size, 2))]
    total = lax.psum_scatter(mine, "gx", scatter_dimension=0, tiled=True, axis_index_groups=groups)
    return lax.optimization_barrier(total)[0]


def direct_gather(part, size):
    return jnp.stack(
        [
            lax.ppermute(part, "gy", [(s, (s + k) % size) for s in range(size)])
            for k in range(1, size)
        ]
    )


def gather_step(pair, step, size, *gates):
    up, down = (after(part, *gates) if gates else part for part in pair)
    return (
        lax.ppermute(up, "gy", [(s, s + 1) for s in range(step, size - 1)]),
        lax.ppermute(down, "gy", [(s + 1, s) for s in range(0, size - 1 - step)]),
    )


def sum_added(parts, pair, step, size, *gates):
    above, below = parts[step], parts[size - step]
    if gates:
        pair = tuple(after(part, *gates) for part in pair)
    if pair is not None:
        above, below = (
            (a.astype(F32) + b.astype(F32)).astype(a.dtype)
            for a, b in zip((above, below), pair)
        )
    return above, below


def sum_sent(added, step, size):
    above, below = added
    return (
        lax.ppermute(above, "gy", [(s, s + 1) for s in range(step)]),
        lax.ppermute(below, "gy", [(size - 1 - s, size - 2 - s) for s in range(step)]),
    )


def sum_step(parts, pair, step, size, *gates):
    return sum_sent(sum_added(parts, pair, step, size, *gates), step, size)


def sum_steps_of(parts, size, gates):
    steps, pair = [], None
    for step in range(1, size):
        pair = sum_step(parts, pair, step, size, *gates.get(step, ()))
        steps.append(pair)
    return steps


def direct_sum(parts, size, *gates):
    taken = [
        lax.ppermute(parts[k], "gy", [(s, (s - k) % size) for s in range(size)])
        for k in range(1, size)
    ]
    total = parts[0].astype(F32)
    for part in taken:
        total = total + after(part, *gates).astype(F32)
    return total


def summed(parts, steps):
    return parts[0].astype(F32) + steps[-1][0].astype(F32) + steps[-1][1].astype(F32)


def shards(
    nx,
    ny,
    tokens,
    attn_gain,
    query_key_value_weight,
    out_weight,
    moe_gain,
    router_weight,
    expert_in,
    expert_out,
    expert_ids,
    route_order,
    segment_ids,
    out_grad,
):
    rows = tokens.shape[0]
    length = segment_ids.shape[1]
    depth = out_weight.shape[1]
    heads_width = out_weight.shape[0]
    groups = heads_width // (HEAD_WIDTH * QUERIES_PER_GROUP)
    spare = -heads_width % LANES
    width = heads_width + spare
    kv_width = groups * 2 * HEAD_WIDTH
    joined = width + kv_width
    experts = router_weight.shape[0]
    all_experts = experts * ny
    chunks = length // CHUNK
    own_chunks = rows // CHUNK
    me = lax.axis_index("gy")
    first_expert = me * experts
    first_row = me * rows
    both = ("gx", "gy")

    pos, ends = pl.pallas_call(
        functools.partial(slots_kernel, experts),
        in_specs=[
            pl.BlockSpec(memory_space=pltpu.SMEM),
            pl.BlockSpec(memory_space=pltpu.VMEM),
            pl.BlockSpec(memory_space=pltpu.VMEM),
        ],
        out_shape=[
            jax.ShapeDtypeStruct((chunks, SUBLANES, CHUNK), jnp.int32),
            jax.ShapeDtypeStruct((SUBLANES, LANES), jnp.int32),
        ],
        compiler_params=params(),
        cost_estimate=cost(3),
        name="slots",
    )(
        first_expert.reshape(1),
        expert_ids.T,
        route_order[0].reshape(length, TOPK).T,
    )
    places = jnp.pad(
        pos.transpose(0, 2, 1).reshape(length, SUBLANES), ((0, 0), (0, LANES - SUBLANES))
    )
    ends = ends[:, : chunks + 1]
    pieces = (me - jnp.arange(ny, dtype=jnp.int32)) % ny
    lane_expert = jnp.arange(LANES, dtype=jnp.int32)
    turned_expert = (me - lane_expert // experts) % ny * experts + lane_expert % experts
    turned_expert = jnp.where(lane_expert < all_experts, turned_expert, -1)
    members = jnp.any(expert_ids[:, :, None] == turned_expert[None, None, :], axis=1)
    members = members.astype(F32).reshape(chunks, CHUNK, LANES)
    own_ids = lax.dynamic_slice_in_dim(expert_ids, first_row, rows, 0)
    own_members = jnp.any(own_ids[:, :, None] == turned_expert[None, None, :], axis=1).astype(F32)

    inputs = tokens.astype(F32)
    scale_one = lax.rsqrt(jnp.mean(inputs * inputs, axis=1, keepdims=True) + EPS)
    normed_one = (inputs * scale_one * attn_gain[None, :]).astype(BF16)
    normed_one_t = normed_one.T
    cosine, sine = rope_tiles(first_row, rows)
    labels = jnp.concatenate([jnp.full((SEGMAX,), -1, jnp.int32), segment_ids[0]])
    labels = lax.dynamic_slice_in_dim(labels, first_row, rows + SEGMAX, 0)
    position = jnp.arange(rows + SEGMAX, dtype=jnp.int32)
    bias = jnp.stack(
        [
            jnp.where(
                (labels[s : s + 2 * SEGMAX, None] == labels[None, s + SEGMAX : s + 2 * SEGMAX])
                & (
                    position[s : s + 2 * SEGMAX, None]
                    <= position[None, s + SEGMAX : s + 2 * SEGMAX]
                ),
                0.0,
                MASKED,
            ).astype(F32)
            for s in range(0, rows, SEGMAX)
        ]
    )
    grouped = query_key_value_weight.reshape(depth, groups, QUERIES_PER_GROUP + 2, HEAD_WIDTH)
    own_joined = jnp.concatenate(
        [
            jnp.pad(
                grouped[:, :, :QUERIES_PER_GROUP].reshape(depth, heads_width), ((0, 0), (0, spare))
            ),
            grouped[:, :, QUERIES_PER_GROUP:].reshape(depth, kv_width),
        ],
        axis=1,
    )
    own_out = jnp.pad(out_weight.T, ((0, 0), (0, spare)))
    own_router = jnp.pad(router_weight.T, ((0, 0), (0, LANES - experts)))
    gap = -(joined + LANES) % width
    own_weights = jnp.concatenate(
        [own_joined, own_router, jnp.zeros((depth, gap), BF16), own_out], axis=1
    )
    own_second = jnp.concatenate([own_out, own_router], axis=1)
    cut = experts * 2 // 5
    bounds = ((0, cut), (cut, experts))
    own_experts = [
        jnp.concatenate([expert_in[lo:hi], expert_out[lo:hi]], axis=2) for lo, hi in bounds
    ]
    first_weights = lax.all_gather(own_weights, "gx", axis=0)
    line_joined = after(direct_gather(own_joined, ny), *own_experts)
    own_second = after(own_second, line_joined)
    line_second = direct_gather(own_second, ny)
    ready = after(out_grad, line_second, bias, cosine, sine, normed_one)
    grad_steps = [gather_step((ready, ready), 0, ny)]
    rest_joined = lax.all_gather(line_joined, "gx", axis=0)
    rest_second = lax.all_gather(line_second, "gx", axis=0)
    wide = []
    for own in own_experts:
        wide.append(lax.all_gather(own, "gx", axis=1, tiled=True))


    out_column = (joined + LANES + gap) // width
    rest_block = lambda b: (0, jnp.maximum(b - 1, 0), 0, 0)
    joined_specs = [
        pl.BlockSpec((nx, depth, joined), lambda b: (0, 0, 0)),
        pl.BlockSpec((nx, pl.Squeezed(), depth, joined), rest_block),
    ]
    out_specs = [
        pl.BlockSpec((nx, depth, width), lambda b: (0, 0, out_column)),
        pl.BlockSpec((nx, pl.Squeezed(), depth, width), rest_block),
    ]
    held_joined = pltpu.VMEM((D, joined), BF16)
    held_out = pltpu.VMEM((D, width), BF16)
    query, kv = pl.pallas_call(
        project_kernel,
        grid=(ny,),
        in_specs=[
            whole((rows, D)),
            *joined_specs,
            whole((rows, LANES)),
            whole((rows, LANES)),
        ],
        out_specs=[
            pl.BlockSpec((rows, width), lambda b: (0, b)),
            pl.BlockSpec((rows, kv_width), lambda b: (0, b)),
        ],
        out_shape=[
            jax.ShapeDtypeStruct((rows, ny * width), BF16),
            jax.ShapeDtypeStruct((rows, ny * kv_width), BF16),
        ],
        scratch_shapes=[held_joined],
        compiler_params=params(),
        cost_estimate=cost(10),
        name="project",
    )(after(normed_one, bias), first_weights, rest_joined, cosine, sine)
    halo = lax.ppermute(kv[rows - SEGMAX :], "gy", [(s, s + 1) for s in range(ny - 1)])
    halves = rows // SEGMAX
    half_rows = lambda n, w: pl.BlockSpec((SEGMAX, w), lambda b: (n, b))
    whole_half = lambda n, w: pl.BlockSpec((SEGMAX, w), lambda b: (n, 0))
    below_rows = pl.BlockSpec((SEGMAX, kv_width), lambda b: (0, (b + ny - 1) % ny))
    bias_half = lambda n: pl.BlockSpec((pl.Squeezed(), 2 * SEGMAX, SEGMAX), lambda b: (n, 0, 0))

    def window(n):
        if n == 0:
            return [half_rows(0, kv_width), below_rows], (kv, halo)
        return [half_rows(n, kv_width), half_rows(n - 1, kv_width)], (kv, kv)

    mixed = [None] * halves
    for n in reversed(range(halves)):
        specs, arrays = window(n)
        mixed[n] = pl.pallas_call(
            attend_kernel,
            grid=(ny,),
            in_specs=[half_rows(n, width), *specs, bias_half(n)],
            out_specs=half_rows(0, width),
            out_shape=jax.ShapeDtypeStruct((SEGMAX, ny * width), BF16),
            compiler_params=params(),
            cost_estimate=cost(8),
            name="attend",
        )(query, *arrays, bias)
    for step in range(1, ny - 2):
        grad_steps.append(gather_step(grad_steps[-1], step, ny, mixed[-1]))
    middle, *normed_chunks = pl.pallas_call(
        functools.partial(branch_kernel, halves),
        grid=(1,),
        in_specs=[whole((SEGMAX, ny * width))] * halves
        + [
            out_specs[0],
            pl.BlockSpec((nx, ny - 1, depth, width), lambda _: (0, 0, 0, 0)),
            whole((rows, D)),
            whole((1, D)),
        ],
        out_specs=[whole((rows, D))] + [whole((CHUNK, D))] * own_chunks,
        out_shape=[jax.ShapeDtypeStruct((rows, D), F32)]
        + [jax.ShapeDtypeStruct((CHUNK, D), BF16)] * own_chunks,
        compiler_params=params(),
        cost_estimate=cost(7),
        name="branch",
    )(*mixed, first_weights, rest_second, tokens, moe_gain[None, :])

    router = jnp.concatenate(
        [
            first_weights[:, None, :, joined : joined + experts],
            rest_second[:, :, :, width : width + experts],
        ],
        axis=1,
    )
    router = router.transpose(0, 2, 1, 3).reshape(D, all_experts)
    router = jnp.pad(router, ((0, 0), (0, LANES - all_experts)))
    normed_two = jnp.concatenate(normed_chunks, axis=0)
    normed_steps = []
    for part in normed_chunks:
        part = after(part, grad_steps[-1])
        normed_steps.append([(part, part)])
    for step in range(ny - 1):
        for steps in normed_steps:
            steps.append(gather_step(steps[-1], step, ny))
    grad_steps.append(
        gather_step(grad_steps[-1], ny - 2, ny, *[steps[-1] for steps in normed_steps])
    )
    normed_pieces = []
    for part, steps in zip(normed_chunks, normed_steps):
        normed_pieces += [part] + [up for up, _ in steps[1:]] + [down for _, down in steps[1:]]
    grad_pieces = [out_grad] + [up for up, _ in grad_steps] + [down for _, down in grad_steps]
    smem = pl.BlockSpec(memory_space=pltpu.SMEM)
    vmem = pl.BlockSpec(memory_space=pltpu.VMEM)
    slot_rows = jax.ShapeDtypeStruct((experts, SLOTS, D), BF16)
    slot_lanes = lambda kind: jax.ShapeDtypeStruct((experts, SLOTS, LANES), kind)
    dispatch_scratch = lambda parts: [
        pltpu.VMEM((experts * SHORT_WINDOW, CHUNK), BF16),
        pltpu.VMEM((ny, rows, D), BF16),
        pltpu.SemaphoreType.DMA((ny, parts)),
    ]
    hbm = pl.BlockSpec(memory_space=pl.ANY)
    slot_grads = pl.pallas_call(
        functools.partial(dispatch_kernel, False, experts, ny),
        in_specs=[smem, smem] + [hbm] * (2 * ny - 1) + [vmem],
        out_specs=vmem,
        out_shape=slot_rows,
        scratch_shapes=dispatch_scratch(1),
        compiler_params=params(),
        cost_estimate=cost(26),
        name="dispatch_grads",
    )(pieces, ends, *grad_pieces, pos)
    dispatched, slot_gates = pl.pallas_call(
        functools.partial(dispatch_kernel, True, experts, ny),
        in_specs=[smem, smem] + [hbm] * len(normed_pieces) + [vmem] * 3,
        out_specs=[vmem, vmem],
        out_shape=[slot_rows, slot_lanes(F32)],
        scratch_shapes=dispatch_scratch(own_chunks),
        compiler_params=params(),
        cost_estimate=cost(31),
        name="dispatch_rows",
    )(pieces, ends, *normed_pieces, pos, router, members)

    half = (lax.axis_index("gx") % 2).reshape(1)
    y_rows, z_rows, slot_pairs, weight_terms = [], [], [], []
    for n, (lo, hi) in enumerate(bounds):
        outer = lambda *shape: pl.BlockSpec((1,) + shape, lambda e, lo=lo: (lo + e, 0, 0))
        inner = lambda *shape: pl.BlockSpec((1,) + shape, lambda e: (e, 0, 0))
        parts = n + 1
        slices = pl.BlockSpec((nx // parts, pl.Squeezed(), depth, 3 * FF), lambda e: (0, e, 0, 0))
        y, z, pair, *terms = pl.pallas_call(
            functools.partial(expert_kernel, lo, experts),
            grid=(hi - lo,),
            in_specs=[
                smem,
                outer(SLOTS, D),
                outer(SLOTS, D),
                outer(SLOTS, LANES),
                inner(D, 3 * FF),
            ],
            out_specs=[inner(SLOTS, D), inner(SLOTS, D), inner(SLOTS, LANES)]
            + [slices] * parts,
            out_shape=[
                jax.ShapeDtypeStruct((hi - lo, SLOTS, D), BF16),
                jax.ShapeDtypeStruct((hi - lo, SLOTS, D), BF16),
                jax.ShapeDtypeStruct((hi - lo, SLOTS, LANES), BF16),
            ]
            + [jax.ShapeDtypeStruct((nx // parts, hi - lo, depth, 3 * FF), BF16)] * parts,
            compiler_params=params(),
            cost_estimate=cost(9 * (hi - lo)),
            name="experts",
        )(half, dispatched, slot_grads, slot_gates, wide[n])
        y_rows.append(y)
        z_rows.append(z)
        slot_pairs.append(pair)
        weight_terms.append(terms)
    def combine(rows_in, which, pairs=None):
        held = pltpu.VMEM((3, experts * WINDOW, D), BF16)
        sems = pltpu.SemaphoreType.DMA((3, experts))
        hot_t = pltpu.VMEM((CHUNK, experts * WINDOW), BF16)
        total = pltpu.VMEM((CHUNK, D), F32)
        more = pairs is not None
        columns = D + LANES * more
        halves = chunks // ny
        here = pieces[jnp.array(which)]

        def place_map(c, piece_ref):
            return (piece_ref[c // halves] * halves + c % halves, 0)

        visits = 1 if more else halves

        def out_map(n):
            return lambda c, piece_ref: (jnp.clip(c - n * visits, 0, visits - 1), 0)

        return pl.pallas_call(
            functools.partial(combine_kernel, more, tuple(hi - lo for lo, hi in bounds), which),
            grid_spec=pltpu.PrefetchScalarGridSpec(
                num_scalar_prefetch=1,
                grid=(halves * len(which),),
                in_specs=[smem, pl.BlockSpec((CHUNK, LANES), place_map)]
                + [hbm] * len(bounds)
                + [once((hi - lo, SLOTS, LANES)) for lo, hi in bounds] * more,
                out_specs=[
                    pl.BlockSpec((CHUNK, columns), out_map(n))
                    for n in range(len(which) * halves // visits)
                ],
                scratch_shapes=[held, sems, hot_t, total]
                + [
                    pltpu.VMEM((experts * WINDOW, LANES), BF16),
                    pltpu.VMEM((CHUNK, LANES), F32),
                ]
                * more,
            ),
            out_shape=[jax.ShapeDtypeStruct((CHUNK * visits, columns), BF16)]
            * (len(which) * halves // visits),
            compiler_params=params(),
            cost_estimate=cost(16),
            name="combine_grads" if more else "combine_rows",
        )(here, ends, places, *rows_in, *(pairs if more else []))

    outer_pieces = sorted({1, ny - 1})
    inner_pieces = [k for k in range(ny) if k not in outer_pieces]
    order = outer_pieces + inner_pieces
    token_sum = combine(z_rows, order, slot_pairs)
    token_sum = [
        [token_sum[order.index(k) * own_chunks + n] for k in range(ny)] for n in range(own_chunks)
    ]
    token_steps = [[] for _ in token_sum]
    for step in range(1, ny):
        for parts, steps in zip(token_sum, token_steps):
            steps.append(sum_step(parts, steps[-1] if steps else None, step, ny))
    own_logits = jnp.where(own_members > 0.5, dot_nn(normed_two, router), MASKED)
    own_raised = jnp.exp(own_logits)
    own_gates = own_raised / jnp.sum(own_raised, axis=1, keepdims=True)
    source = lane_expert // (2 * experts) * experts + lane_expert % experts
    source = jnp.where(lane_expert < 2 * all_experts, source, -1)
    select = (source[:, None] == lane_expert[None, :]).astype(BF16)
    weight_sums = [
        lax.psum_scatter(weight_terms[0][0], "gx", scatter_dimension=0, tiled=True)[0],
        pair_scatter(*weight_terms[1], nx, token_sum[0][0]),
    ]
    combined = combine([after(y, [steps[-2] for steps in token_steps]) for y in y_rows], order)
    combined = [combined[order.index(k)] for k in range(ny)]
    row_block = lambda w: pl.BlockSpec((LANES, w), lambda r: (r, 0))
    later_block = lambda n, w: pl.BlockSpec((LANES, w), lambda r: (r + n * CHUNK // LANES, 0))
    backs = []
    for n, (parts, steps) in enumerate(zip(token_sum, token_steps)):
        backs.append(
            pl.pallas_call(
                middle_back_kernel,
                grid=(CHUNK // LANES,),
                in_specs=[row_block(D + LANES)] * 3
                + [later_block(n, LANES), whole((LANES, LANES)), whole((D, LANES))]
                + [later_block(n, D), whole((1, D)), later_block(n, D)],
                out_specs=[row_block(D), row_block(D), row_block(LANES), row_block(LANES)]
                + [whole((1, D))],
                out_shape=[
                    jax.ShapeDtypeStruct((CHUNK, D), F32),
                    jax.ShapeDtypeStruct((CHUNK, D), BF16),
                    jax.ShapeDtypeStruct((CHUNK, LANES), BF16),
                    jax.ShapeDtypeStruct((CHUNK, LANES), BF16),
                    jax.ShapeDtypeStruct((1, D), F32),
                ],
                compiler_params=params(),
                cost_estimate=cost(4),
                name="middle_back",
            )(after(parts[0], *combined), *steps[-1], own_gates, select, router, middle,
              moe_gain[None, :], out_grad)
        )
    middle_grads, branch_grads, highs, lows, moe_gain_grads = zip(*backs)
    moe_gain_grad = sum(moe_gain_grads)

    combined_steps = [sum_step(combined, None, 1, ny)]

    dquery, dkv, dbefore = [], [], []
    for n in range(halves):
        specs, arrays = window(n)
        outs = pl.pallas_call(
            attend_back_kernel,
            grid=(ny,),
            in_specs=[
                half_rows(n, width),
                *specs,
                bias_half(n),
                *out_specs,
                whole((SEGMAX, D)),
                whole_half(n, LANES),
                whole_half(n, LANES),
            ],
            out_specs=[half_rows(0, width), half_rows(0, kv_width), half_rows(0, kv_width)],
            out_shape=[
                jax.ShapeDtypeStruct((SEGMAX, ny * width), BF16),
                jax.ShapeDtypeStruct((SEGMAX, ny * kv_width), F32),
                jax.ShapeDtypeStruct((SEGMAX, ny * kv_width), F32 if n else BF16),
            ],
            scratch_shapes=[pltpu.VMEM((SEGMAX, width), F32), held_out],
            compiler_params=params(),
            cost_estimate=cost(17),
            name="attend_back",
        )(query, *arrays, bias, first_weights, rest_second, after(branch_grads[n], *branch_grads, *combined, *dbefore),
          cosine, sine)
        for kept, out in zip((dquery, dkv, dbefore), outs):
            kept.append(out)
    halo_grad = lax.ppermute(dbefore[0], "gy", [(s + 1, s) for s in range(ny - 1)])
    second_term = pl.pallas_call(
        functools.partial(branch_weights_kernel, experts, halves),
        grid=(ny,),
        in_specs=[whole((D, rows))]
        + [whole((CHUNK, D))] * halves
        + [whole((CHUNK, LANES))] * (2 * halves)
        + [half_rows(0, width)] * halves,
        out_specs=pl.BlockSpec((nx, pl.Squeezed(), depth, width + LANES), lambda b: (0, b, 0, 0)),
        out_shape=jax.ShapeDtypeStruct((nx, ny, depth, width + LANES), BF16),
        scratch_shapes=[pltpu.VMEM((D, rows), BF16), pltpu.VMEM((D, LANES), F32)],
        compiler_params=params(),
        cost_estimate=cost(9),
        name="branch_weights",
    )(normed_two.T, *branch_grads, *highs, *lows, *mixed)
    added = ()
    for step in range(2, ny):
        gates = (halo_grad,) if step == 2 else ()
        added = sum_added(combined, combined_steps[-1], step, ny, *gates)
        combined_steps.append(sum_sent(added, step, ny))
    next_rows = pl.BlockSpec((SEGMAX, kv_width), lambda b: (0, (b + 1) % ny))
    *joined_terms, normed_one_grad = pl.pallas_call(
        functools.partial(project_back_kernel, halves),
        grid=(ny,),
        in_specs=[half_rows(0, width)] * halves
        + [half_rows(0, kv_width)] * (2 * halves - 1)
        + [
            next_rows,
            smem,
            whole((D, rows)),
            *joined_specs,
            whole((rows, LANES)),
            whole((rows, LANES)),
        ],
        out_specs=[pl.BlockSpec((nx // 2, pl.Squeezed(), depth, joined), lambda b: (0, b, 0, 0))] * 2
        + [whole((rows, D))],
        out_shape=[jax.ShapeDtypeStruct((nx // 2, ny, depth, joined), BF16)] * 2
        + [jax.ShapeDtypeStruct((rows, D), F32)],
        scratch_shapes=[held_joined],
        compiler_params=params(),
        cost_estimate=cost(22),
        name="project_back",
    )(*dquery, *dkv, *dbefore[1:], halo_grad, half, normed_one_t, first_weights, rest_joined, cosine,
      sine)
    in_grad, down_grad = [], []
    for part in after(tuple(weight_sums), joined_terms):
        in_grad.append(part[..., : 2 * FF].astype(F32))
        down_grad.append(part[..., 2 * FF :].astype(F32))
    in_grad, down_grad = jnp.concatenate(in_grad), jnp.concatenate(down_grad)
    input_grad, attn_gain_grad = pl.pallas_call(
        input_back_kernel,
        grid=(rows // LANES,),
        in_specs=[row_block(D), row_block(D), whole((1, D)), row_block(D)],
        out_specs=[row_block(D), whole((1, D))],
        out_shape=[
            jax.ShapeDtypeStruct((rows, D), F32),
            jax.ShapeDtypeStruct((1, D), F32),
        ],
        compiler_params=params(),
        cost_estimate=cost(6),
        name="input_back",
    )(tokens, normed_one_grad, attn_gain[None, :], jnp.concatenate(middle_grads))

    gain_sums = jnp.concatenate([attn_gain_grad, moe_gain_grad])
    bit = 1
    while bit < nx:
        pairs = [(s, s ^ bit) for s in range(nx)]
        gain_sums = gain_sums + lax.ppermute(gain_sums, "gx", pairs)
        bit = 2 * bit
    last = tuple(after(part, in_grad, down_grad, gain_sums) for part in combined_steps[-1])
    layer_out = (middle + summed(combined, [last])).astype(BF16)

    second_sum = lax.psum_scatter(
        after(second_term, weight_sums[0]), "gx", scatter_dimension=0, tiled=True
    )
    second_sum = lax.optimization_barrier(second_sum)[0]
    mine, other = joined_terms
    other = after(other, combined_steps[1], attn_gain_grad)
    joined_sum = pair_scatter(mine, other, nx, second_sum, *added, *weight_sums)
    high = gain_sums.astype(BF16)
    low = (gain_sums - high.astype(F32)).astype(BF16)
    gains = jnp.stack([high, low]).reshape(-1)
    gain_rows = -(-gains.shape[0] // joined)
    gain_rows += -gain_rows % SUBLANES
    gains = jnp.pad(gains, (0, gain_rows * joined - gains.shape[0])).reshape(gain_rows, joined)
    second_sum = direct_sum(second_sum, ny, layer_out)
    out_weight_grad = second_sum[:, :heads_width].T
    router_grad = second_sum[:, width : width + experts].T
    joined_sum = after(joined_sum, gains, out_weight_grad, router_grad)
    joined_parts, gain_parts = [joined_sum[0]], [gains]
    for k in range(1, ny):
        part = jnp.concatenate([joined_sum[k], gains], axis=0)
        part = lax.ppermute(part, "gy", [(s, (s - k) % ny) for s in range(ny)])
        joined_parts.append(part)
        gain_parts.append(part[depth:])
    qkv_grad = pl.pallas_call(
        functools.partial(joined_sum_kernel, groups),
        out_shape=jax.ShapeDtypeStruct(query_key_value_weight.shape, F32),
        compiler_params=params(),
        cost_estimate=cost(2),
        name="joined_sum",
    )(*joined_parts)
    gain_sums = jnp.roll(jnp.stack(gain_parts), me, axis=0).astype(F32)
    gain_sums = gain_sums.reshape(ny, -1)[:, : 4 * D].reshape(ny, 2, 2, D)
    gain_sums = jnp.sum(gain_sums, axis=(0, 1))
    return (
        layer_out,
        input_grad,
        gain_sums[0],
        qkv_grad,
        out_weight_grad,
        gain_sums[1],
        router_grad,
        in_grad,
        down_grad,
    )


def solution(mesh):
    in_specs = (
        P(("gx", "gy"), None),
        P(),
        P("gx", "gy"),
        P("gy", "gx"),
        P(),
        P("gy", "gx"),
        P("gy", "gx", None),
        P("gy", "gx", None),
        P("gx", None),
        P("gx", None),
        P("gx", None),
        P(("gx", "gy"), None),
    )
    out_specs = (
        P(("gx", "gy"), None),
        P(("gx", "gy"), None),
        P(),
        P("gx", "gy"),
        P("gy", "gx"),
        P(),
        P("gy", "gx"),
        P("gy", "gx", None),
        P("gy", "gx", None),
    )
    body = functools.partial(shards, mesh.shape["gx"], mesh.shape["gy"])
    return jax.shard_map(body, mesh=mesh, in_specs=in_specs, out_specs=out_specs, check_vma=False)
```
